32 devices in a mesh: ctx: 16 (over z, y, core), fsdp: 2 (over x).
Axes of the slice: x: 2, y: 2, z: 4, core: 2. Of those that a mesh axis runs over, the one named last changes fastest.
Arguments:
- hidden_in: bfloat16 [2, 4096, 2048], P('fsdp', 'ctx'), may hold values from -6 to 6
- norm_gain: float32 [2048], P(('ctx', 'fsdp')), may hold values from 0.5 to 1.5
- in_proj: float32 [2048, 8192], P(('ctx', 'fsdp')), may hold values from -0.125 to 0.125
- conv_weight: float32 [4, 4096], P(None, ('ctx', 'fsdp')), may hold values from -3 to 3
- conv_bias: float32 [4096], P(('ctx', 'fsdp')), may hold values from -3 to 3
- state_proj: float32 [4096, 160], P(('ctx', 'fsdp')), may hold values from -0.09375 to 0.09375
- delta_proj: float32 [128, 4096], P(None, ('ctx', 'fsdp')), may hold values from -0.5 to 0.5
- delta_bias: float32 [4096], P(('ctx', 'fsdp')), may hold values from -4 to -2
- decay_log: float32 [16, 4096], P(None, ('ctx', 'fsdp')), may hold values from -9 to -0.5
- skip_gain: float32 [4096], P(('ctx', 'fsdp')), may hold values from 0.03 to 20, as said below
- out_proj: float32 [4096, 2048], P(('ctx', 'fsdp')), may hold values from -0.09375 to 0.09375
- cotangent: bfloat16 [2, 4096, 2048], P('fsdp', 'ctx'), may hold values from -6 to 6
Outputs:
- block_out: bfloat16 [2, 4096, 2048], P('fsdp', 'ctx')
- input_grad: bfloat16 [2, 4096, 2048], P('fsdp', 'ctx')
- norm_gain_grad: float32 [2048], P(('ctx', 'fsdp'))
- in_proj_grad: float32 [2048, 8192], P(('ctx', 'fsdp'))
- conv_weight_grad: float32 [4, 4096], P(None, ('ctx', 'fsdp'))
- conv_bias_grad: float32 [4096], P(('ctx', 'fsdp'))
- state_proj_grad: float32 [4096, 160], P(('ctx', 'fsdp'))
- delta_proj_grad: float32 [128, 4096], P(None, ('ctx', 'fsdp'))
- delta_bias_grad: float32 [4096], P(('ctx', 'fsdp'))
- decay_log_grad: float32 [16, 4096], P(None, ('ctx', 'fsdp'))
- skip_gain_grad: float32 [4096], P(('ctx', 'fsdp'))
- out_proj_grad: float32 [4096, 2048], P(('ctx', 'fsdp'))
The draws below stay inside these ranges and needn't reach their ends.
Inputs may be any that keep to these rules, and one draw needn't show every extreme that they name: `skip_gain`: positive skip coefficients.
All inputs are finite; a program needn't handle non-finite values.
Results may differ from the reference program's by a relative error of at most 0.012.
The reference program's roundings to bfloat16 on the way count: a program that leaves them out, or rounds other values in their place, can miss the bound.
Values may be sent and summed in bfloat16 or wider, within the bound.
A program may use at most 384 MiB of HBM per device.

```python
import math
import jax
import jax.numpy as jnp
from jax import lax

D = 2048
DI = 4096
STATE = 16
DT_RANK = 128
KW = 4
SEQS = 2
LENGTH = 4096


def log_spread(key, lower, upper):
    fraction = jax.random.uniform(key, (DI,), jnp.float32)
    return jnp.exp(math.log(lower) + fraction * (math.log(upper) - math.log(lower)))


def draw_skip_gain(key, part):
    key = jax.random.fold_in(key, 11)
    values = log_spread(key, 0.25, 4.0)
    return values.astype(jnp.float32)


def level_of(rng, dims, split, least, top_value):
    gain, own = 1.0, jax.random.fold_in(rng, 6)
    for position, shards_of in split:
        steps = jnp.exp(jax.random.uniform(jax.random.fold_in(own, position), (shards_of,), jnp.float32, least / len(split), top_value / len(split)))
        gain = gain * jnp.repeat(steps, dims[position] // shards_of).reshape([-1 if axis == position else 1 for axis in range(len(dims))])
    return gain


def noise(stream_key, dims, width, bound, cuts=(), kind=jnp.bfloat16):
    values = jax.random.normal(stream_key, dims, jnp.float32) * width
    if len(cuts) > 0:
        values = level_of(stream_key, dims, cuts, -0.22, 0.18) * values
    return jnp.clip(values, min=-bound, max=bound).astype(kind)


def setup_inputs(seed: int = 0) -> dict:
    streams_of = jax.random.split(jax.random.key(seed), 13)
    hidden_in = noise(streams_of[0], (SEQS, LENGTH, D), 1.0, 6.0, ((0, 2), (1, 16)))
    norm_gain = jnp.clip(1.0 + 0.1 * jax.random.normal(streams_of[1], (D,), jnp.float32), 0.5, 1.5)
    in_proj = noise(streams_of[2], (D, 2 * DI), D ** -0.5, 0.125, ((0, 32),), jnp.float32)
    conv_weight = noise(streams_of[3], (KW, DI), KW ** -0.5, 3.0, ((1, 32),), jnp.float32)
    conv_bias = noise(streams_of[4], (DI,), 0.5, 3.0, ((0, 32),), jnp.float32)
    state_proj = noise(streams_of[5], (DI, DT_RANK + 2 * STATE), DI ** -0.5, 0.09375, ((0, 32),), jnp.float32)
    delta_proj = noise(streams_of[6], (DT_RANK, DI), DT_RANK ** -0.5, 0.5, ((1, 32),), jnp.float32)
    delta_bias = jnp.clip(-4.0 + 2.0 * jax.random.uniform(streams_of[7], (DI,), jnp.float32) ** level_of(streams_of[7], (DI,), ((0, 32),), -0.2, 0.2), -4.0, -2.0)
    decay_log = jnp.clip(-9.0 + 8.5 * jax.random.uniform(streams_of[8], (STATE, DI), jnp.float32) ** level_of(streams_of[8], (STATE, DI), ((1, 32),), -0.2, 0.2), -9.0, -0.5)
    skip_gain = draw_skip_gain(jax.random.fold_in(streams_of[12], 71), 0)
    out_proj = noise(streams_of[10], (DI, D), DI ** -0.5, 0.09375, ((0, 32),), jnp.float32)
    cotangent = noise(streams_of[11], (SEQS, LENGTH, D), 1.0, 6.0, ((0, 2), (1, 16)))
    return dict(hidden_in=hidden_in, norm_gain=norm_gain, in_proj=in_proj, conv_weight=conv_weight, conv_bias=conv_bias, state_proj=state_proj, delta_proj=delta_proj, delta_bias=delta_bias, decay_log=decay_log, skip_gain=skip_gain, out_proj=out_proj, cotangent=cotangent)


EPS = 1e-05

@jax.custom_vjp
def low(v):
    return lax.optimization_barrier(v.astype(jnp.bfloat16)).astype(jnp.float32)

@jax.custom_vjp
def low_back(v):
    return v

def low_keep(v):
    return (low(v), None)

def low_pass(kept, grad):
    return (grad,)

def back_keep(v):
    return (v, None)

def back_low(kept, grad):
    return (low(grad),)
low.defvjp(low_keep, low_pass)
low_back.defvjp(back_keep, back_low)

def matmul(left, right):
    return jnp.dot(left, right, precision=lax.Precision.HIGHEST, preferred_element_type=jnp.float32)

def scan_block(decay_rate, state, block_in):

    def advance(running, token):
        delta_tok, act_tok, in_tok, out_tok = token
        running = jnp.exp(delta_tok[None, :] * decay_rate) * running + in_tok[:, None] * (delta_tok * act_tok)[None, :]
        return (running, lax.optimization_barrier(jnp.sum(out_tok[:, None] * running, axis=0)))
    return lax.scan(advance, state, block_in)
checked_block = jax.checkpoint(scan_block)

def selective(delta, activated, in_coef, out_coef, decay_rate):
    length = delta.shape[0]
    piece_len = 64
    count = length // piece_len
    pieces = (delta.reshape(count, piece_len, DI), activated.reshape(count, piece_len, DI), in_coef.reshape(count, piece_len, STATE), out_coef.reshape(count, piece_len, STATE))
    start = jnp.zeros((STATE, DI), jnp.float32)
    spent, outputs = lax.scan(lambda running, piece: checked_block(decay_rate, running, piece), start, pieces)
    return outputs.reshape(length, DI)

def forward(hidden, norm_gain, in_proj, conv_weight, conv_bias, state_proj, delta_proj, delta_bias, decay_log, skip_gain, out_proj):
    length = hidden.shape[0]
    inv_rms = lax.rsqrt(lax.optimization_barrier(jnp.mean(hidden * hidden, axis=1, keepdims=True)) + EPS)
    unit_rows = hidden * inv_rms
    normed = low(unit_rows * low(norm_gain)[None, :])
    mixed = low_back(low(matmul(normed, low(in_proj))))
    conv_in = mixed[:, :DI]
    gate_in = mixed[:, DI:]
    padded = jnp.concatenate([jnp.zeros((KW - 1, DI), jnp.float32), conv_in], axis=0)
    kernel = low(conv_weight)
    conv_out = jnp.broadcast_to(low(conv_bias)[None, :], (length, DI))
    for offset in range(KW):
        conv_out = conv_out + kernel[offset][None, :] * padded[offset:offset + length]
    activated = low(jax.nn.silu(conv_out))
    selected = low_back(matmul(activated, low(state_proj)))
    delta_in = low(selected[:, :DT_RANK])
    in_coef = selected[:, DT_RANK:DT_RANK + STATE]
    out_coef = selected[:, DT_RANK + STATE:]
    delta = jax.nn.softplus(low_back(matmul(delta_in, low(delta_proj))) + low(delta_bias)[None, :])
    decay_rate = -jnp.exp(low(decay_log))
    scanned = selective(delta, activated, in_coef, out_coef, decay_rate) + low(skip_gain)[None, :] * activated
    gated = low(scanned * jax.nn.silu(gate_in))
    return hidden + matmul(gated, low(out_proj))

def reference(hidden_in, norm_gain, in_proj, conv_weight, conv_bias, state_proj, delta_proj, delta_bias, decay_log, skip_gain, out_proj, cotangent):
    weights = (norm_gain, in_proj, conv_weight, conv_bias, state_proj, delta_proj, delta_bias, decay_log, skip_gain, out_proj)

    def one_sequence(totals, pair):
        rows, cot_rows = pair
        value, pullback = jax.vjp(forward, rows.astype(jnp.float32), *weights)
        grads = pullback(cot_rows.astype(jnp.float32))
        totals = tuple((total + grad for total, grad in zip(totals, grads[1:])))
        return (totals, (value.astype(jnp.bfloat16), grads[0].astype(jnp.bfloat16)))
    start = tuple((jnp.zeros_like(weight) for weight in weights))
    totals, (block_out, input_grad) = lax.scan(one_sequence, start, (hidden_in, cotangent))
    return (block_out, input_grad, totals[0], totals[1], totals[2], totals[3], totals[4], totals[5], totals[6], totals[7], totals[8], totals[9])
```

```python
import functools

import jax
import jax.numpy as jnp
import numpy as np
from jax import lax
from jax.experimental import pallas as pl
from jax.experimental.pallas import tpu as pltpu
from jax.sharding import PartitionSpec as P

D = 2048
DI = 4096
STATE = 16
DT_RANK = 128
KW = 4
EPS = 1e-05
LOG2E = 1.4426950408889634
STEPS = 16
MESH = pl.DeviceIdType.MESH
BF16 = jnp.bfloat16
F32 = jnp.float32


class Grid:
    def __init__(self, ctx, fsdp):
        self.ctx, self.fsdp = ctx, fsdp
        self.planes = ctx // 4
        self.members = 4 * fsdp
        self.devices = ctx * fsdp

    def here(self):
        c, f = lax.axis_index("ctx"), lax.axis_index("fsdp")
        return c // 4, c % 4, f

    def at(self, z, q, f):
        return {"ctx": z * 4 + q, "fsdp": f}

    def member(self, z, j):
        return self.at(z, j // self.fsdp, j % self.fsdp)


def remote(src, dst, send, recv, where):
    return pltpu.make_async_remote_copy(
        src_ref=src, dst_ref=dst, send_sem=send, recv_sem=recv, device_id=where, device_id_type=MESH
    )


def greet(places):
    barrier = pltpu.get_barrier_semaphore()
    for place in places:
        pl.semaphore_signal(barrier, inc=1, device_id=place, device_id_type=MESH)
    pl.semaphore_wait(barrier, len(places))


def comm_call(kernel, outs, scratch, ident, name, args, vmem=None, in_vmem=()):
    spaces = [pl.BlockSpec(memory_space=pltpu.VMEM if i in in_vmem else pl.ANY) for i in range(len(args))]
    return pl.pallas_call(
        kernel,
        in_specs=spaces,
        out_specs=[pl.BlockSpec(memory_space=pl.ANY)] * len(outs),
        out_shape=outs,
        scratch_shapes=scratch,
        compiler_params=pltpu.CompilerParams(
            collective_id=ident, has_side_effects=True, vmem_limit_bytes=vmem or 16 * 2**20
        ),
        name=name,
    )(*args)


def gather_kernel(grid, n_ref, c_ref, wi_ref, wo_ref, sm_ref, n_all, c_all, wi_all, wo_all, sm_all,
                  local, n_send, n_recv, c_send, c_recv, a_send, a_recv, z_send, z_recv):
    z, q, f = grid.here()
    F, C, Z = grid.fsdp, grid.members, grid.planes
    me = q * F + f
    opposite, twin = q ^ 2, q ^ 1
    plane = [grid.member(z, lax.rem(me + d, C)) for d in range(1, C)]
    barrier = pltpu.get_barrier_semaphore()
    for place in plane:
        pl.semaphore_signal(barrier, inc=1, device_id=place, device_id_type=MESH)

    @pl.when(z > 0)
    def _():
        pl.semaphore_signal(barrier, inc=1, device_id=grid.at(z - 1, q, f), device_id_type=MESH)

    @pl.when(z < Z - 1)
    def _():
        pl.semaphore_signal(barrier, inc=1, device_id=grid.at(z + 1, q, f), device_id_type=MESH)

    inner = jnp.where((z > 0) & (z < Z - 1), 2, 1)
    pl.semaphore_wait(barrier, C - 1 + inner)

    mine = [
        pltpu.make_async_copy(n_ref, n_all.at[me], local.at[0]),
        pltpu.make_async_copy(c_ref, c_all.at[me], local.at[1]),
        pltpu.make_async_copy(wi_ref.at[me], wi_all.at[z * C + me], local.at[2]),
        pltpu.make_async_copy(wo_ref, wo_all.at[z], local.at[3]),
        pltpu.make_async_copy(sm_ref, sm_all.at[z], local.at[4]),
    ]
    for copy in mine:
        copy.start()
    sends = []

    def push(copy):
        copy.start()
        sends.append(copy)

    for d in range(1, C):
        j = lax.rem(me + d, C)
        push(remote(wi_ref.at[j], wi_all.at[z * C + me], a_send.at[d], a_recv.at[d], grid.member(z, j)))

    n_sent, c_sent = [0], [0]

    def push_n(block, src, where):
        push(remote(src, n_all.at[block], n_send.at[n_sent[0]], n_recv.at[block], where))
        n_sent[0] += 1

    def push_c(block, src, where):
        push(remote(src, c_all.at[block], c_send.at[c_sent[0]], c_recv.at[block], where))
        c_sent[0] += 1

    def arrived(ref, sems, block):
        remote(ref.at[block], ref.at[block], n_send.at[0], sems.at[block], grid.at(z, twin, f)).wait_recv()

    others = [lax.rem(f + d, F) for d in range(1, F)]
    for g in others:
        push_n(me, n_ref, grid.at(z, q, g))
    push_c(me, c_ref, grid.at(z, opposite, f))
    push_n(me, n_ref, grid.at(z, opposite, f))
    for g in others:
        push_c(me, c_ref, grid.at(z, q, g))
    push_n(me, n_ref, grid.at(z, twin, f))
    push_c(me, c_ref, grid.at(z, twin, f))

    def line_send(src_of, dst, k, step):
        block_right, block_left = z - step, z + step
        right = remote(src_of(block_right), dst(block_right), z_send.at[k, 0, step], z_recv.at[k, 0, step], grid.at(z + 1, q, f))
        left = remote(src_of(block_left), dst(block_left), z_send.at[k, 1, step], z_recv.at[k, 1, step], grid.at(z - 1, q, f))
        return right, left, (z < Z - 1) & (block_right >= 0), (z > 0) & (block_left <= Z - 1)

    def line_start(src_of, dst, k, step):
        right, left, to_right, to_left = line_send(src_of, dst, k, step)

        @pl.when(to_right)
        def _():
            right.start()

        @pl.when(to_left)
        def _():
            left.start()

    def line_done(src_of, dst, k, step):
        right, left, to_right, to_left = line_send(src_of, dst, k, step)

        @pl.when(to_right)
        def _():
            right.wait_send()

        @pl.when(to_left)
        def _():
            left.wait_send()

    def line_arrived(dst, k, step):
        from_left, from_right = z - 1 - step, z + 1 + step

        @pl.when(from_left >= 0)
        def _():
            remote(dst(from_left), dst(from_left), z_send.at[k, 0, step], z_recv.at[k, 0, step], grid.at(z - 1, q, f)).wait_recv()

        @pl.when(from_right <= Z - 1)
        def _():
            remote(dst(from_right), dst(from_right), z_send.at[k, 1, step], z_recv.at[k, 1, step], grid.at(z + 1, q, f)).wait_recv()

    lines = [
        (lambda b: wi_all.at[pl.ds(b * C, C)], lambda b: wi_all.at[pl.ds(b * C, C)]),
        (lambda b: wo_all.at[b], lambda b: wo_all.at[b]),
        (lambda b: sm_all.at[b], lambda b: sm_all.at[b]),
    ]
    line_start(lambda b: sm_ref, lines[2][1], 2, 0)
    mine[2].wait()
    for d in range(1, C):
        back = lax.rem(me + C - d, C)
        remote(wi_ref.at[me], wi_all.at[z * C + back], a_send.at[d], a_recv.at[d], grid.member(z, back)).wait_recv()
    line_start(*lines[0], 0, 0)
    line_start(lambda b: wo_ref, lines[1][1], 1, 0)
    for g in others:
        block = q * F + g
        arrived(n_all, n_recv, block)
        push_n(block, n_all.at[block], grid.at(z, opposite, f))
        push_n(block, n_all.at[block], grid.at(z, twin, f))
    arrived(c_all, c_recv, opposite * F + f)
    for g in others:
        push_c(opposite * F + f, c_all.at[opposite * F + f], grid.at(z, q, g))
    push_c(opposite * F + f, c_all.at[opposite * F + f], grid.at(z, twin, f))
    for g in others:
        arrived(c_all, c_recv, q * F + g)
        push_c(q * F + g, c_all.at[q * F + g], grid.at(z, twin, f))
    for g in [f] + others:
        block = opposite * F + g
        arrived(n_all, n_recv, block)
        push_n(block, n_all.at[block], grid.at(z, twin, f))
    for g in others:
        block = opposite * F + g
        arrived(c_all, c_recv, block)
        push_c(block, c_all.at[block], grid.at(z, twin, f))
    for step in range(Z - 1):
        for k in (2, 0, 1):
            line_arrived(lines[k][1], k, step)
            if step < Z - 2:
                line_start(*lines[k], k, step + 1)
    for side in (twin, twin ^ 2):
        for g in [f] + others:
            arrived(n_all, n_recv, side * F + g)
            arrived(c_all, c_recv, side * F + g)
    for i in (0, 1, 3, 4):
        mine[i].wait()
    for copy in sends:
        copy.wait_send()
    line_done(lambda b: sm_ref, lines[2][1], 2, 0)
    line_done(lambda b: wo_ref, lines[1][1], 1, 0)
    line_done(*lines[0], 0, 0)
    for step in range(1, Z - 1):
        for k in range(3):
            line_done(*lines[k], k, step)


def gather_all(grid, normed, cot, wi, wo, small):
    F, C, Z = grid.fsdp, grid.members, grid.planes
    tokens = normed.shape[0]
    dma = pltpu.SemaphoreType.DMA
    outs = [
        jax.ShapeDtypeStruct((C, tokens, D), BF16),
        jax.ShapeDtypeStruct((C, tokens, D), BF16),
        jax.ShapeDtypeStruct((Z * C,) + wi.shape[1:], BF16),
        jax.ShapeDtypeStruct((Z,) + wo.shape, BF16),
        jax.ShapeDtypeStruct((Z,) + small.shape, BF16),
    ]
    count = (F - 1) + F + 2 * F
    scratch = [dma((5,)), dma((count,)), dma((C,)), dma((count,)), dma((C,)), dma((C,)), dma((C,)), dma((3, 2, Z)), dma((3, 2, Z))]
    return comm_call(functools.partial(gather_kernel, grid), outs, scratch, 1, "gather_weights_and_tokens", (normed, cot, wi, wo, small))


def plane_sum_kernel(grid, part_ref, out_ref, send_buf, recv_buf, result, send, recv, out_send, out_recv, own):
    z, q, f = grid.here()
    C = grid.members
    me = q * grid.fsdp + f
    rows = recv_buf.shape[1]
    greet([grid.member(z, lax.rem(me + d, C)) for d in range(1, C)])
    lane = lax.broadcasted_iota(jnp.int32, (rows, 128), 1)

    def packed(v):
        high = v.astype(BF16).astype(F32)
        return high + pltpu.roll(v - high, 32, 1)

    @pl.loop(0, C)
    def _(k):
        at = pl.ds(pl.multiple_of(k * rows, 16), rows)
        send_buf[k, :, 0:128] = part_ref[at, 0:128].astype(BF16)
        send_buf[k, :, 128:256] = packed(part_ref[at, 128:256]).astype(BF16)

    copies = []
    for d in range(1, C):
        j = lax.rem(me + d, C)
        copy = remote(send_buf.at[j], recv_buf.at[d], send.at[d], recv.at[d], grid.member(z, j))
        copy.start()
        copies.append(copy)
    low = send_buf[me, :, 0:128].astype(F32)
    high = send_buf[me, :, 128:256].astype(F32)
    for d in range(1, C):
        copies[d - 1].wait_recv()
        low = low + recv_buf[d, :, 0:128].astype(F32)
        high = high + recv_buf[d, :, 128:256].astype(F32)
    total = jnp.where(lane < 32, high + pltpu.roll(high, 96, 1), 0.0)
    result[:, 0:128] = low.astype(BF16)
    result[:, 128:256] = packed(total).astype(BF16)
    for copy in copies:
        copy.wait_send()
    mine = pltpu.make_async_copy(result, out_ref.at[me], own)
    mine.start()
    copies = []
    for d in range(1, C):
        j = lax.rem(me + d, C)
        copy = remote(result, out_ref.at[me], out_send.at[d], out_recv.at[d], grid.member(z, j))
        copy.start()
        copies.append(copy)
    mine.wait()
    for d in range(1, C):
        back = lax.rem(me + C - d, C)
        remote(result, out_ref.at[back], out_send.at[d], out_recv.at[d], grid.member(z, back)).wait_recv()
    for copy in copies:
        copy.wait_send()


def plane_sum(grid, part, ident):
    C = grid.members
    rows = part.shape[0] // C
    dma = pltpu.SemaphoreType.DMA
    out = comm_call(
        functools.partial(plane_sum_kernel, grid),
        [jax.ShapeDtypeStruct((C, rows, 256), BF16)],
        [pltpu.VMEM((C, rows, 256), BF16), pltpu.VMEM((C, rows, 256), BF16), pltpu.VMEM((rows, 256), BF16)]
        + [dma((C,))] * 4 + [dma],
        ident, "plane_sum", (part,), vmem=40 * 2**20, in_vmem=(0,),
    )[0]
    return out.reshape(C * rows, 256)


def line_gather_kernel(grid, count, *refs):
    z, q, f = grid.here()
    Z = grid.planes
    ins, outs = refs[:count], refs[count:2 * count]
    local, send, recv = refs[2 * count:]
    greet([grid.at(lax.rem(z + d, Z), q, f) for d in range(1, Z)])
    copies = []
    for i in range(count):
        mine = pltpu.make_async_copy(ins[i], outs[i].at[z], local.at[i])
        mine.start()
        copies.append(mine)
    pushes = []
    for i in range(count):
        for d in range(1, Z):
            copy = remote(ins[i], outs[i].at[z], send.at[i, d], recv.at[i, d], grid.at(lax.rem(z + d, Z), q, f))
            copy.start()
            pushes.append(copy)
    for mine in copies:
        mine.wait()
    for i in range(count):
        for d in range(1, Z):
            back = lax.rem(z + Z - d, Z)
            remote(ins[i], outs[i].at[back], send.at[i, d], recv.at[i, d], grid.at(back, q, f)).wait_recv()
    for copy in pushes:
        copy.wait_send()


def line_gather(grid, arrays, ident, name):
    dma = pltpu.SemaphoreType.DMA
    n, Z = len(arrays), grid.planes
    return comm_call(
        functools.partial(line_gather_kernel, grid, n),
        [jax.ShapeDtypeStruct((Z,) + a.shape, a.dtype) for a in arrays],
        [dma((n,)), dma((n, Z)), dma((n, Z))], ident, name, tuple(arrays),
    )


def twin_swap_kernel(grid, count, *refs):
    z, q, f = grid.here()
    ins, outs = refs[:count], refs[count:2 * count]
    send, recv = refs[2 * count:]
    twin = grid.at(z, q ^ 1, f)
    greet([twin])
    copies = [remote(ins[i], outs[i], send.at[i], recv.at[i], twin) for i in range(count)]
    for copy in copies:
        copy.start()
    for copy in copies:
        copy.wait()


def twin_swap(grid, arrays, ident):
    dma = pltpu.SemaphoreType.DMA
    n = len(arrays)
    return comm_call(
        functools.partial(twin_swap_kernel, grid, n),
        [jax.ShapeDtypeStruct(a.shape, a.dtype) for a in arrays],
        [dma((n,)), dma((n,))], ident, "twin_swap", tuple(arrays),
    )


def owners_kernel(grid, planes_in, lines_in, *refs):
    z, q, f = grid.here()
    C, Z, N = grid.members, grid.planes, grid.devices
    me = q * grid.fsdp + f
    lin = z * C + me
    total = 1 + planes_in + lines_in
    ins, outs = refs[:total], refs[total:2 * total]
    local, w_send, w_recv, p_send, p_recv, l_send, l_recv = refs[2 * total:]
    barrier = pltpu.get_barrier_semaphore()

    def place(d):
        other = lax.rem(lin + d, N)
        return other, grid.member(other // C, lax.rem(other, C))

    @pl.loop(1, N)
    def _(d):
        pl.semaphore_signal(barrier, inc=1, device_id=place(d)[1], device_id_type=MESH)

    pl.semaphore_wait(barrier, N - 1)

    def weight(d):
        other, where = place(d)
        return remote(ins[0].at[other], outs[0].at[lin], w_send.at[d], w_recv.at[d], where)

    @pl.loop(1, N)
    def _(d):
        weight(d).start()

    mine = [pltpu.make_async_copy(ins[0].at[lin], outs[0].at[lin], local.at[0])]
    pushes, waits = [], []
    for i in range(planes_in):
        mine.append(pltpu.make_async_copy(ins[1 + i].at[me], outs[1 + i].at[me], local.at[1 + i]))
        for d in range(1, C):
            j, back = lax.rem(me + d, C), lax.rem(me + C - d, C)
            pushes.append(remote(ins[1 + i].at[j], outs[1 + i].at[me], p_send.at[i, d], p_recv.at[i, d], grid.member(z, j)))
            waits.append(remote(ins[1 + i].at[me], outs[1 + i].at[back], p_send.at[i, d], p_recv.at[i, d], grid.member(z, back)))
    for i in range(lines_in):
        k = 1 + planes_in + i
        mine.append(pltpu.make_async_copy(ins[k].at[z], outs[k].at[z], local.at[k]))
        for d in range(1, Z):
            j, back = lax.rem(z + d, Z), lax.rem(z + Z - d, Z)
            pushes.append(remote(ins[k].at[j], outs[k].at[z], l_send.at[i, d], l_recv.at[i, d], grid.at(j, q, f)))
            waits.append(remote(ins[k].at[z], outs[k].at[back], l_send.at[i, d], l_recv.at[i, d], grid.at(back, q, f)))
    for copy in pushes + mine:
        copy.start()
    for copy in mine:
        copy.wait()
    for copy in waits:
        copy.wait_recv()
    for copy in pushes:
        copy.wait_send()

    @pl.loop(1, N)
    def _(d):
        back = lax.rem(lin + N - d, N)
        remote(ins[0].at[lin], outs[0].at[back], w_send.at[d], w_recv.at[d], grid.member(back // C, lax.rem(back, C))).wait_recv()
        weight(d).wait_send()


def to_owners(grid, weight, plane_arrays, line_arrays, ident):
    dma = pltpu.SemaphoreType.DMA
    C, Z, N = grid.members, grid.planes, grid.devices
    p, l = len(plane_arrays), len(line_arrays)
    args = (weight,) + tuple(plane_arrays) + tuple(line_arrays)
    return comm_call(
        functools.partial(owners_kernel, grid, p, l),
        [jax.ShapeDtypeStruct(a.shape, a.dtype) for a in args],
        [dma((1 + p + l,)), dma((N,)), dma((N,)), dma((p, C)), dma((p, C)), dma((l, Z)), dma((l, Z))],
        ident, "to_owners", args,
    )

def spread(coef_ref, fan_ref, splat, tc):
    c = coef_ref[...].reshape(8 * tc, 128)
    for k in range(0, 2 * STATE, 4):
        l = pl.ds(k * 128, 512)
        splat[:, l] = jnp.dot(c, fan_ref[:, l], preferred_element_type=F32)

def rows8(t):
    return pl.ds(pl.multiple_of(t * 8, 8), 8)

def ends_kernel(cd, tc, delta_ref, w_ref, ds_ref, coef_ref, rate_ref, fan_ref, hs_ref, cum_ref, e_ref, g_ref, tot_ref, p_scr, splat):
    ch = pl.program_id(1)
    tiles = cd // 128
    @pl.when(ch == 0)
    def _():
        e_ref[...] = jnp.zeros_like(e_ref)
        g_ref[...] = jnp.zeros_like(g_ref)
        tot_ref[...] = jnp.zeros_like(tot_ref)
        p_scr[...] = jnp.ones_like(p_scr)
    hs_ref[...] = e_ref[...].reshape(hs_ref.shape)
    cum_ref[...] = tot_ref[...].reshape(cum_ref.shape)
    spread(coef_ref, fan_ref, splat, tc)
    group = 4
    for tile in range(tiles):
        lanes = pl.ds(tile * 128, 128)
        for n0 in range(0, STATE, group):
            rates = [rate_ref[(n0 + i) * 8:(n0 + i + 1) * 8, lanes] for i in range(group)]
            def body(t, carry):
                hs, ps, gs = carry
                tok = pl.ds(pl.multiple_of(t * 8, 8), 8)
                d, w, s = delta_ref[t, :, lanes], w_ref[t, :, lanes], ds_ref[t, :, lanes]
                nh, np_, ng = [], [], []
                for i in range(group):
                    a = jnp.exp2(d * rates[i])
                    cin = splat[rows8(t), pl.ds((n0 + i) * 128, 128)]
                    cout = splat[rows8(t), pl.ds((STATE + n0 + i) * 128, 128)]
                    nh.append(a * hs[i] + cin * w)
                    p = ps[i] * a
                    np_.append(p)
                    ng.append(gs[i] + p * (cout * s))
                return tuple(nh), tuple(np_), tuple(ng)
            rows = [pl.ds((n0 + i) * 8, 8) for i in range(group)]
            init = (tuple(e_ref[0, r, lanes] for r in rows), tuple(p_scr[r, lanes] for r in rows), tuple(g_ref[0, r, lanes] for r in rows))
            hs, ps, gs = lax.fori_loop(0, tc, body, init, unroll=tc)
            for i, r in enumerate(rows):
                e_ref[0, r, lanes] = hs[i]
                p_scr[r, lanes] = ps[i]
                g_ref[0, r, lanes] = gs[i]
        def total(t, acc):
            return acc + delta_ref[t, :, lanes]
        tot_ref[0, :, lanes] = lax.fori_loop(0, tc, total, tot_ref[0, :, lanes], unroll=tc)

def scan_ends(delta, w, ds, coef, rate, fan, tc=STEPS, vmem=48 * 2**20):
    tokens, members, cd = delta.shape
    sg, nch = members // 8, tokens // tc
    rows = STATE * 8
    tok = lambda width: pl.BlockSpec((tc, 8, width), lambda s, c: (c, s, 0))
    keep = lambda r: pl.BlockSpec((1, r, cd), lambda s, c: (s, 0, 0))
    return pl.pallas_call(
        functools.partial(ends_kernel, cd, tc),
        grid=(sg, nch),
        in_specs=[tok(cd), tok(cd), tok(cd), pl.BlockSpec((tc, 8, 128), lambda s, c: (c, s, 0)), pl.BlockSpec((rows, cd), lambda s, c: (0, 0)), pl.BlockSpec(fan.shape, lambda s, c: (0, 0))],
        out_specs=[pl.BlockSpec((1, 1, rows, cd), lambda s, c: (s, c, 0, 0)), pl.BlockSpec((1, 1, 8, cd), lambda s, c: (s, c, 0, 0)), keep(rows), keep(rows), keep(8)],
        out_shape=[jax.ShapeDtypeStruct((sg, nch, rows, cd), F32), jax.ShapeDtypeStruct((sg, nch, 8, cd), F32),
                   jax.ShapeDtypeStruct((sg, rows, cd), F32), jax.ShapeDtypeStruct((sg, rows, cd), F32), jax.ShapeDtypeStruct((sg, 8, cd), F32)],
        scratch_shapes=[pltpu.VMEM((rows, cd), F32), pltpu.VMEM((tc * 8, 2 * STATE * 128), F32)],
        compiler_params=pltpu.CompilerParams(vmem_limit_bytes=vmem),
        name="segment_ends",
    )(delta, w, ds, coef, rate, fan)

def sweep_kernel(cd, tc, delta_ref, w_ref, ds_ref, coef_ref, rate_ref, fan_ref, fold_ref, hs_ref, cum_ref, sin_ref, gin_ref,
                 y_ref, a_ref, s_ref, dc_ref, rs_ref, hist, h_scr, g_scr, splat, acc_in, acc_out):
    ch = pl.program_id(1)
    tiles = cd // 128
    @pl.when(ch == 0)
    def _():
        rs_ref[...] = jnp.zeros_like(rs_ref)
        g_scr[...] = gin_ref[0]
    spread(coef_ref, fan_ref, splat, tc)
    at = [pl.ds(tile * 128, 128) for tile in range(tiles)]
    nt = [(n, i) for n in range(STATE) for i in range(tiles)]

    for n0 in range(0, STATE, 4):
        pairs = [(n, i) for n in range(n0, n0 + 4) for i in range(tiles)]
        init = tuple(hs_ref[0, 0, pl.ds(n * 8, 8), at[i]] + jnp.exp2(cum_ref[0, 0, :, at[i]] * rate_ref[pl.ds(n * 8, 8), at[i]]) * sin_ref[0, pl.ds(n * 8, 8), at[i]] for n, i in pairs)
        def forward(t, hs, n0=n0, pairs=pairs):
            d = [delta_ref[t, :, l] for l in at]
            w = [w_ref[t, :, l] for l in at]
            s = [ds_ref[t, :, l] for l in at]
            y = [None] * tiles if n0 == 0 else [y_ref[t, :, l] for l in at]
            out = []
            for n in range(n0, n0 + 4):
                cin = splat[rows8(t), pl.ds(n * 128, 128)]
                cout = splat[rows8(t), pl.ds((STATE + n) * 128, 128)]
                acc = None
                for i in range(tiles):
                    r = pl.ds(n * 8, 8)
                    old = hs[len(out)]
                    hist[t, r, at[i]] = old
                    h = jnp.exp2(d[i] * rate_ref[r, at[i]]) * old + cin * w[i]
                    out.append(h)
                    y[i] = cout * h if n == 0 else y[i] + cout * h
                    acc = s[i] * h if i == 0 else acc + s[i] * h
                acc_out[rows8(t), pl.ds(n * 128, 128)] = acc
            for i in range(tiles):
                y_ref[t, :, at[i]] = y[i]
            return tuple(out)
        lax.fori_loop(0, tc, forward, init, unroll=tc)

    for n0 in range(0, STATE, 2):
        pairs = [(n, i) for n in range(n0, n0 + 2) for i in range(tiles)]
        init = (tuple(g_scr[pl.ds(n * 8, 8), at[i]] for n, i in pairs), tuple(rs_ref[0, pl.ds(n * 8, 8), at[i]] for n, i in pairs))
        def backward(k, carry, n0=n0, pairs=pairs):
            gs, rs = carry
            t = tc - 1 - k
            d = [delta_ref[t, :, l] for l in at]
            w = [w_ref[t, :, l] for l in at]
            s = [ds_ref[t, :, l] for l in at]
            da = [None] * tiles if n0 == 0 else [a_ref[t, :, l] for l in at]
            cs = [None] * tiles if n0 == 0 else [s_ref[t, :, l] for l in at]
            ng, nr = [], []
            for n in range(n0, n0 + 2):
                cin = splat[rows8(t), pl.ds(n * 128, 128)]
                cout = splat[rows8(t), pl.ds((STATE + n) * 128, 128)]
                acc = None
                for i in range(tiles):
                    r = pl.ds(n * 8, 8)
                    rate = rate_ref[r, at[i]]
                    j = len(ng)
                    a = jnp.exp2(d[i] * rate)
                    g = gs[j] + cout * s[i]
                    ga = g * a
                    ng.append(ga)
                    th = ga * hist[t, r, at[i]]
                    da[i] = th * rate if n == 0 else da[i] + th * rate
                    cs[i] = cin * g if n == 0 else cs[i] + cin * g
                    acc = g * w[i] if i == 0 else acc + g * w[i]
                    nr.append(rs[j] + th * d[i])
                acc_in[rows8(t), pl.ds(n * 128, 128)] = acc
            for i in range(tiles):
                a_ref[t, :, at[i]] = da[i]
                s_ref[t, :, at[i]] = cs[i]
            return tuple(ng), tuple(nr)
        gs, rs = lax.fori_loop(0, tc, backward, init, unroll=tc)
        for j, (n, i) in enumerate(pairs):
            g_scr[pl.ds(n * 8, 8), at[i]] = gs[j]
            rs_ref[0, pl.ds(n * 8, 8), at[i]] = rs[j]
    sums = jnp.dot(acc_in[...].astype(BF16), fold_ref[0], preferred_element_type=F32) + jnp.dot(acc_out[...].astype(BF16), fold_ref[1], preferred_element_type=F32)
    dc_ref[...] = sums.reshape(tc, 8, 128)

def scan_sweep(delta, w, ds, coef, rate, fan, fold, hs, cum, s_in, g_in, tc=STEPS, vmem=56 * 2**20):
    tokens, members, cd = delta.shape
    sg, nch = members // 8, tokens // tc
    rows = STATE * 8
    tok = lambda width: pl.BlockSpec((tc, 8, width), lambda s, c: (nch - 1 - c, s, 0))
    keep = lambda r: pl.BlockSpec((1, r, cd), lambda s, c: (s, 0, 0))
    cf = pl.BlockSpec((tc, 8, 128), lambda s, c: (nch - 1 - c, s, 0))
    f32 = F32
    return pl.pallas_call(
        functools.partial(sweep_kernel, cd, tc),
        grid=(sg, nch),
        in_specs=[tok(cd), tok(cd), tok(cd), cf, pl.BlockSpec((rows, cd), lambda s, c: (0, 0)), pl.BlockSpec(fan.shape, lambda s, c: (0, 0)), pl.BlockSpec(fold.shape, lambda s, c: (0, 0, 0)),
                  pl.BlockSpec((1, 1, rows, cd), lambda s, c: (s, nch - 1 - c, 0, 0)), pl.BlockSpec((1, 1, 8, cd), lambda s, c: (s, nch - 1 - c, 0, 0)), keep(rows), keep(rows)],
        out_specs=[tok(cd), tok(cd), tok(cd), cf, keep(rows)],
        out_shape=[jax.ShapeDtypeStruct(delta.shape, f32)] * 3 + [jax.ShapeDtypeStruct((tokens, members, 128), f32), jax.ShapeDtypeStruct((sg, rows, cd), f32)],
        scratch_shapes=[pltpu.VMEM((tc, rows, cd), f32), pltpu.VMEM((rows, cd), f32), pltpu.VMEM((rows, cd), f32), pltpu.VMEM((tc * 8, 2 * STATE * 128), f32), pltpu.VMEM((tc * 8, STATE * 128), f32), pltpu.VMEM((tc * 8, STATE * 128), f32)],
        compiler_params=pltpu.CompilerParams(vmem_limit_bytes=vmem),
        name="segment_sweep",
    )(delta, w, ds, coef, rate, fan, fold, hs, cum, s_in, g_in)


def rounded(value):
    return lax.reduce_precision(value, 8, 7)


def silu_slope(value):
    sigma = jax.nn.sigmoid(value)
    return sigma * (1.0 + value * (1.0 - sigma))


def contract_rows(left, right):
    return lax.dot_general(left, right, (((0,), (0,)), ((), ())), preferred_element_type=F32)


def contract_cols(left, right):
    return lax.dot_general(left, right, (((1,), (1,)), ((), ())), preferred_element_type=F32)


def dot(left, right):
    return jnp.dot(left, right, preferred_element_type=F32)


def spread_tables():
    fan = np.zeros((128, 2 * STATE * 128), np.float32)
    for k in range(2 * STATE):
        fan[k, k * 128:(k + 1) * 128] = 1
        fan[2 * STATE + k, k * 128:(k + 1) * 128] = 1
    fold = np.zeros((2, STATE * 128, 128), np.float32)
    for n in range(STATE):
        fold[0, n * 128:(n + 1) * 128, n] = 1
        fold[1, n * 128:(n + 1) * 128, STATE + n] = 1
    return jnp.asarray(fan, BF16), jnp.asarray(fold, BF16)


def shards(grid, hidden_in, norm_gain, in_proj, conv_weight, conv_bias, state_proj, delta_proj, delta_bias,
           decay_log, skip_gain, out_proj, cotangent):
    F, C, Z = grid.fsdp, grid.members, grid.planes
    tokens = hidden_in.shape[1]
    rows = in_proj.shape[0]
    block = out_proj.shape[0]
    chans = Z * block
    z, q, f = grid.here()

    hidden = hidden_in.reshape(tokens, D).astype(F32)
    cot_rows = cotangent.reshape(tokens, D)
    inv_rms = lax.rsqrt(jnp.mean(hidden * hidden, axis=1, keepdims=True) + EPS)
    unit = hidden * inv_rms
    gain_rows = rounded(norm_gain)
    gain_tile = jnp.broadcast_to(jnp.pad(gain_rows, (0, 128 - rows))[None, :], (8, 128))
    gains = everyone(grid, gain_tile)[:, 0, :rows].reshape(D)
    normed = (unit * gains[None, :]).astype(BF16)

    in_low = rounded(in_proj).astype(BF16)
    wi = in_low.reshape(rows, 2, Z, C, block).transpose(3, 0, 1, 2, 4).reshape(C, rows, 2 * chans)
    small = jnp.concatenate(
        [conv_weight, conv_bias[None], delta_bias[None], skip_gain[None], decay_log, jnp.zeros((9, block), F32), delta_proj, state_proj.T], axis=0
    ).astype(BF16)
    normed_all, cot_all, wi_all, wo_all, small_all = gather_all(grid, normed, cot_rows, wi, out_proj.astype(BF16), small)
    count = C * tokens
    normed_all = normed_all.reshape(count, D)
    cot_all = cot_all.reshape(count, D)
    w_in = wi_all.reshape(D, 2 * chans)
    w_out = wo_all.reshape(chans, D)
    small_all = small_all.transpose(1, 0, 2).reshape(small.shape[0], chans)
    taps = small_all[:KW].astype(F32)
    conv_shift = small_all[KW].astype(F32)
    delta_shift = small_all[KW + 1].astype(F32)
    skip = small_all[KW + 2].astype(F32)
    decay_rate = -jnp.exp(small_all[KW + 3:KW + 3 + STATE].astype(F32))
    w_delta = small_all[32:32 + DT_RANK]
    w_state = small_all[32 + DT_RANK:]
    rate8 = jnp.repeat(decay_rate * LOG2E, 8, axis=0)

    def by_step(value):
        return value.reshape(C, tokens, -1).transpose(1, 0, 2)

    def by_member(value):
        return value.transpose(1, 0, 2).reshape(count, -1)

    mixed = by_step(dot(normed_all, w_in).astype(BF16))
    conv_in = mixed[:, :, :chans]
    gate = mixed[:, :, chans:].astype(F32)
    edge_rows = -(-(KW - 1) * F // 16) * 16
    tail = conv_in[tokens - (KW - 1):, C - F:].reshape((KW - 1) * F, chans)
    tails = line_gather(grid, [jnp.pad(tail, ((0, edge_rows - (KW - 1) * F), (0, 0)))], 3, "conv_edges")[0]
    before = lax.dynamic_index_in_dim(tails, jnp.maximum(z - 1, 0), 0, False)[: (KW - 1) * F]
    before = jnp.where(z > 0, before, jnp.zeros_like(before)).reshape(KW - 1, F, chans)
    edge = jnp.concatenate([before, conv_in[tokens - (KW - 1):, : C - F]], axis=1)
    padded = jnp.concatenate([edge, conv_in], axis=0).astype(F32)
    conv_out = jnp.broadcast_to(conv_shift, (tokens, C, chans))
    for k in range(KW):
        conv_out = conv_out + taps[k] * padded[k:k + tokens]
    act = rounded(jax.nn.silu(conv_out))
    act_rows = lax.optimization_barrier(act.astype(BF16).reshape(count, chans))
    pad_lanes = 256 - DT_RANK - 2 * STATE
    selected = contract_cols(act_rows, jnp.pad(w_state, ((0, pad_lanes), (0, 0))))
    selected = plane_sum(grid, selected, 4)
    delta_in = selected[:, :DT_RANK]
    coef = selected[:, DT_RANK:].reshape(tokens, C, 128)
    delta_pre = (dot(delta_in, w_delta) + delta_shift).reshape(tokens, C, chans)
    delta = jax.nn.softplus(delta_pre)
    drive = delta * act
    gate_act = jax.nn.silu(gate)
    d_gated = lax.optimization_barrier(by_step(contract_cols(cot_all, w_out)))
    d_scanned = d_gated * gate_act

    fan, fold = spread_tables()
    starts, elapsed, ends, adjoints, totals = scan_ends(delta, drive, d_scanned, coef, rate8, fan)
    def by_segment(value):
        groups = C // 8
        value = value.reshape(groups, -1, 8, chans).transpose(0, 2, 1, 3)
        return value.reshape(4, F, -1, chans)

    def by_sublane(value):
        return value.reshape(C // 8, 8, STATE, chans).transpose(0, 2, 1, 3).reshape(C // 8, STATE * 8, chans)

    totals = by_segment(totals)
    kept, ends, adjoints = jnp.exp(decay_rate * totals), by_segment(ends), by_segment(adjoints)
    end = ends[0]
    for c in range(1, 4):
        end = kept[c] * end + ends[c]
    adj = adjoints[3]
    for c in reversed(range(3)):
        adj = kept[c] * adj + adjoints[c]
    flat = [end.reshape(F * STATE, chans), adj.reshape(F * STATE, chans), jnp.broadcast_to(jnp.sum(totals, axis=0), (F, 8, chans)).reshape(F * 8, chans)]
    all_end, all_adj, all_tot = line_gather(grid, flat, 5, "segment_states")
    plane_kept = jnp.exp(decay_rate * all_tot.reshape(Z, F, 8, chans)[:, :, :1])
    all_end, all_adj = all_end.reshape(Z, F, STATE, chans), all_adj.reshape(Z, F, STATE, chans)
    state = jnp.zeros((F, STATE, chans), F32)
    adj = state
    for p in range(Z - 1):
        state = jnp.where(p < z, plane_kept[p] * state + all_end[p], state)
    for p in reversed(range(1, Z)):
        adj = jnp.where(p > z, plane_kept[p] * adj + all_adj[p], adj)
    before_state, after_adj = [], []
    for c in range(4):
        before_state.append(state)
        state = kept[c] * state + ends[c]
    for c in reversed(range(4)):
        after_adj.append(adj)
        adj = kept[c] * adj + adjoints[c]
    after_adj.reverse()

    y, d_delta_a, coef_sum, d_coef, rate_sum = scan_sweep(
        delta, drive, d_scanned, coef, rate8, fan, fold, starts, elapsed, by_sublane(jnp.stack(before_state)), by_sublane(jnp.stack(after_adj))
    )
    decay_grad = rate_sum.reshape(C // 8, STATE, 8, chans).sum(axis=(0, 2)) * decay_rate
    scanned = y + skip * act
    gated = (scanned * gate_act).astype(BF16)
    d_gate = d_gated * scanned * silu_slope(gate)
    skip_grad = jnp.sum(d_scanned * act, axis=(0, 1))
    d_delta_pre = (d_delta_a * (1.0 / LOG2E) + act * coef_sum) * jax.nn.sigmoid(delta_pre)
    shift_grad = jnp.sum(d_delta_pre, axis=(0, 1))
    d_delta_low = d_delta_pre.astype(BF16).reshape(count, chans)
    dproj_grad = contract_rows(delta_in, d_delta_low)
    d_delta_in = contract_cols(d_delta_low, w_delta)
    d_selected = plane_sum(grid, jnp.concatenate([d_delta_in, d_coef.reshape(count, 128)], axis=1), 6)
    d_selected = d_selected[:, :DT_RANK + 2 * STATE]
    sproj_grad = contract_rows(d_selected, act_rows)
    d_activated = delta * coef_sum + skip * d_scanned + dot(d_selected, w_state).reshape(tokens, C, chans)
    d_conv = d_activated * silu_slope(conv_out)
    cbias_grad = jnp.sum(d_conv, axis=(0, 1))
    kernel_grad = jnp.stack([jnp.sum(d_conv * padded[k:k + tokens], axis=(0, 1)) for k in range(KW)])
    head = d_conv[:KW - 1, :F].reshape((KW - 1) * F, chans)
    head_rows = -(-(KW - 1) * F // 8) * 8
    heads = line_gather(grid, [jnp.pad(head, ((0, head_rows - (KW - 1) * F), (0, 0)))], 7, "conv_grad_edges")[0]
    after = lax.dynamic_index_in_dim(heads, jnp.minimum(z + 1, Z - 1), 0, False)[: (KW - 1) * F]
    after = jnp.where(z < Z - 1, after, jnp.zeros_like(after)).reshape(KW - 1, F, chans)
    edge_grad = jnp.concatenate([d_conv[:KW - 1, F:], after], axis=1)
    grad_padded = jnp.concatenate([d_conv, edge_grad], axis=0)
    d_conv_in = jnp.zeros((tokens, C, chans), F32)
    for k in range(KW):
        d_conv_in = d_conv_in + taps[k] * grad_padded[KW - 1 - k:KW - 1 - k + tokens]
    d_mixed = by_member(jnp.concatenate([d_conv_in, d_gate], axis=2).astype(BF16))
    gated = by_member(lax.optimization_barrier(gated))

    in_part = contract_rows(normed_all, d_mixed).astype(BF16).reshape(Z * C, rows, 2 * chans)
    out_part = contract_rows(gated, cot_all).astype(BF16).reshape(Z, block, D)
    half = D // 2
    core = q % 2
    w_out_mine = lax.dynamic_slice_in_dim(w_out, core * half, half, 1)
    w_out_twin = lax.dynamic_slice_in_dim(w_out, (1 - core) * half, half, 1)
    w_in_mine = lax.dynamic_slice_in_dim(w_in, core * half, half, 0)
    w_in_twin = lax.dynamic_slice_in_dim(w_in, (1 - core) * half, half, 0)
    twin_out = dot(gated, w_out_twin).astype(BF16)
    twin_in = contract_cols(d_mixed, w_in_twin).astype(BF16)
    from_out, from_in = twin_swap(grid, [twin_out, twin_in], 8)
    part_out = (dot(gated, w_out_mine) + from_out.astype(F32)).astype(BF16).reshape(C, tokens, half)
    part_in = (contract_cols(d_mixed, w_in_mine) + from_in.astype(F32)).astype(BF16).reshape(C, tokens, half)

    fine = jnp.concatenate([kernel_grad, cbias_grad[None], shift_grad[None], skip_grad[None], decay_grad, jnp.zeros((9, chans), F32)], axis=0)
    fine = fine.reshape(32, Z, block).transpose(1, 0, 2)
    coarse = jnp.concatenate([dproj_grad, sproj_grad], axis=0).astype(BF16)
    coarse = coarse.reshape(-1, Z, block).transpose(1, 0, 2)
    got = to_owners(grid, in_part, [part_out, part_in], [out_part, coarse, fine], 9)
    in_grad = got[0].astype(F32).reshape(Z, C, rows, 2, Z, block).sum(axis=0)
    in_grad = in_grad.transpose(1, 2, 3, 0, 4).reshape(rows, 2 * DI)

    def owned(value):
        value = value.astype(F32).reshape(2, 2, F, tokens, half).sum(axis=(0, 2))
        return jnp.concatenate([value[0], value[1]], axis=1)

    block_out = (hidden + owned(got[1])).astype(BF16)
    d_unit = owned(got[2]) * gains[None, :]
    out_grad = got[3].astype(F32).sum(axis=0)
    coarse = got[4].astype(F32).sum(axis=0)
    fine = got[5].sum(axis=0)
    gain_grad = jnp.sum(rounded(in_proj) * in_grad, axis=1) / gain_rows
    mean_term = jnp.mean(d_unit * unit, axis=1, keepdims=True)
    input_grad = (cot_rows.astype(F32) + inv_rms * (d_unit - unit * mean_term)).astype(BF16)
    return (
        block_out.reshape(1, tokens, D),
        input_grad.reshape(1, tokens, D),
        gain_grad,
        in_grad,
        fine[:KW],
        fine[KW],
        coarse[DT_RANK:].T,
        coarse[:DT_RANK],
        fine[KW + 1],
        fine[KW + 3:KW + 3 + STATE],
        fine[KW + 2],
        out_grad,
    )


def everyone_kernel(grid, in_ref, out_ref, local, send, recv):
    z, q, f = grid.here()
    C, N = grid.members, grid.devices
    lin = z * C + q * grid.fsdp + f
    barrier = pltpu.get_barrier_semaphore()

    def copy(d):
        other = lax.rem(lin + d, N)
        where = grid.member(other // C, lax.rem(other, C))
        return remote(in_ref, out_ref.at[lin], send.at[d], recv.at[d], where), where

    @pl.loop(1, N)
    def _(d):
        pl.semaphore_signal(barrier, inc=1, device_id=copy(d)[1], device_id_type=MESH)

    pl.semaphore_wait(barrier, N - 1)

    @pl.loop(1, N)
    def _(d):
        copy(d)[0].start()

    mine = pltpu.make_async_copy(in_ref, out_ref.at[lin], local)
    mine.start()
    mine.wait()

    @pl.loop(1, N)
    def _(d):
        back = lax.rem(lin + N - d, N)
        remote(in_ref, out_ref.at[back], send.at[d], recv.at[d], grid.member(back // C, lax.rem(back, C))).wait_recv()
        copy(d)[0].wait_send()


def everyone(grid, value):
    dma = pltpu.SemaphoreType.DMA
    N = grid.devices
    return comm_call(
        functools.partial(everyone_kernel, grid),
        [jax.ShapeDtypeStruct((N,) + value.shape, value.dtype)],
        [dma, dma((N,)), dma((N,))], 10, "gather_gain", (value,),
    )[0]


def solution(mesh):
    grid = Grid(mesh.shape["ctx"], mesh.shape["fsdp"])
    both = ("ctx", "fsdp")
    tokens, flat, by_row, by_col = P("fsdp", "ctx", None), P(both), P(both, None), P(None, both)
    in_specs = (tokens, flat, by_row, by_col, flat, by_row, by_col, flat, by_col, flat, by_row, tokens)
    out_specs = (tokens, tokens, flat, by_row, by_col, flat, by_row, by_col, flat, by_col, flat, by_row)
    return jax.shard_map(functools.partial(shards, grid), mesh=mesh, in_specs=in_specs, out_specs=out_specs, check_vma=False)
```

```python
import functools

import jax
import jax.numpy as jnp
import numpy as np
from jax import lax
from jax.experimental import pallas as pl
from jax.experimental.pallas import tpu as pltpu
from jax.sharding import PartitionSpec as P

D = 2048
DI = 4096
STATE = 16
DT_RANK = 128
KW = 4
EPS = 1e-05
LOG2E = 1.4426950408889634
STEPS = 16
MESH = pl.DeviceIdType.MESH
BF16 = jnp.bfloat16
F32 = jnp.float32


class Grid:
    def __init__(self, ctx, fsdp):
        self.ctx, self.fsdp = ctx, fsdp
        self.planes = ctx // 4
        self.members = 4 * fsdp
        self.devices = ctx * fsdp

    def here(self):
        c, f = lax.axis_index("ctx"), lax.axis_index("fsdp")
        return c // 4, c % 4, f

    def at(self, z, q, f):
        return {"ctx": z * 4 + q, "fsdp": f}

    def member(self, z, j):
        return self.at(z, j // self.fsdp, j % self.fsdp)


def remote(src, dst, send, recv, where):
    return pltpu.make_async_remote_copy(
        src_ref=src, dst_ref=dst, send_sem=send, recv_sem=recv, device_id=where, device_id_type=MESH
    )


def greet(places):
    barrier = pltpu.get_barrier_semaphore()
    for place in places:
        pl.semaphore_signal(barrier, inc=1, device_id=place, device_id_type=MESH)
    pl.semaphore_wait(barrier, len(places))


def comm_call(kernel, outs, scratch, ident, name, args, vmem=None, in_vmem=()):
    spaces = [pl.BlockSpec(memory_space=pltpu.VMEM if i in in_vmem else pl.ANY) for i in range(len(args))]
    return pl.pallas_call(
        kernel,
        in_specs=spaces,
        out_specs=[pl.BlockSpec(memory_space=pl.ANY)] * len(outs),
        out_shape=outs,
        scratch_shapes=scratch,
        compiler_params=pltpu.CompilerParams(
            collective_id=ident, has_side_effects=True, vmem_limit_bytes=vmem or 16 * 2**20
        ),
        name=name,
    )(*args)


def gather_kernel(grid, rows, h_ref, g_ref, c_ref, wi_ref, sm_ref, n_all, c_all, wi_all, sm_all, gain_out,
                  gain_buf, gains, n_low, local, g_send, g_recv, n_send, n_recv, c_send, c_recv, a_send, a_recv,
                  z_send, z_recv, s_send, s_recv):
    z, q, f = grid.here()
    F, C, Z, N = grid.fsdp, grid.members, grid.planes, grid.devices
    me = q * F + f
    lin = z * C + me
    opposite, twin = q ^ 2, q ^ 1
    barrier = pltpu.get_barrier_semaphore()

    def other(d):
        to = lax.rem(lin + d, N)
        return grid.member(to // C, lax.rem(to, C))

    @pl.loop(1, N)
    def _(d):
        pl.semaphore_signal(barrier, inc=1, device_id=other(d), device_id_type=MESH)

    pl.semaphore_wait(barrier, N - 1)

    def gain_copy(d):
        return remote(g_ref, gain_buf.at[lin], g_send.at[d], g_recv.at[d], other(d))

    @pl.loop(1, N)
    def _(d):
        gain_copy(d).start()

    sends = []

    def push(copy):
        copy.start()
        sends.append(copy)

    def block_of(i):
        return lax.rem(me + C - i, C)

    def line_pair(step, i):
        right, left = z - step, z + step
        if step == 0 and i == 0:
            src_right = src_left = wi_ref.at[me]
        else:
            src_right, src_left = wi_all.at[right * C + block_of(i)], wi_all.at[left * C + block_of(i)]
        return (
            (z < Z - 1) & (right >= 0),
            remote(src_right, wi_all.at[right * C + block_of(i)], z_send.at[0, step, i], z_recv.at[0, step, i], grid.at(z + 1, q, f)),
            (z > 0) & (left <= Z - 1),
            remote(src_left, wi_all.at[left * C + block_of(i)], z_send.at[1, step, i], z_recv.at[1, step, i], grid.at(z - 1, q, f)),
        )

    def line_start(step, i):
        to_right, right, to_left, left = line_pair(step, i)

        @pl.when(to_right)
        def _():
            right.start()

        @pl.when(to_left)
        def _():
            left.start()

    def line_done(step, i):
        to_right, right, to_left, left = line_pair(step, i)

        @pl.when(to_right)
        def _():
            right.wait_send()

        @pl.when(to_left)
        def _():
            left.wait_send()

    def line_arrived(step, i):
        from_left, from_right = z - 1 - step, z + 1 + step

        @pl.when(from_left >= 0)
        def _():
            ref = wi_all.at[from_left * C + block_of(i)]
            remote(ref, ref, z_send.at[0, step, i], z_recv.at[0, step, i], grid.at(z - 1, q, f)).wait_recv()

        @pl.when(from_right <= Z - 1)
        def _():
            ref = wi_all.at[from_right * C + block_of(i)]
            remote(ref, ref, z_send.at[1, step, i], z_recv.at[1, step, i], grid.at(z + 1, q, f)).wait_recv()

    line_start(0, 0)
    for d in range(1, C):
        j = lax.rem(me + d, C)
        push(remote(wi_ref.at[j], wi_all.at[lin], a_send.at[d], a_recv.at[d], grid.member(z, j)))
    for d in range(1, Z):
        push(remote(sm_ref, sm_all.at[z], s_send.at[d], s_recv.at[d], grid.at(lax.rem(z + d, Z), q, f)))

    n_sent, c_sent = [0], [0]

    def push_n(block, src, where):
        push(remote(src, n_all.at[block], n_send.at[n_sent[0]], n_recv.at[block], where))
        n_sent[0] += 1

    def push_c(block, src, where):
        push(remote(src, c_all.at[block], c_send.at[c_sent[0]], c_recv.at[block], where))
        c_sent[0] += 1

    def arrived(ref, sems, block):
        remote(ref.at[block], ref.at[block], n_send.at[0], sems.at[block], grid.at(z, twin, f)).wait_recv()

    others = [lax.rem(f + d, F) for d in range(1, F)]
    push_c(me, c_ref, grid.at(z, opposite, f))

    gain_buf[lin] = g_ref[...]

    @pl.loop(1, N)
    def _(d):
        back = lax.rem(lin + N - d, N)
        remote(g_ref, gain_buf.at[back], g_send.at[d], g_recv.at[d], grid.member(back // C, lax.rem(back, C))).wait_recv()

    per = max(1, 128 // rows)
    for chunk in range(D // 128):
        gain = gain_buf[chunk * per]
        for k in range(1, per):
            gain = gain + gain_buf[chunk * per + k]
        gains[:, chunk * 128:(chunk + 1) * 128] = gain

    @pl.loop(0, h_ref.shape[0] // 16)
    def _(r):
        at = pl.ds(pl.multiple_of(r * 16, 16), 16)
        hidden = h_ref[at, :].astype(F32)
        scale = lax.rsqrt(jnp.mean(hidden * hidden, axis=1, keepdims=True) + EPS)
        n_low[at, :] = (hidden * scale * gains[0:1, :]).astype(BF16)

    for g in others:
        push_n(me, n_low, grid.at(z, q, g))
    push_n(me, n_low, grid.at(z, opposite, f))
    for g in others:
        push_c(me, c_ref, grid.at(z, q, g))
    push_n(me, n_low, grid.at(z, twin, f))
    push_c(me, c_ref, grid.at(z, twin, f))
    mine = [
        pltpu.make_async_copy(n_low, n_all.at[me], local.at[0]),
        pltpu.make_async_copy(c_ref, c_all.at[me], local.at[1]),
        pltpu.make_async_copy(wi_ref.at[me], wi_all.at[lin], local.at[2]),
        pltpu.make_async_copy(sm_ref, sm_all.at[z], local.at[3]),
        pltpu.make_async_copy(gains, gain_out, local.at[4]),
    ]
    for copy in mine:
        copy.start()
    for d in range(1, C):
        back = block_of(d)
        remote(wi_ref.at[me], wi_all.at[z * C + back], a_send.at[d], a_recv.at[d], grid.member(z, back)).wait_recv()
        line_start(0, d)
    mine[2].wait()

    def pass_on(step, blocks):
        for i in blocks:
            line_arrived(step, i)
            if step < Z - 2:
                line_start(step + 1, i)

    pass_on(0, range(C // 2))
    for g in others:
        block = q * F + g
        arrived(n_all, n_recv, block)
        push_n(block, n_all.at[block], grid.at(z, opposite, f))
        push_n(block, n_all.at[block], grid.at(z, twin, f))
    arrived(c_all, c_recv, opposite * F + f)
    for g in others:
        push_c(opposite * F + f, c_all.at[opposite * F + f], grid.at(z, q, g))
    push_c(opposite * F + f, c_all.at[opposite * F + f], grid.at(z, twin, f))
    pass_on(0, range(C // 2, C))
    for step in range(1, Z - 2):
        pass_on(step, range(C))
    for g in others:
        arrived(c_all, c_recv, q * F + g)
        push_c(q * F + g, c_all.at[q * F + g], grid.at(z, twin, f))
    for g in [f] + others:
        block = opposite * F + g
        arrived(n_all, n_recv, block)
        push_n(block, n_all.at[block], grid.at(z, twin, f))
    for g in others:
        block = opposite * F + g
        arrived(c_all, c_recv, block)
        push_c(block, c_all.at[block], grid.at(z, twin, f))
    pass_on(Z - 2, range(C))
    for side in (twin, twin ^ 2):
        for g in [f] + others:
            arrived(n_all, n_recv, side * F + g)
            arrived(c_all, c_recv, side * F + g)
    for d in range(1, Z):
        back = lax.rem(z + Z - d, Z)
        remote(sm_ref, sm_all.at[back], s_send.at[d], s_recv.at[d], grid.at(back, q, f)).wait_recv()
    for i in (0, 1, 3, 4):
        mine[i].wait()
    for copy in sends:
        copy.wait_send()
    for step in range(Z - 1):
        for i in range(C):
            line_done(step, i)

    @pl.loop(1, N)
    def _(d):
        gain_copy(d).wait_send()


def gather_all(grid, hidden, gain_tile, cot, wi, small):
    F, C, Z, N = grid.fsdp, grid.members, grid.planes, grid.devices
    tokens, rows = hidden.shape[0], wi.shape[1]
    dma = pltpu.SemaphoreType.DMA
    outs = [
        jax.ShapeDtypeStruct((C, tokens, D), BF16),
        jax.ShapeDtypeStruct((C, tokens, D), BF16),
        jax.ShapeDtypeStruct((Z * C,) + wi.shape[1:], BF16),
        jax.ShapeDtypeStruct((Z,) + small.shape, BF16),
        jax.ShapeDtypeStruct((8, D), F32),
    ]
    count = (F - 1) + F + 2 * F
    scratch = [pltpu.VMEM((N, 8, 128), F32), pltpu.VMEM((8, D), F32), pltpu.VMEM((tokens, D), BF16)]
    scratch += [dma((5,)), dma((N,)), dma((N,)), dma((count,)), dma((C,)), dma((count,)), dma((C,)), dma((C,)), dma((C,))]
    scratch += [dma((2, Z, C)), dma((2, Z, C)), dma((Z,)), dma((Z,))]
    return comm_call(
        functools.partial(gather_kernel, grid, rows), outs, scratch, 1, "gather_weights_and_tokens",
        (hidden, gain_tile, cot, wi, small), in_vmem=(0, 1),
    )


def plane_sum_kernel(grid, part_ref, out_ref, send_buf, recv_buf, result, send, recv, out_send, out_recv, own):
    z, q, f = grid.here()
    C = grid.members
    me = q * grid.fsdp + f
    rows = recv_buf.shape[1]
    greet([grid.member(z, lax.rem(me + d, C)) for d in range(1, C)])
    lane = lax.broadcasted_iota(jnp.int32, (rows, 128), 1)

    def packed(v):
        high = v.astype(BF16).astype(F32)
        return high + pltpu.roll(v - high, 32, 1)

    @pl.loop(0, C)
    def _(k):
        at = pl.ds(pl.multiple_of(k * rows, 16), rows)
        send_buf[k, :, 0:128] = part_ref[at, 0:128].astype(BF16)
        send_buf[k, :, 128:256] = packed(part_ref[at, 128:256]).astype(BF16)

    copies = []
    for d in range(1, C):
        j = lax.rem(me + d, C)
        copy = remote(send_buf.at[j], recv_buf.at[d], send.at[d], recv.at[d], grid.member(z, j))
        copy.start()
        copies.append(copy)
    low = send_buf[me, :, 0:128].astype(F32)
    high = send_buf[me, :, 128:256].astype(F32)
    for d in range(1, C):
        copies[d - 1].wait_recv()
        low = low + recv_buf[d, :, 0:128].astype(F32)
        high = high + recv_buf[d, :, 128:256].astype(F32)
    total = jnp.where(lane < 32, high + pltpu.roll(high, 96, 1), 0.0)
    result[:, 0:128] = low.astype(BF16)
    result[:, 128:256] = packed(total).astype(BF16)
    for copy in copies:
        copy.wait_send()
    mine = pltpu.make_async_copy(result, out_ref.at[me], own)
    mine.start()
    copies = []
    for d in range(1, C):
        j = lax.rem(me + d, C)
        copy = remote(result, out_ref.at[me], out_send.at[d], out_recv.at[d], grid.member(z, j))
        copy.start()
        copies.append(copy)
    mine.wait()
    for d in range(1, C):
        back = lax.rem(me + C - d, C)
        remote(result, out_ref.at[back], out_send.at[d], out_recv.at[d], grid.member(z, back)).wait_recv()
    for copy in copies:
        copy.wait_send()


def plane_sum(grid, part, ident):
    C = grid.members
    rows = part.shape[0] // C
    dma = pltpu.SemaphoreType.DMA
    out = comm_call(
        functools.partial(plane_sum_kernel, grid),
        [jax.ShapeDtypeStruct((C, rows, 256), BF16)],
        [pltpu.VMEM((C, rows, 256), BF16), pltpu.VMEM((C, rows, 256), BF16), pltpu.VMEM((rows, 256), BF16)]
        + [dma((C,))] * 4 + [dma],
        ident, "plane_sum", (part,), vmem=40 * 2**20, in_vmem=(0,),
    )[0]
    return out.reshape(C * rows, 256)


def line_gather_kernel(grid, count, *refs):
    z, q, f = grid.here()
    Z = grid.planes
    ins, outs = refs[:count], refs[count:2 * count]
    local, send, recv = refs[2 * count:]
    greet([grid.at(lax.rem(z + d, Z), q, f) for d in range(1, Z)])
    copies = []
    for i in range(count):
        mine = pltpu.make_async_copy(ins[i], outs[i].at[z], local.at[i])
        mine.start()
        copies.append(mine)
    pushes = []
    for i in range(count):
        for d in range(1, Z):
            copy = remote(ins[i], outs[i].at[z], send.at[i, d], recv.at[i, d], grid.at(lax.rem(z + d, Z), q, f))
            copy.start()
            pushes.append(copy)
    for mine in copies:
        mine.wait()
    for i in range(count):
        for d in range(1, Z):
            back = lax.rem(z + Z - d, Z)
            remote(ins[i], outs[i].at[back], send.at[i, d], recv.at[i, d], grid.at(back, q, f)).wait_recv()
    for copy in pushes:
        copy.wait_send()


def line_gather(grid, arrays, ident, name):
    dma = pltpu.SemaphoreType.DMA
    n, Z = len(arrays), grid.planes
    return comm_call(
        functools.partial(line_gather_kernel, grid, n),
        [jax.ShapeDtypeStruct((Z,) + a.shape, a.dtype) for a in arrays],
        [dma((n,)), dma((n, Z)), dma((n, Z))], ident, name, tuple(arrays),
    )


def owners_kernel(grid, planes_in, lines_in, *refs):
    z, q, f = grid.here()
    C, Z = grid.members, grid.planes
    me = q * grid.fsdp + f
    total = 1 + planes_in + lines_in
    ins, outs = refs[:total], refs[total:2 * total]
    slots, own, result, local, w_send, w_recv, r_send, r_recv, p_send, p_recv, l_send, l_recv = refs[2 * total:]
    greet([grid.member(z, lax.rem(me + d, C)) for d in range(1, C)] + [grid.at(lax.rem(z + d, Z), q, f) for d in range(1, Z)])
    load = pltpu.make_async_copy(ins[0].at[z], own, local.at[0])
    load.start()
    weights, mine, pushes, waits = [], [], [], []
    for d in range(1, Z):
        j = lax.rem(z + d, Z)
        weights.append(remote(ins[0].at[j], slots.at[d], w_send.at[d], w_recv.at[d], grid.at(j, q, f)))
    for copy in weights:
        copy.start()
    for i in range(planes_in):
        mine.append(pltpu.make_async_copy(ins[1 + i].at[me], outs[1 + i].at[me], local.at[1 + i]))
        for d in range(1, C):
            j, back = lax.rem(me + d, C), lax.rem(me + C - d, C)
            pushes.append(remote(ins[1 + i].at[j], outs[1 + i].at[me], p_send.at[i, d], p_recv.at[i, d], grid.member(z, j)))
            waits.append(remote(ins[1 + i].at[me], outs[1 + i].at[back], p_send.at[i, d], p_recv.at[i, d], grid.member(z, back)))
    for i in range(lines_in):
        k = 1 + planes_in + i
        mine.append(pltpu.make_async_copy(ins[k].at[z], outs[k].at[z], local.at[k]))
        for d in range(1, Z):
            j, back = lax.rem(z + d, Z), lax.rem(z + Z - d, Z)
            pushes.append(remote(ins[k].at[j], outs[k].at[z], l_send.at[i, d], l_recv.at[i, d], grid.at(j, q, f)))
            waits.append(remote(ins[k].at[z], outs[k].at[back], l_send.at[i, d], l_recv.at[i, d], grid.at(back, q, f)))
    for copy in pushes + mine:
        copy.start()
    load.wait()
    for copy in weights:
        copy.wait_recv()

    @pl.loop(0, C)
    def _(j):
        value = own[j].astype(F32)
        for d in range(1, Z):
            value = value + slots[d, j].astype(F32)
        result[j] = value.astype(BF16)

    mine.append(pltpu.make_async_copy(result.at[me], outs[0].at[me], local.at[0]))
    mine[-1].start()
    for d in range(1, C):
        j, back = lax.rem(me + d, C), lax.rem(me + C - d, C)
        copy = remote(result.at[j], outs[0].at[me], r_send.at[d], r_recv.at[d], grid.member(z, j))
        copy.start()
        pushes.append(copy)
        waits.append(remote(result.at[me], outs[0].at[back], r_send.at[d], r_recv.at[d], grid.member(z, back)))
    for copy in mine:
        copy.wait()
    for copy in waits:
        copy.wait_recv()
    for copy in pushes + weights:
        copy.wait_send()


def to_owners(grid, weight, plane_arrays, line_arrays, ident):
    dma = pltpu.SemaphoreType.DMA
    C, Z = grid.members, grid.planes
    p, l = len(plane_arrays), len(line_arrays)
    args = (weight,) + tuple(plane_arrays) + tuple(line_arrays)
    part = weight.shape[1:]
    outs = [jax.ShapeDtypeStruct(part, BF16)] + [jax.ShapeDtypeStruct(a.shape, a.dtype) for a in args[1:]]
    return comm_call(
        functools.partial(owners_kernel, grid, p, l), outs,
        [pltpu.VMEM((Z,) + part, BF16), pltpu.VMEM(part, BF16), pltpu.VMEM(part, BF16)]
        + [dma((1 + p + l,)), dma((Z,)), dma((Z,)), dma((C,)), dma((C,)), dma((p, C)), dma((p, C)), dma((l, Z)), dma((l, Z))],
        ident, "to_owners", args,
    )


def place_kernel(grid, *refs):
    z, _, _ = grid.here()
    Z = grid.planes
    for d in range(Z):
        refs[Z][lax.rem(z + Z - d, Z)] = refs[d][...]


def in_place_order(grid, pieces):
    Z = grid.planes
    return pl.pallas_call(
        functools.partial(place_kernel, grid),
        in_specs=[pl.BlockSpec(memory_space=pltpu.VMEM)] * Z,
        out_specs=pl.BlockSpec(memory_space=pltpu.VMEM),
        out_shape=jax.ShapeDtypeStruct((Z,) + pieces[0].shape, pieces[0].dtype),
        compiler_params=pltpu.CompilerParams(vmem_limit_bytes=16 * 2**20),
        name="in_place_order",
    )(*pieces)

def spread(coef_ref, fan_ref, splat, tc):
    c = coef_ref[...].reshape(8 * tc, 128)
    for k in range(0, 2 * STATE, 4):
        l = pl.ds(k * 128, 512)
        splat[:, l] = jnp.dot(c, fan_ref[:, l], preferred_element_type=F32)

def rows8(t):
    return pl.ds(pl.multiple_of(t * 8, 8), 8)

def ends_kernel(cd, tc, delta_ref, w_ref, ds_ref, coef_ref, rate_ref, fan_ref, e_ref, g_ref, tot_ref, p_scr, splat):
    ch = pl.program_id(1)
    tiles = cd // 128
    @pl.when(ch == 0)
    def _():
        e_ref[...] = jnp.zeros_like(e_ref)
        g_ref[...] = jnp.zeros_like(g_ref)
        tot_ref[...] = jnp.zeros_like(tot_ref)
        p_scr[...] = jnp.ones_like(p_scr)
    spread(coef_ref, fan_ref, splat, tc)
    group = 4
    for tile in range(tiles):
        lanes = pl.ds(tile * 128, 128)
        for n0 in range(0, STATE, group):
            rates = [rate_ref[(n0 + i) * 8:(n0 + i + 1) * 8, lanes] for i in range(group)]
            def body(t, carry):
                hs, ps, gs = carry
                tok = pl.ds(pl.multiple_of(t * 8, 8), 8)
                d, w, s = delta_ref[t, :, lanes], w_ref[t, :, lanes], ds_ref[t, :, lanes]
                nh, np_, ng = [], [], []
                for i in range(group):
                    a = jnp.exp2(d * rates[i])
                    cin = splat[rows8(t), pl.ds((n0 + i) * 128, 128)]
                    cout = splat[rows8(t), pl.ds((STATE + n0 + i) * 128, 128)]
                    nh.append(a * hs[i] + cin * w)
                    p = ps[i] * a
                    np_.append(p)
                    ng.append(gs[i] + p * (cout * s))
                return tuple(nh), tuple(np_), tuple(ng)
            rows = [pl.ds((n0 + i) * 8, 8) for i in range(group)]
            init = (tuple(e_ref[0, r, lanes] for r in rows), tuple(p_scr[r, lanes] for r in rows), tuple(g_ref[0, r, lanes] for r in rows))
            hs, ps, gs = lax.fori_loop(0, tc, body, init, unroll=tc)
            for i, r in enumerate(rows):
                e_ref[0, r, lanes] = hs[i]
                p_scr[r, lanes] = ps[i]
                g_ref[0, r, lanes] = gs[i]
        def total(t, acc):
            return acc + delta_ref[t, :, lanes]
        tot_ref[0, :, lanes] = lax.fori_loop(0, tc, total, tot_ref[0, :, lanes], unroll=tc)

def scan_ends(delta, w, ds, coef, rate, fan, tc=STEPS, vmem=48 * 2**20):
    tokens, members, cd = delta.shape
    sg, nch = members // 8, tokens // tc
    rows = STATE * 8
    tok = lambda width: pl.BlockSpec((tc, 8, width), lambda s, c: (c, s, 0))
    keep = lambda r: pl.BlockSpec((1, r, cd), lambda s, c: (s, 0, 0))
    return pl.pallas_call(
        functools.partial(ends_kernel, cd, tc),
        grid=(sg, nch),
        in_specs=[tok(cd), tok(cd), tok(cd), pl.BlockSpec((tc, 8, 128), lambda s, c: (c, s, 0)), pl.BlockSpec((rows, cd), lambda s, c: (0, 0)), pl.BlockSpec(fan.shape, lambda s, c: (0, 0))],
        out_specs=[keep(rows), keep(rows), keep(8)],
        out_shape=[jax.ShapeDtypeStruct((sg, rows, cd), F32), jax.ShapeDtypeStruct((sg, rows, cd), F32), jax.ShapeDtypeStruct((sg, 8, cd), F32)],
        scratch_shapes=[pltpu.VMEM((rows, cd), F32), pltpu.VMEM((tc * 8, 2 * STATE * 128), F32)],
        compiler_params=pltpu.CompilerParams(vmem_limit_bytes=vmem),
        name="segment_ends",
    )(delta, w, ds, coef, rate, fan)

def forward_kernel(cd, tc, delta_ref, w_ref, ds_ref, coef_ref, rate_ref, fan_ref, fold_ref, sin_ref,
                   y_ref, hist_ref, dc_ref, h_scr, splat, acc_out):
    ch = pl.program_id(1)
    tiles = cd // 128

    @pl.when(ch == 0)
    def _():
        h_scr[...] = sin_ref[0]

    spread(coef_ref, fan_ref, splat, tc)
    at = [pl.ds(tile * 128, 128) for tile in range(tiles)]
    group = 4
    for n0 in range(0, STATE, group):
        pairs = [(n, i) for n in range(n0, n0 + group) for i in range(tiles)]
        init = tuple(h_scr[pl.ds(n * 8, 8), at[i]] for n, i in pairs)

        def forward(t, hs, n0=n0):
            d = [delta_ref[t, :, l] for l in at]
            w = [w_ref[t, :, l] for l in at]
            s = [ds_ref[t, :, l] for l in at]
            y = [None] * tiles if n0 == 0 else [y_ref[t, :, l] for l in at]
            out = []
            for n in range(n0, n0 + group):
                r = pl.ds(n * 8, 8)
                cin = splat[rows8(t), pl.ds(n * 128, 128)]
                cout = splat[rows8(t), pl.ds((STATE + n) * 128, 128)]
                acc = None
                for i in range(tiles):
                    old = hs[len(out)]
                    hist_ref[0, t, r, at[i]] = old
                    h = jnp.exp2(d[i] * rate_ref[r, at[i]]) * old + cin * w[i]
                    out.append(h)
                    y[i] = cout * h if n == 0 else y[i] + cout * h
                    acc = s[i] * h if i == 0 else acc + s[i] * h
                acc_out[rows8(t), pl.ds(n * 128, 128)] = acc
            for i in range(tiles):
                y_ref[t, :, at[i]] = y[i]
            return tuple(out)

        hs = lax.fori_loop(0, tc, forward, init, unroll=tc)
        for j, (n, i) in enumerate(pairs):
            h_scr[pl.ds(n * 8, 8), at[i]] = hs[j]
    sums = jnp.dot(acc_out[...].astype(BF16), fold_ref[1], preferred_element_type=F32)
    dc_ref[...] = sums.reshape(tc, 8, 128)


def scan_forward(delta, w, ds, coef, rate, fan, fold, s_in, tc=STEPS, vmem=56 * 2**20):
    tokens, members, cd = delta.shape
    sg, nch = members // 8, tokens // tc
    rows = STATE * 8
    tok = lambda width: pl.BlockSpec((tc, 8, width), lambda s, c: (c, s, 0))
    keep = lambda r: pl.BlockSpec((1, r, cd), lambda s, c: (s, 0, 0))
    whole = lambda a: pl.BlockSpec(a.shape, lambda s, c: (0,) * a.ndim)
    return pl.pallas_call(
        functools.partial(forward_kernel, cd, tc),
        grid=(sg, nch),
        in_specs=[tok(cd), tok(cd), tok(cd), tok(128), whole(rate), whole(fan), whole(fold), keep(rows)],
        out_specs=[tok(cd), pl.BlockSpec((1, tc, rows, cd), lambda s, c: (s, c, 0, 0)), tok(128)],
        out_shape=[jax.ShapeDtypeStruct(delta.shape, F32), jax.ShapeDtypeStruct((sg, tokens, rows, cd), F32), jax.ShapeDtypeStruct((tokens, members, 128), F32)],
        scratch_shapes=[pltpu.VMEM((rows, cd), F32), pltpu.VMEM((tc * 8, 2 * STATE * 128), F32), pltpu.VMEM((tc * 8, STATE * 128), F32)],
        compiler_params=pltpu.CompilerParams(vmem_limit_bytes=vmem),
        cost_estimate=pl.CostEstimate(flops=30 * 10**9, bytes_accessed=90 * 10**6, transcendentals=0),
        name="scan_forward",
    )(delta, w, ds, coef, rate, fan, fold, s_in)


def backward_kernel(cd, tc, delta_ref, w_ref, ds_ref, coef_ref, rate_ref, fan_ref, fold_ref, hist_ref, dout_ref, gin_ref,
                    a_ref, s_ref, dc_ref, rs_ref, g_scr, splat, acc_in):
    ch = pl.program_id(1)
    tiles = cd // 128

    @pl.when(ch == 0)
    def _():
        rs_ref[...] = jnp.zeros_like(rs_ref)
        g_scr[...] = gin_ref[0]

    spread(coef_ref, fan_ref, splat, tc)
    at = [pl.ds(tile * 128, 128) for tile in range(tiles)]
    group = 2
    for n0 in range(0, STATE, group):
        pairs = [(n, i) for n in range(n0, n0 + group) for i in range(tiles)]
        init = (tuple(g_scr[pl.ds(n * 8, 8), at[i]] for n, i in pairs), tuple(rs_ref[0, pl.ds(n * 8, 8), at[i]] for n, i in pairs))

        def backward(k, carry, n0=n0):
            gs, rs = carry
            t = tc - 1 - k
            d = [delta_ref[t, :, l] for l in at]
            w = [w_ref[t, :, l] for l in at]
            s = [ds_ref[t, :, l] for l in at]
            da = [None] * tiles if n0 == 0 else [a_ref[t, :, l] for l in at]
            cs = [None] * tiles if n0 == 0 else [s_ref[t, :, l] for l in at]
            ng, nr = [], []
            for n in range(n0, n0 + group):
                r = pl.ds(n * 8, 8)
                cin = splat[rows8(t), pl.ds(n * 128, 128)]
                cout = splat[rows8(t), pl.ds((STATE + n) * 128, 128)]
                acc = None
                for i in range(tiles):
                    rate = rate_ref[r, at[i]]
                    j = len(ng)
                    a = jnp.exp2(d[i] * rate)
                    g = gs[j] + cout * s[i]
                    ga = g * a
                    ng.append(ga)
                    th = ga * hist_ref[0, t, r, at[i]]
                    da[i] = th * rate if n == 0 else da[i] + th * rate
                    cs[i] = cin * g if n == 0 else cs[i] + cin * g
                    acc = g * w[i] if i == 0 else acc + g * w[i]
                    nr.append(rs[j] + th * d[i])
                acc_in[rows8(t), pl.ds(n * 128, 128)] = acc
            for i in range(tiles):
                a_ref[t, :, at[i]] = da[i]
                s_ref[t, :, at[i]] = cs[i]
            return tuple(ng), tuple(nr)

        gs, rs = lax.fori_loop(0, tc, backward, init, unroll=tc)
        for j, (n, i) in enumerate(pairs):
            g_scr[pl.ds(n * 8, 8), at[i]] = gs[j]
            rs_ref[0, pl.ds(n * 8, 8), at[i]] = rs[j]
    sums = jnp.dot(acc_in[...].astype(BF16), fold_ref[0], preferred_element_type=F32)
    dc_ref[...] = sums.reshape(tc, 8, 128) + dout_ref[...]


def scan_backward(delta, w, ds, coef, rate, fan, fold, hist, dout, g_in, tc=STEPS, vmem=56 * 2**20):
    tokens, members, cd = delta.shape
    sg, nch = members // 8, tokens // tc
    rows = STATE * 8
    tok = lambda width: pl.BlockSpec((tc, 8, width), lambda s, c: (nch - 1 - c, s, 0))
    keep = lambda r: pl.BlockSpec((1, r, cd), lambda s, c: (s, 0, 0))
    whole = lambda a: pl.BlockSpec(a.shape, lambda s, c: (0,) * a.ndim)
    return pl.pallas_call(
        functools.partial(backward_kernel, cd, tc),
        grid=(sg, nch),
        in_specs=[tok(cd), tok(cd), tok(cd), tok(128), whole(rate), whole(fan), whole(fold),
                  pl.BlockSpec((1, tc, rows, cd), lambda s, c: (s, nch - 1 - c, 0, 0)), tok(128), keep(rows)],
        out_specs=[tok(cd), tok(cd), tok(128), keep(rows)],
        out_shape=[jax.ShapeDtypeStruct(delta.shape, F32)] * 2 + [jax.ShapeDtypeStruct((tokens, members, 128), F32), jax.ShapeDtypeStruct((sg, rows, cd), F32)],
        scratch_shapes=[pltpu.VMEM((rows, cd), F32), pltpu.VMEM((tc * 8, 2 * STATE * 128), F32), pltpu.VMEM((tc * 8, STATE * 128), F32)],
        compiler_params=pltpu.CompilerParams(vmem_limit_bytes=vmem),
        cost_estimate=pl.CostEstimate(flops=45 * 10**9, bytes_accessed=90 * 10**6, transcendentals=0),
        name="scan_backward",
    )(delta, w, ds, coef, rate, fan, fold, hist, dout, g_in)


def rounded(value):
    return lax.reduce_precision(value, 8, 7)


def silu_slope(value):
    sigma = jax.nn.sigmoid(value)
    return sigma * (1.0 + value * (1.0 - sigma))


def contract_rows(left, right):
    return lax.dot_general(left, right, (((0,), (0,)), ((), ())), preferred_element_type=F32)


def contract_cols(left, right):
    return lax.dot_general(left, right, (((1,), (1,)), ((), ())), preferred_element_type=F32)


def dot(left, right):
    return jnp.dot(left, right, preferred_element_type=F32)


def along_z(grid, value, d):
    ctx = grid.ctx
    return lax.ppermute(value, "ctx", [(c, (c + 4 * d) % ctx) for c in range(ctx)])


def swap(grid, value, bit):
    return lax.ppermute(value, "ctx", [(c, c ^ bit) for c in range(grid.ctx)])


def spread_tables():
    fan = np.zeros((128, 2 * STATE * 128), np.float32)
    for k in range(2 * STATE):
        fan[k, k * 128:(k + 1) * 128] = 1
        fan[2 * STATE + k, k * 128:(k + 1) * 128] = 1
    fold = np.zeros((2, STATE * 128, 128), np.float32)
    for n in range(STATE):
        fold[0, n * 128:(n + 1) * 128, n] = 1
        fold[1, n * 128:(n + 1) * 128, STATE + n] = 1
    return jnp.asarray(fan, BF16), jnp.asarray(fold, BF16)


def shards(grid, hidden_in, norm_gain, in_proj, conv_weight, conv_bias, state_proj, delta_proj, delta_bias,
           decay_log, skip_gain, out_proj, cotangent):
    F, C, Z = grid.fsdp, grid.members, grid.planes
    tokens = hidden_in.shape[1]
    rows = in_proj.shape[0]
    block = out_proj.shape[0]
    chans = Z * block
    z, q, f = grid.here()

    hidden_low = hidden_in.reshape(tokens, D)
    cot_rows = cotangent.reshape(tokens, D)
    gain_rows = rounded(norm_gain)
    lin = z * C + q * F + f
    slots = 128 // rows
    gain_tile = jnp.where(lax.broadcasted_iota(jnp.int32, (slots, 1), 0) == lin % slots, gain_rows[None, :], 0.0).reshape(1, 128)
    gain_tile = jnp.broadcast_to(gain_tile, (8, 128))
    out_low = out_proj.astype(BF16)
    in_low = rounded(in_proj).astype(BF16)
    wi = in_low.reshape(rows, 2, Z, C, block).transpose(3, 0, 1, 2, 4).reshape(C, rows, 2 * chans)
    small = jnp.concatenate(
        [conv_weight, conv_bias[None], delta_bias[None], skip_gain[None], decay_log, jnp.zeros((9, block), F32), delta_proj, state_proj.T], axis=0
    ).astype(BF16)
    normed_all, cot_all, wi_all, small_all, gains = gather_all(grid, hidden_low, gain_tile, cot_rows, wi, small)
    gains = gains[0]
    count = C * tokens
    normed_all = normed_all.reshape(count, D)
    cot_all = cot_all.reshape(count, D)
    w_in = wi_all.reshape(D, 2 * chans)
    small_all = small_all.transpose(1, 0, 2).reshape(small.shape[0], chans)
    taps = small_all[:KW].astype(F32)
    conv_shift = small_all[KW].astype(F32)
    delta_shift = small_all[KW + 1].astype(F32)
    skip = small_all[KW + 2].astype(F32)
    decay_rate = -jnp.exp(small_all[KW + 3:KW + 3 + STATE].astype(F32))
    w_delta = small_all[32:32 + DT_RANK]
    w_state = small_all[32 + DT_RANK:]
    rate8 = jnp.repeat(decay_rate * LOG2E, 8, axis=0)

    def by_step(value):
        return value.reshape(C, tokens, -1).transpose(1, 0, 2)

    def by_member(value):
        return value.transpose(1, 0, 2).reshape(count, -1)

    mixed = by_step(dot(normed_all, w_in).astype(BF16))
    conv_in = mixed[:, :, :chans]
    gate = mixed[:, :, chans:].astype(F32)
    edge_rows = -(-(KW - 1) * F // 16) * 16
    tail = conv_in[tokens - (KW - 1):, C - F:].reshape((KW - 1) * F, chans)
    tails = line_gather(grid, [jnp.pad(tail, ((0, edge_rows - (KW - 1) * F), (0, 0)))], 3, "conv_edges")[0]
    out_low, tails = lax.optimization_barrier((out_low, tails))
    w_out = [out_low] + [along_z(grid, out_low, d) for d in range(1, Z)]
    before = lax.dynamic_index_in_dim(tails, jnp.maximum(z - 1, 0), 0, False)[: (KW - 1) * F]
    before = jnp.where(z > 0, before, jnp.zeros_like(before)).reshape(KW - 1, F, chans)
    edge = jnp.concatenate([before, conv_in[tokens - (KW - 1):, : C - F]], axis=1)
    padded = jnp.concatenate([edge, conv_in], axis=0).astype(F32)
    conv_out = jnp.broadcast_to(conv_shift, (tokens, C, chans))
    for k in range(KW):
        conv_out = conv_out + taps[k] * padded[k:k + tokens]
    act = rounded(jax.nn.silu(conv_out))
    act_rows = lax.optimization_barrier(act.astype(BF16).reshape(count, chans))
    pad_lanes = 256 - DT_RANK - 2 * STATE
    selected = contract_cols(act_rows, jnp.pad(w_state, ((0, pad_lanes), (0, 0))))
    selected, *w_out = lax.optimization_barrier((plane_sum(grid, selected, 4), *w_out))
    delta_in = selected[:, :DT_RANK]
    coef = selected[:, DT_RANK:].reshape(tokens, C, 128)
    delta_pre = (dot(delta_in, w_delta) + delta_shift).reshape(tokens, C, chans)
    delta = jax.nn.softplus(delta_pre)
    drive = delta * act
    gate_act = jax.nn.silu(gate)
    w_out = in_place_order(grid, w_out).reshape(chans, D)
    d_gated = lax.optimization_barrier(by_step(contract_cols(cot_all, w_out)))
    d_scanned = d_gated * gate_act

    fan, fold = spread_tables()
    ends, adjoints, totals = scan_ends(delta, drive, d_scanned, coef, rate8, fan)
    def by_segment(value):
        groups = C // 8
        value = value.reshape(groups, -1, 8, chans).transpose(0, 2, 1, 3)
        return value.reshape(4, F, -1, chans)

    def by_sublane(value):
        return value.reshape(C // 8, 8, STATE, chans).transpose(0, 2, 1, 3).reshape(C // 8, STATE * 8, chans)

    totals = by_segment(totals)
    kept, ends, adjoints = jnp.exp(decay_rate * totals), by_segment(ends), by_segment(adjoints)
    end = ends[0]
    for c in range(1, 4):
        end = kept[c] * end + ends[c]
    adj = adjoints[3]
    for c in reversed(range(3)):
        adj = kept[c] * adj + adjoints[c]
    flat = [end.reshape(F * STATE, chans), adj.reshape(F * STATE, chans), jnp.broadcast_to(jnp.sum(totals, axis=0), (F, 8, chans)).reshape(F * 8, chans)]
    all_end, all_adj, all_tot = line_gather(grid, flat, 5, "segment_states")
    plane_kept = jnp.exp(decay_rate * all_tot.reshape(Z, F, 8, chans)[:, :, :1])
    all_end, all_adj = all_end.reshape(Z, F, STATE, chans), all_adj.reshape(Z, F, STATE, chans)
    state = jnp.zeros((F, STATE, chans), F32)
    adj = state
    for p in range(Z - 1):
        state = jnp.where(p < z, plane_kept[p] * state + all_end[p], state)
    for p in reversed(range(1, Z)):
        adj = jnp.where(p > z, plane_kept[p] * adj + all_adj[p], adj)
    before_state, after_adj = [], []
    for c in range(4):
        before_state.append(state)
        state = kept[c] * state + ends[c]
    for c in reversed(range(4)):
        after_adj.append(adj)
        adj = kept[c] * adj + adjoints[c]
    after_adj.reverse()

    y, history, d_out_coef = scan_forward(delta, drive, d_scanned, coef, rate8, fan, fold, by_sublane(jnp.stack(before_state)))
    scanned = y + skip * act
    gated = (scanned * gate_act).astype(BF16)
    d_gate = d_gated * scanned * silu_slope(gate)
    gated, d_gate = lax.optimization_barrier((gated, d_gate.astype(BF16)))
    gated, d_gate = by_member(gated), by_member(d_gate)
    half = D // 2
    core = q % 2
    w_out_mine = lax.dynamic_slice_in_dim(w_out, core * half, half, 1)
    w_out_twin = lax.dynamic_slice_in_dim(w_out, (1 - core) * half, half, 1)

    def sent_along_z(part):
        pick = lambda d: lax.dynamic_index_in_dim(part, (z + d) % Z, 0, False)
        return [pick(0)] + [along_z(grid, pick(d), d) for d in range(1, Z)]

    def total(parts):
        return functools.reduce(lambda t, v: t + v.astype(F32), parts[1:], parts[0].astype(F32))

    def twin_summed(mine, twin_part):
        return (mine + swap(grid, twin_part, 1).astype(F32)).astype(BF16).reshape(4, F, tokens, half)

    def other_sequences(total):
        pieces = [lax.dynamic_index_in_dim(total, (f + d) % F, 1, False) for d in range(F)]
        return pieces[:1] + [lax.ppermute(pieces[d], "fsdp", [(g, (g + d) % F) for g in range(F)]) for d in range(1, F)]

    def own_tokens(own):
        own = own.reshape(2, 2, tokens, half)
        keep = lax.dynamic_index_in_dim(own, q // 2, 0, False)
        give = lax.dynamic_index_in_dim(own, 1 - q // 2, 0, False).astype(BF16)
        keep = keep + swap(grid, give, 2).astype(F32)
        final = lax.dynamic_index_in_dim(keep, core, 0, False)
        give = lax.dynamic_index_in_dim(keep, 1 - core, 0, False).astype(BF16)
        return final, swap(grid, give, 1)

    twin_part = dot(gated, w_out_twin).astype(BF16)
    out_part = contract_rows(gated, cot_all).astype(BF16).reshape(Z, block, D)
    gate_part = contract_rows(normed_all, d_gate).astype(BF16).reshape(Z, C * rows, chans)
    out_part, gate_part, chip_out = lax.optimization_barrier((out_part, gate_part, twin_summed(dot(gated, w_out_mine), twin_part)))
    sent_out, sent_gate, sent_tokens = sent_along_z(out_part), sent_along_z(gate_part), other_sequences(chip_out)
    history, _ = lax.optimization_barrier((history, (out_part, gate_part, chip_out)))
    swept = scan_backward(delta, drive, d_scanned, coef, rate8, fan, fold, history, d_out_coef, by_sublane(jnp.stack(after_adj)))
    near = [d for d in range(1, Z) if d != 2]
    (d_delta_a, coef_sum, d_coef, rate_sum), arrived_out, arrived_gate, sent_tokens = lax.optimization_barrier(
        (swept, [sent_out[d] for d in near], [sent_gate[d] for d in near], sent_tokens)
    )
    mixer_own, mixer_twin = own_tokens(total(sent_tokens))
    decay_grad = rate_sum.reshape(C // 8, STATE, 8, chans).sum(axis=(0, 2)) * decay_rate
    skip_grad = jnp.sum(d_scanned * act, axis=(0, 1))
    d_delta_pre = (d_delta_a * (1.0 / LOG2E) + act * coef_sum) * jax.nn.sigmoid(delta_pre)
    shift_grad = jnp.sum(d_delta_pre, axis=(0, 1))
    d_delta_low = d_delta_pre.astype(BF16).reshape(count, chans)
    dproj_grad = contract_rows(delta_in, d_delta_low)
    d_delta_in = contract_cols(d_delta_low, w_delta)
    partial = jnp.concatenate([d_delta_in, d_coef.reshape(count, 128)], axis=1)
    d_selected, far_out = lax.optimization_barrier((plane_sum(grid, partial, 6), sent_out[2]))
    d_selected = d_selected[:, :DT_RANK + 2 * STATE]
    sproj_grad = contract_rows(d_selected, act_rows)
    d_activated = delta * coef_sum + skip * d_scanned + dot(d_selected, w_state).reshape(tokens, C, chans)
    d_conv = d_activated * silu_slope(conv_out)
    cbias_grad = jnp.sum(d_conv, axis=(0, 1))
    kernel_grad = jnp.stack([jnp.sum(d_conv * padded[k:k + tokens], axis=(0, 1)) for k in range(KW)])
    head = d_conv[:KW - 1, :F].reshape((KW - 1) * F, chans)
    head_rows = -(-(KW - 1) * F // 8) * 8
    heads = line_gather(grid, [jnp.pad(head, ((0, head_rows - (KW - 1) * F), (0, 0)))], 7, "conv_grad_edges")[0]
    after = lax.dynamic_index_in_dim(heads, jnp.minimum(z + 1, Z - 1), 0, False)[: (KW - 1) * F]
    after = jnp.where(z < Z - 1, after, jnp.zeros_like(after)).reshape(KW - 1, F, chans)
    edge_grad = jnp.concatenate([d_conv[:KW - 1, F:], after], axis=1)
    grad_padded = jnp.concatenate([d_conv, edge_grad], axis=0)
    d_conv_in = jnp.zeros((tokens, C, chans), F32)
    for k in range(KW):
        d_conv_in = d_conv_in + taps[k] * grad_padded[KW - 1 - k:KW - 1 - k + tokens]
    d_conv_in, far_gate, mixer_own, mixer_twin = lax.optimization_barrier((d_conv_in.astype(BF16), sent_gate[2], mixer_own, mixer_twin))
    d_conv_in = by_member(d_conv_in)
    out_grad = total([sent_out[0], far_out] + arrived_out)
    gate_sum = total([sent_gate[0], far_gate] + arrived_gate).astype(BF16).reshape(C, rows, chans)
    mixer_twin = mixer_twin.astype(F32)
    mixer_out = jnp.where(core == 0, jnp.concatenate([mixer_own, mixer_twin], 1), jnp.concatenate([mixer_twin, mixer_own], 1))
    d_mixed = jnp.concatenate([d_conv_in, d_gate], axis=1)
    w_in_mine = lax.dynamic_slice_in_dim(w_in, core * half, half, 0)
    w_in_twin = lax.dynamic_slice_in_dim(w_in, (1 - core) * half, half, 0)
    from_twin = swap(grid, contract_cols(d_mixed, w_in_twin).astype(BF16), 1)
    conv_part = contract_rows(normed_all, d_conv_in).astype(BF16).reshape(Z, C, rows, chans)
    part_in = (contract_cols(d_mixed, w_in_mine) + from_twin.astype(F32)).astype(BF16).reshape(C, tokens, half)

    fine = jnp.concatenate([kernel_grad, cbias_grad[None], shift_grad[None], skip_grad[None], decay_grad, jnp.zeros((9, chans), F32)], axis=0)
    fine = fine.reshape(32, Z, block).transpose(1, 0, 2)
    coarse = jnp.concatenate([dproj_grad, sproj_grad], axis=0).astype(BF16)
    coarse = coarse.reshape(-1, Z, block).transpose(1, 0, 2)
    got = to_owners(grid, conv_part, [gate_sum, part_in], [coarse, fine], 9)
    in_grad = jnp.stack([got[0], got[1]], axis=0).reshape(2, C, rows, Z, block).transpose(2, 0, 3, 1, 4)
    in_grad = in_grad.reshape(rows, 2 * DI).astype(F32)
    d_normed = got[2].astype(F32).reshape(2, 2, F, tokens, half).sum(axis=(0, 2))
    d_unit = jnp.concatenate([d_normed[0], d_normed[1]], axis=1) * gains[None, :]
    hidden = hidden_low.astype(F32)
    inv_rms = lax.rsqrt(jnp.mean(hidden * hidden, axis=1, keepdims=True) + EPS)
    unit = hidden * inv_rms
    block_out = (hidden + mixer_out).astype(BF16)
    coarse = got[3].astype(F32).sum(axis=0)
    fine = got[4].sum(axis=0)
    gain_grad = jnp.sum(rounded(in_proj) * in_grad, axis=1) / gain_rows
    mean_term = jnp.mean(d_unit * unit, axis=1, keepdims=True)
    input_grad = (cot_rows.astype(F32) + inv_rms * (d_unit - unit * mean_term)).astype(BF16)
    return (
        block_out.reshape(1, tokens, D),
        input_grad.reshape(1, tokens, D),
        gain_grad,
        in_grad,
        fine[:KW],
        fine[KW],
        coarse[DT_RANK:].T,
        coarse[:DT_RANK],
        fine[KW + 1],
        fine[KW + 3:KW + 3 + STATE],
        fine[KW + 2],
        out_grad,
    )


def solution(mesh):
    grid = Grid(mesh.shape["ctx"], mesh.shape["fsdp"])
    both = ("ctx", "fsdp")
    tokens, flat, by_row, by_col = P("fsdp", "ctx", None), P(both), P(both, None), P(None, both)
    in_specs = (tokens, flat, by_row, by_col, flat, by_row, by_col, flat, by_col, flat, by_row, tokens)
    out_specs = (tokens, tokens, flat, by_row, by_col, flat, by_row, by_col, flat, by_col, flat, by_row)
    return jax.shard_map(functools.partial(shards, grid), mesh=mesh, in_specs=in_specs, out_specs=out_specs, check_vma=False)
```

```python
import functools

import jax
import jax.numpy as jnp
import numpy as np
from jax import lax
from jax.experimental import pallas as pl
from jax.experimental.pallas import tpu as pltpu
from jax.sharding import PartitionSpec as P

D = 2048
DI = 4096
STATE = 16
DT_RANK = 128
KW = 4
EPS = 1e-05
LOG2E = 1.4426950408889634
STEPS = 16
MESH = pl.DeviceIdType.MESH
BF16 = jnp.bfloat16
F32 = jnp.float32


class Grid:
    def __init__(self, ctx, fsdp):
        self.ctx, self.fsdp = ctx, fsdp
        self.planes = ctx // 4
        self.members = 4 * fsdp
        self.devices = ctx * fsdp

    def here(self):
        c, f = lax.axis_index("ctx"), lax.axis_index("fsdp")
        return c // 4, c % 4, f

    def at(self, z, q, f):
        return {"ctx": z * 4 + q, "fsdp": f}

    def member(self, z, j):
        return self.at(z, j // self.fsdp, j % self.fsdp)


def remote(src, dst, send, recv, where):
    return pltpu.make_async_remote_copy(
        src_ref=src, dst_ref=dst, send_sem=send, recv_sem=recv, device_id=where, device_id_type=MESH
    )


def greet(places):
    barrier = pltpu.get_barrier_semaphore()
    for place in places:
        pl.semaphore_signal(barrier, inc=1, device_id=place, device_id_type=MESH)
    pl.semaphore_wait(barrier, len(places))


def comm_call(kernel, outs, scratch, ident, name, args, vmem=None, in_vmem=(), out_vmem=False):
    spaces = [pl.BlockSpec(memory_space=pltpu.VMEM if i in in_vmem else pl.ANY) for i in range(len(args))]
    return pl.pallas_call(
        kernel,
        in_specs=spaces,
        out_specs=[pl.BlockSpec(memory_space=pltpu.VMEM if out_vmem else pl.ANY)] * len(outs),
        out_shape=outs,
        scratch_shapes=scratch,
        compiler_params=pltpu.CompilerParams(
            collective_id=ident, has_side_effects=True, vmem_limit_bytes=vmem or 16 * 2**20
        ),
        name=name,
    )(*args)


def gather_kernel(grid, rows, h_ref, g_ref, c_ref, in_ref, sm_ref, n_all, c_all, wi_all, sm_all, gain_out,
                  gain_buf, gains, n_low, wi_cut, local, g_send, g_recv, n_send, n_recv, c_send, c_recv, a_send, a_recv,
                  z_send, z_recv, s_send, s_recv):
    z, q, f = grid.here()
    F, C, Z, N = grid.fsdp, grid.members, grid.planes, grid.devices
    me = q * F + f
    lin = z * C + me
    opposite, twin = q ^ 2, q ^ 1
    barrier = pltpu.get_barrier_semaphore()

    def other(d):
        to = lax.rem(lin + d, N)
        return grid.member(to // C, lax.rem(to, C))

    @pl.loop(1, N)
    def _(d):
        pl.semaphore_signal(barrier, inc=1, device_id=other(d), device_id_type=MESH)

    wi_ref = in_ref
    if in_ref.dtype == F32:
        wi_ref, lanes = wi_cut, wi_cut.shape[2] // (2 * Z)
        for j in range(C):
            for m in range(2 * Z):
                wi_cut[j, :, m * lanes:(m + 1) * lanes] = in_ref[:, (m * C + j) * lanes:(m * C + j + 1) * lanes].astype(BF16)
    pl.semaphore_wait(barrier, N - 1)

    def gain_copy(d):
        return remote(g_ref, gain_buf.at[lin], g_send.at[d], g_recv.at[d], other(d))

    @pl.loop(1, N)
    def _(d):
        gain_copy(d).start()

    sends = []

    def push(copy):
        copy.start()
        sends.append(copy)

    def block_of(i):
        return lax.rem(me + C - i, C)

    def line_pair(step, i):
        right, left = z - step, z + step
        if step == 0 and i == 0:
            src_right = src_left = wi_ref.at[me]
        else:
            src_right, src_left = wi_all.at[right * C + block_of(i)], wi_all.at[left * C + block_of(i)]
        return (
            (z < Z - 1) & (right >= 0),
            remote(src_right, wi_all.at[right * C + block_of(i)], z_send.at[0, step, i], z_recv.at[0, step, i], grid.at(z + 1, q, f)),
            (z > 0) & (left <= Z - 1),
            remote(src_left, wi_all.at[left * C + block_of(i)], z_send.at[1, step, i], z_recv.at[1, step, i], grid.at(z - 1, q, f)),
        )

    def line_start(step, i):
        to_right, right, to_left, left = line_pair(step, i)

        @pl.when(to_right)
        def _():
            right.start()

        @pl.when(to_left)
        def _():
            left.start()

    def line_done(step, i):
        to_right, right, to_left, left = line_pair(step, i)

        @pl.when(to_right)
        def _():
            right.wait_send()

        @pl.when(to_left)
        def _():
            left.wait_send()

    def line_arrived(step, i):
        from_left, from_right = z - 1 - step, z + 1 + step

        @pl.when(from_left >= 0)
        def _():
            ref = wi_all.at[from_left * C + block_of(i)]
            remote(ref, ref, z_send.at[0, step, i], z_recv.at[0, step, i], grid.at(z - 1, q, f)).wait_recv()

        @pl.when(from_right <= Z - 1)
        def _():
            ref = wi_all.at[from_right * C + block_of(i)]
            remote(ref, ref, z_send.at[1, step, i], z_recv.at[1, step, i], grid.at(z + 1, q, f)).wait_recv()

    line_start(0, 0)
    for d in range(1, C):
        j = lax.rem(me + d, C)
        push(remote(wi_ref.at[j], wi_all.at[lin], a_send.at[d], a_recv.at[d], grid.member(z, j)))
    for d in range(1, Z):
        push(remote(sm_ref, sm_all.at[z], s_send.at[d], s_recv.at[d], grid.at(lax.rem(z + d, Z), q, f)))

    n_sent, c_sent = [0], [0]

    def push_n(block, src, where):
        push(remote(src, n_all.at[block], n_send.at[n_sent[0]], n_recv.at[block], where))
        n_sent[0] += 1

    def push_c(block, src, where):
        push(remote(src, c_all.at[block], c_send.at[c_sent[0]], c_recv.at[block], where))
        c_sent[0] += 1

    def arrived(ref, sems, block):
        remote(ref.at[block], ref.at[block], n_send.at[0], sems.at[block], grid.at(z, twin, f)).wait_recv()

    others = [lax.rem(f + d, F) for d in range(1, F)]

    gain_buf[lin] = g_ref[...]

    @pl.loop(1, N)
    def _(d):
        back = lax.rem(lin + N - d, N)
        remote(g_ref, gain_buf.at[back], g_send.at[d], g_recv.at[d], grid.member(back // C, lax.rem(back, C))).wait_recv()

    per = max(1, 128 // rows)
    for chunk in range(D // 128):
        gain = gain_buf[chunk * per]
        for k in range(1, per):
            gain = gain + gain_buf[chunk * per + k]
        gains[:, chunk * 128:(chunk + 1) * 128] = gain

    @pl.loop(0, h_ref.shape[0] // 16)
    def _(r):
        at = pl.ds(pl.multiple_of(r * 16, 16), 16)
        hidden = h_ref[at, :].astype(F32)
        scale = lax.rsqrt(jnp.mean(hidden * hidden, axis=1, keepdims=True) + EPS)
        n_low[at, :] = (hidden * scale * gains[0:1, :]).astype(BF16)

    for g in others:
        push_n(me, n_low, grid.at(z, q, g))
    push_c(me, c_ref, grid.at(z, opposite, f))
    push_n(me, n_low, grid.at(z, opposite, f))
    for g in others:
        push_c(me, c_ref, grid.at(z, q, g))
    push_n(me, n_low, grid.at(z, twin, f))
    push_c(me, c_ref, grid.at(z, twin, f))
    mine = [
        pltpu.make_async_copy(n_low, n_all.at[me], local.at[0]),
        pltpu.make_async_copy(c_ref, c_all.at[me], local.at[1]),
        pltpu.make_async_copy(wi_ref.at[me], wi_all.at[lin], local.at[2]),
        pltpu.make_async_copy(sm_ref, sm_all.at[z], local.at[3]),
        pltpu.make_async_copy(gains, gain_out, local.at[4]),
    ]
    for copy in mine:
        copy.start()
    for d in range(1, C):
        back = block_of(d)
        remote(wi_ref.at[me], wi_all.at[z * C + back], a_send.at[d], a_recv.at[d], grid.member(z, back)).wait_recv()
        line_start(0, d)
    mine[2].wait()

    def pass_on(step, blocks):
        for i in blocks:
            line_arrived(step, i)
            if step < Z - 2:
                line_start(step + 1, i)

    pass_on(0, range(C // 2))
    for g in others:
        block = q * F + g
        arrived(n_all, n_recv, block)
        push_n(block, n_all.at[block], grid.at(z, opposite, f))
        push_n(block, n_all.at[block], grid.at(z, twin, f))
    arrived(c_all, c_recv, opposite * F + f)
    for g in others:
        push_c(opposite * F + f, c_all.at[opposite * F + f], grid.at(z, q, g))
    push_c(opposite * F + f, c_all.at[opposite * F + f], grid.at(z, twin, f))
    pass_on(0, range(C // 2, C))
    for step in range(1, Z - 2):
        pass_on(step, range(C))
    for g in others:
        arrived(c_all, c_recv, q * F + g)
        push_c(q * F + g, c_all.at[q * F + g], grid.at(z, twin, f))
    for g in [f] + others:
        block = opposite * F + g
        arrived(n_all, n_recv, block)
        push_n(block, n_all.at[block], grid.at(z, twin, f))
    for g in others:
        block = opposite * F + g
        arrived(c_all, c_recv, block)
        push_c(block, c_all.at[block], grid.at(z, twin, f))
    pass_on(Z - 2, range(C))
    for side in (twin, twin ^ 2):
        for g in [f] + others:
            arrived(n_all, n_recv, side * F + g)
            arrived(c_all, c_recv, side * F + g)
    for d in range(1, Z):
        back = lax.rem(z + Z - d, Z)
        remote(sm_ref, sm_all.at[back], s_send.at[d], s_recv.at[d], grid.at(back, q, f)).wait_recv()
    for i in (0, 1, 3, 4):
        mine[i].wait()
    for copy in sends:
        copy.wait_send()
    for step in range(Z - 1):
        for i in range(C):
            line_done(step, i)

    @pl.loop(1, N)
    def _(d):
        gain_copy(d).wait_send()


def gather_all(grid, hidden, gain_tile, cot, wi, small):
    F, C, Z, N = grid.fsdp, grid.members, grid.planes, grid.devices
    cut = wi.dtype == F32
    rows, width = wi.shape[0 if cut else 1], 2 * DI // C
    tokens = hidden.shape[0]
    dma = pltpu.SemaphoreType.DMA
    outs = [
        jax.ShapeDtypeStruct((C, tokens, D), BF16),
        jax.ShapeDtypeStruct((C, tokens, D), BF16),
        jax.ShapeDtypeStruct((Z * C, rows, width), BF16),
        jax.ShapeDtypeStruct((Z,) + small.shape, BF16),
        jax.ShapeDtypeStruct((8, D), F32),
    ]
    count = (F - 1) + F + 2 * F
    scratch = [pltpu.VMEM((N, 8, 128), F32), pltpu.VMEM((8, D), F32), pltpu.VMEM((tokens, D), BF16)]
    scratch += [pltpu.VMEM((C, rows, width) if cut else (1, 16, 128), BF16)]
    scratch += [dma((5,)), dma((N,)), dma((N,)), dma((count,)), dma((C,)), dma((count,)), dma((C,)), dma((C,)), dma((C,))]
    scratch += [dma((2, Z, C)), dma((2, Z, C)), dma((Z,)), dma((Z,))]
    return comm_call(
        functools.partial(gather_kernel, grid, rows), outs, scratch, 1, "gather_weights_and_tokens",
        (hidden, gain_tile, cot, wi, small), vmem=32 * 2**20, in_vmem=(0, 1, 3) if cut else (0, 1),
    )


def plane_sum_kernel(grid, split, part_ref, *refs):
    outs, (send_buf, recv_buf, result, landed, send, recv, out_send, out_recv) = refs[:1 + split], refs[1 + split:]
    out_low, out_coef = outs if split else (outs[0].at[:, pl.ds(0, 128)], outs[0].at[:, pl.ds(128, 128)])
    z, q, f = grid.here()
    C = grid.members
    me = q * grid.fsdp + f
    rows = part_ref.shape[0] // C
    quarter = rows // 4
    greet([grid.member(z, lax.rem(me + d, C)) for d in range(1, C)])
    lane = lax.broadcasted_iota(jnp.int32, (quarter, 128), 1)

    def span(k, m, size):
        return pl.ds(pl.multiple_of(k * rows + m * size, 16), size)

    def pack(k):
        send_buf[k, 0:rows, :] = part_ref[span(k, 0, rows), 0:128].astype(BF16)
        mixed = part_ref[span(k, 0, quarter), 128:256]
        for m in range(1, 4):
            mixed = mixed + pltpu.roll(part_ref[span(k, m, quarter), 128:256], 32 * m, 1)
        send_buf[k, rows:, :] = mixed.astype(BF16)

    copies = []
    for d in range(1, C):
        j = lax.rem(me + d, C)
        pack(j)
        copy = remote(send_buf.at[j], recv_buf.at[d], send.at[d], recv.at[d], grid.member(z, j))
        copy.start()
        copies.append(copy)
    pack(me)
    total = send_buf[me].astype(F32)
    for d in range(1, C):
        copies[d - 1].wait_recv()
        total = total + recv_buf[d].astype(F32)
    result[...] = total.astype(BF16)
    pushes = []
    for d in range(1, C):
        copy = remote(result, landed.at[me], out_send.at[d], out_recv.at[d], grid.member(z, lax.rem(me + d, C)))
        copy.start()
        pushes.append(copy)

    def unpack(k, block):
        out_low[span(k, 0, rows), :] = block[0:rows, :]
        mixed = block[rows:, :].astype(F32)
        for m in range(4):
            part = pltpu.roll(mixed, 128 - 32 * m, 1) if m else mixed
            out_coef[span(k, m, quarter), :] = jnp.where(lane < 32, part, 0.0).astype(BF16)

    unpack(me, result)
    for d in range(1, C):
        back = lax.rem(me + C - d, C)
        remote(result, landed.at[back], out_send.at[d], out_recv.at[d], grid.member(z, back)).wait_recv()
        unpack(back, landed.at[back])
    for copy in copies + pushes:
        copy.wait_send()


def plane_sum(grid, part, split, ident):
    C = grid.members
    count = part.shape[0]
    rows = count // C
    packed = rows + rows // 4
    dma = pltpu.SemaphoreType.DMA
    return comm_call(
        functools.partial(plane_sum_kernel, grid, split),
        [jax.ShapeDtypeStruct((count, 128), BF16)] * 2 if split else [jax.ShapeDtypeStruct((count, 256), BF16)],
        [pltpu.VMEM((C, packed, 128), BF16), pltpu.VMEM((C, packed, 128), BF16), pltpu.VMEM((packed, 128), BF16), pltpu.VMEM((C, packed, 128), BF16)]
        + [dma((C,))] * 4,
        ident, "plane_sum", (part,), vmem=40 * 2**20, in_vmem=(0,), out_vmem=True,
    )


def edges_kernel(grid, step, count, edge_ref, *refs):
    z, q, f = grid.here()
    C, Z = grid.members, grid.planes
    me = q * grid.fsdp + f
    ins, edge_out, outs = refs[:count], refs[count], refs[count + 1:2 * count + 1]
    e_send, e_recv, local, send, recv = refs[2 * count + 1:]
    above, below = z < Z - 1, z > 0
    to, source = (above, below) if step > 0 else (below, above)
    barrier = pltpu.get_barrier_semaphore()

    @pl.when(above)
    def _():
        pl.semaphore_signal(barrier, inc=1, device_id=grid.at(z + 1, q, f), device_id_type=MESH)

    @pl.when(below)
    def _():
        pl.semaphore_signal(barrier, inc=1, device_id=grid.at(z - 1, q, f), device_id_type=MESH)

    members = [lax.rem(me + d, C) for d in range(1, C)] if count else []
    for j in members:
        pl.semaphore_signal(barrier, inc=1, device_id=grid.member(z, j), device_id_type=MESH)
    pl.semaphore_wait(barrier, len(members) + jnp.where(above & below, 2, 1))
    edge = remote(edge_ref, edge_out, e_send, e_recv, grid.at(z + step, q, f))

    @pl.when(to)
    def _():
        edge.start()

    pushes, waits = [], []
    for i in range(count):
        for d, j in enumerate(members, 1):
            back = lax.rem(me + C - d, C)
            pushes.append(remote(ins[i].at[j], outs[i].at[me], send.at[i, d], recv.at[i, d], grid.member(z, j)))
            waits.append(remote(ins[i].at[me], outs[i].at[back], send.at[i, d], recv.at[i, d], grid.member(z, back)))
    for copy in pushes:
        copy.start()
    for i in range(count):
        own = pltpu.make_async_copy(ins[i].at[me], outs[i].at[me], local.at[i])
        own.start()
        own.wait()
    for copy in waits:
        copy.wait_recv()

    @pl.when(source)
    def _():
        remote(edge_ref, edge_out, e_send, e_recv, grid.at(z - step, q, f)).wait_recv()

    for copy in pushes:
        copy.wait_send()

    @pl.when(to)
    def _():
        edge.wait_send()


def send_edges(grid, edge, step, arrays, ident, name):
    dma = pltpu.SemaphoreType.DMA
    n, C = len(arrays), grid.members
    m = max(n, 1)
    args = (edge,) + tuple(arrays)
    return comm_call(
        functools.partial(edges_kernel, grid, step, n), [jax.ShapeDtypeStruct(a.shape, a.dtype) for a in args],
        [dma, dma, dma((m,)), dma((m, C)), dma((m, C))], ident, name, args,
        in_vmem=tuple(range(n + 1)), out_vmem=True,
    )


def token_sums_kernel(grid, lines_in, part_ref, rows_ref, gate_ref, *refs):
    ins, outs = refs[:lines_in], refs[3 + lines_in:3 + 2 * lines_in]
    out_ref, row_out, gate_out = refs[lines_in:lines_in + 3]
    (x_in, y_in, x_sum, y_sum, x_last, y_last, final, landed, row_in, row_sum, local, x_send, x_recv, y_send, y_recv, b_send,
     b_recv, a_send, a_recv, t_send, t_recv, l_send, l_recv, f_send, f_recv, r_send, r_recv, g_send, g_recv) = refs[3 + 2 * lines_in:]
    z, q, f = grid.here()
    F, Z, C = grid.fsdp, grid.planes, grid.members
    me = q * F + f
    y, core = q // 2, lax.rem(q, 2)
    rows = part_ref.shape[2] // 2
    first, second = pl.ds(0, rows), pl.ds(rows, rows)
    across, twin = grid.at(z, q ^ 2, f), grid.at(z, q ^ 1, f)
    others = [lax.rem(f + d, F) for d in range(1, F)]
    greet([grid.member(z, lax.rem(me + d, C)) for d in range(1, C)] + [grid.at(lax.rem(z + d, Z), q, f) for d in range(1, Z)])
    far, near = pl.ds(2 * (1 - y), 2), pl.ds(2 * y, 2)

    def add(target, sources):
        @pl.loop(0, rows // 16)
        def _(r):
            at = pl.ds(pl.multiple_of(r * 16, 16), 16)
            value = sources[0][at, :].astype(F32)
            for source in sources[1:]:
                value = value + source[at, :].astype(F32)
            target[at, :] = value.astype(BF16)

    x_copies = [
        remote(part_ref.at[pl.ds(0, 4), g, first], x_in.at[d], x_send.at[d], x_recv.at[d], grid.at(z, q, g))
        for d, g in enumerate(others, 1)
    ]
    y_copy = remote(part_ref.at[far, :, second], y_in, y_send, y_recv, across)
    row_copies = []
    for d in range(1, Z):
        j = lax.rem(z + d, Z)
        row_copies.append(remote(rows_ref.at[j], row_in.at[d], f_send.at[d], f_recv.at[d], grid.at(j, q, f)))
    for copy in row_copies + x_copies + [y_copy]:
        copy.start()
    mine, pushes, waits = [], [], []
    for d in range(1, C):
        j, back = lax.rem(me + d, C), lax.rem(me + C - d, C)
        pushes.append(remote(gate_ref.at[j], gate_out.at[me], g_send.at[d], g_recv.at[d], grid.member(z, j)))
        waits.append(remote(gate_ref.at[me], gate_out.at[back], g_send.at[d], g_recv.at[d], grid.member(z, back)))
    gate_out[me] = gate_ref[me]
    for i in range(lines_in):
        mine.append(pltpu.make_async_copy(ins[i].at[z], outs[i].at[z], local.at[i]))
        for d in range(1, Z):
            j, back = lax.rem(z + d, Z), lax.rem(z + Z - d, Z)
            pushes.append(remote(ins[i].at[j], outs[i].at[z], l_send.at[i, d], l_recv.at[i, d], grid.at(j, q, f)))
            waits.append(remote(ins[i].at[z], outs[i].at[back], l_send.at[i, d], l_recv.at[i, d], grid.at(back, q, f)))
    for copy in pushes + mine:
        copy.start()
    for copy in x_copies:
        copy.wait_recv()

    def x_block(k):
        add(x_sum.at[k], [part_ref.at[k, f, first]] + [x_in.at[d, k] for d in range(1, F)])

    for c in range(2):
        x_block(2 * (1 - y) + c)
    a_copy = remote(x_sum.at[far], x_last, a_send, a_recv, across)
    a_copy.start()
    y_copy.wait_recv()
    b_copies = []
    for d, g in enumerate(others, 1):
        for c in range(2):
            add(y_sum.at[g, c], [part_ref.at[2 * y + c, g, second], y_in.at[c, g]])
        copy = remote(y_sum.at[g], y_last.at[d], b_send.at[d], b_recv.at[d], grid.at(z, q, g))
        copy.start()
        b_copies.append(copy)
    for c in range(2):
        x_block(2 * y + c)
        add(y_sum.at[f, c], [part_ref.at[2 * y + c, f, second], y_in.at[c, f]])
    a_copy.wait_recv()
    for c in range(2):
        add(final.at[c, first], [x_sum.at[2 * y + c], x_last.at[c]])
    for copy in b_copies:
        copy.wait_recv()
    for c in range(2):
        add(final.at[c, second], [y_sum.at[f, c]] + [y_last.at[d, c] for d in range(1, F)])
    t_copy = remote(final.at[1 - core], landed, t_send, t_recv, twin)
    t_copy.start()
    for copy in row_copies:
        copy.wait_recv()

    @pl.loop(0, C)
    def _(j):
        value = rows_ref[z, j].astype(F32)
        for d in range(1, Z):
            value = value + row_in[d, j].astype(F32)
        row_sum[j] = value.astype(BF16)

    for d in range(1, C):
        j, back = lax.rem(me + d, C), lax.rem(me + C - d, C)
        copy = remote(row_sum.at[j], row_out.at[me], r_send.at[d], r_recv.at[d], grid.member(z, j))
        copy.start()
        pushes.append(copy)
        waits.append(remote(row_sum.at[me], row_out.at[back], r_send.at[d], r_recv.at[d], grid.member(z, back)))
    row_out[me] = row_sum[me]
    out_ref[core] = final[core]
    t_copy.wait_recv()
    out_ref[1 - core] = landed[...]
    for copy in mine:
        copy.wait()
    for copy in waits:
        copy.wait_recv()
    for copy in x_copies + [y_copy, a_copy, t_copy] + b_copies + row_copies + pushes:
        copy.wait_send()


def token_sums(grid, part, weight_rows, gate_rows, line_arrays, ident):
    dma = pltpu.SemaphoreType.DMA
    F, Z, n = grid.fsdp, grid.planes, len(line_arrays)
    tokens, half = part.shape[2:]
    rows = tokens // 2
    buf = lambda *shape: pltpu.VMEM(shape + (rows, half), BF16)
    hbm, vmem = pl.BlockSpec(memory_space=pl.ANY), pl.BlockSpec(memory_space=pltpu.VMEM)
    return pl.pallas_call(
        functools.partial(token_sums_kernel, grid, n),
        in_specs=[vmem] * 3 + [hbm] * n,
        out_specs=[vmem] * 3 + [hbm] * n,
        out_shape=[jax.ShapeDtypeStruct((2, tokens, half), BF16), jax.ShapeDtypeStruct(gate_rows.shape, BF16), jax.ShapeDtypeStruct(gate_rows.shape, BF16)] + [jax.ShapeDtypeStruct(a.shape, a.dtype) for a in line_arrays],
        scratch_shapes=[buf(F, 4), buf(2, F), buf(4), buf(F, 2), buf(2), buf(F, 2), pltpu.VMEM((2, tokens, half), BF16), pltpu.VMEM((tokens, half), BF16), pltpu.VMEM(weight_rows.shape, BF16), pltpu.VMEM(weight_rows.shape[1:], BF16)]
        + [dma((n,)), dma((F,)), dma((F,)), dma, dma, dma((F,)), dma((F,)), dma, dma, dma, dma, dma((n, Z)), dma((n, Z)), dma((Z,)), dma((Z,))] + [dma((grid.members,))] * 4,
        compiler_params=pltpu.CompilerParams(collective_id=ident, has_side_effects=True, vmem_limit_bytes=56 * 2**20),
        cost_estimate=pl.CostEstimate(flops=45 * 10**9, bytes_accessed=10**8, transcendentals=0),
        name="token_sums",
    )(part, weight_rows, gate_rows, *line_arrays)


def pack_kernel(grid, out_ref, gate_ref, *outs):
    z, _, _ = grid.here()
    rows, chans = gate_ref.shape[1:]
    block, width = out_ref.shape[1:]
    for d in range(grid.planes):
        p = lax.rem(z + d, grid.planes)
        outs[d][0:rows, :] = gate_ref[p]
        for i in range(width // chans):
            outs[d][rows + i * block:rows + (i + 1) * block, :] = out_ref[p, :, i * chans:(i + 1) * chans]


def packed_for_planes(grid, out_part, gate_part):
    Z, rows, chans = gate_part.shape
    shape = (rows + out_part.shape[1] * out_part.shape[2] // chans, chans)
    vmem = pl.BlockSpec(memory_space=pltpu.VMEM)
    return pl.pallas_call(
        functools.partial(pack_kernel, grid),
        in_specs=[vmem] * 2,
        out_specs=[vmem] * Z,
        out_shape=[jax.ShapeDtypeStruct(shape, BF16)] * Z,
        compiler_params=pltpu.CompilerParams(vmem_limit_bytes=32 * 2**20),
        name="packed_for_planes",
    )(out_part, gate_part)


def states_kernel(grid, up_ref, down_ref, up_all, down_all, send, recv):
    z, q, f = grid.here()
    Z = grid.planes
    greet([grid.at(lax.rem(z + d, Z), q, f) for d in range(1, Z)])

    def each(act):
        for d in range(1, Z):
            above, below = z + d, z - d

            @pl.when(above <= Z - 1)
            def _():
                act(
                    remote(up_ref, up_all.at[z], send.at[0, d], recv.at[0, d], grid.at(above, q, f)),
                    remote(down_ref, down_all.at[above], send.at[1, d], recv.at[1, d], grid.at(above, q, f)),
                )

            @pl.when(below >= 0)
            def _():
                act(
                    remote(down_ref, down_all.at[z], send.at[1, d], recv.at[1, d], grid.at(below, q, f)),
                    remote(up_ref, up_all.at[below], send.at[0, d], recv.at[0, d], grid.at(below, q, f)),
                )

    each(lambda push, pull: push.start())
    each(lambda push, pull: pull.wait_recv())
    each(lambda push, pull: push.wait_send())


def exchange_states(grid, up, down, ident):
    dma = pltpu.SemaphoreType.DMA
    Z = grid.planes
    return comm_call(
        functools.partial(states_kernel, grid),
        [jax.ShapeDtypeStruct((Z,) + a.shape, a.dtype) for a in (up, down)],
        [dma((2, Z)), dma((2, Z))], ident, "segment_states", (up, down),
    )


def owners_kernel(grid, planes_in, lines_in, *refs):
    z, q, f = grid.here()
    C, Z = grid.members, grid.planes
    me = q * grid.fsdp + f
    total = 1 + planes_in + lines_in
    ins, outs = refs[:total], refs[total:2 * total]
    slots, own, result, local, w_send, w_recv, r_send, r_recv, p_send, p_recv, l_send, l_recv = refs[2 * total:]
    greet([grid.member(z, lax.rem(me + d, C)) for d in range(1, C)] + [grid.at(lax.rem(z + d, Z), q, f) for d in range(1, Z)])
    load = pltpu.make_async_copy(ins[0].at[z], own, local.at[0])
    load.start()
    weights, mine, pushes, waits = [], [], [], []
    for d in range(1, Z):
        j = lax.rem(z + d, Z)
        weights.append(remote(ins[0].at[j], slots.at[d], w_send.at[d], w_recv.at[d], grid.at(j, q, f)))
    for copy in weights:
        copy.start()
    for i in range(planes_in):
        mine.append(pltpu.make_async_copy(ins[1 + i].at[me], outs[1 + i].at[me], local.at[1 + i]))
        for d in range(1, C):
            j, back = lax.rem(me + d, C), lax.rem(me + C - d, C)
            pushes.append(remote(ins[1 + i].at[j], outs[1 + i].at[me], p_send.at[i, d], p_recv.at[i, d], grid.member(z, j)))
            waits.append(remote(ins[1 + i].at[me], outs[1 + i].at[back], p_send.at[i, d], p_recv.at[i, d], grid.member(z, back)))
    for i in range(lines_in):
        k = 1 + planes_in + i
        mine.append(pltpu.make_async_copy(ins[k].at[z], outs[k].at[z], local.at[k]))
        for d in range(1, Z):
            j, back = lax.rem(z + d, Z), lax.rem(z + Z - d, Z)
            pushes.append(remote(ins[k].at[j], outs[k].at[z], l_send.at[i, d], l_recv.at[i, d], grid.at(j, q, f)))
            waits.append(remote(ins[k].at[z], outs[k].at[back], l_send.at[i, d], l_recv.at[i, d], grid.at(back, q, f)))
    for copy in pushes + mine:
        copy.start()
    load.wait()
    for copy in weights:
        copy.wait_recv()

    @pl.loop(0, C)
    def _(j):
        value = own[j].astype(F32)
        for d in range(1, Z):
            value = value + slots[d, j].astype(F32)
        result[j] = value.astype(BF16)

    mine.append(pltpu.make_async_copy(result.at[me], outs[0].at[me], local.at[0]))
    mine[-1].start()
    for d in range(1, C):
        j, back = lax.rem(me + d, C), lax.rem(me + C - d, C)
        copy = remote(result.at[j], outs[0].at[me], r_send.at[d], r_recv.at[d], grid.member(z, j))
        copy.start()
        pushes.append(copy)
        waits.append(remote(result.at[me], outs[0].at[back], r_send.at[d], r_recv.at[d], grid.member(z, back)))
    for copy in mine:
        copy.wait()
    for copy in waits:
        copy.wait_recv()
    for copy in pushes + weights:
        copy.wait_send()


def to_owners(grid, weight, plane_arrays, line_arrays, ident):
    dma = pltpu.SemaphoreType.DMA
    C, Z = grid.members, grid.planes
    p, l = len(plane_arrays), len(line_arrays)
    args = (weight,) + tuple(plane_arrays) + tuple(line_arrays)
    part = weight.shape[1:]
    outs = [jax.ShapeDtypeStruct(part, BF16)] + [jax.ShapeDtypeStruct(a.shape, a.dtype) for a in args[1:]]
    return comm_call(
        functools.partial(owners_kernel, grid, p, l), outs,
        [pltpu.VMEM((Z,) + part, BF16), pltpu.VMEM(part, BF16), pltpu.VMEM(part, BF16)]
        + [dma((1 + p + l,)), dma((Z,)), dma((Z,)), dma((C,)), dma((C,)), dma((p, C)), dma((p, C)), dma((l, Z)), dma((l, Z))],
        ident, "to_owners", args,
    )


def place_kernel(grid, *refs):
    z, _, _ = grid.here()
    Z = grid.planes
    for d in range(Z):
        refs[Z][lax.rem(z + Z - d, Z)] = refs[d][...]


def in_place_order(grid, pieces):
    Z = grid.planes
    return pl.pallas_call(
        functools.partial(place_kernel, grid),
        in_specs=[pl.BlockSpec(memory_space=pltpu.VMEM)] * Z,
        out_specs=pl.BlockSpec(memory_space=pltpu.VMEM),
        out_shape=jax.ShapeDtypeStruct((Z,) + pieces[0].shape, pieces[0].dtype),
        compiler_params=pltpu.CompilerParams(vmem_limit_bytes=16 * 2**20),
        name="in_place_order",
    )(*pieces)

def spread(coef_ref, fan_ref, splat, tc):
    c = coef_ref[...].reshape(8 * tc, 128)
    for k in range(0, 2 * STATE, 4):
        l = pl.ds(k * 128, 512)
        splat[:, l] = jnp.dot(c, fan_ref[:, l], preferred_element_type=F32)

def rows8(t):
    return pl.ds(pl.multiple_of(t * 8, 8), 8)

def ends_kernel(cd, tc, delta_ref, w_ref, ds_ref, coef_ref, rate_ref, fan_ref, e_ref, g_ref, tot_ref, p_scr, splat):
    ch = pl.program_id(1)
    tiles = cd // 128
    @pl.when(ch == 0)
    def _():
        e_ref[...] = jnp.zeros_like(e_ref)
        g_ref[...] = jnp.zeros_like(g_ref)
        tot_ref[...] = jnp.zeros_like(tot_ref)
        p_scr[...] = jnp.ones_like(p_scr)
    spread(coef_ref, fan_ref, splat, tc)
    group = 4
    for tile in range(tiles):
        lanes = pl.ds(tile * 128, 128)
        for n0 in range(0, STATE, group):
            rates = [rate_ref[(n0 + i) * 8:(n0 + i + 1) * 8, lanes] for i in range(group)]
            def body(t, carry):
                hs, ps, gs = carry
                tok = pl.ds(pl.multiple_of(t * 8, 8), 8)
                d, w, s = delta_ref[t, :, lanes], w_ref[t, :, lanes], ds_ref[t, :, lanes]
                nh, np_, ng = [], [], []
                for i in range(group):
                    a = jnp.exp2(d * rates[i])
                    cin = splat[rows8(t), pl.ds((n0 + i) * 128, 128)]
                    cout = splat[rows8(t), pl.ds((STATE + n0 + i) * 128, 128)]
                    nh.append(a * hs[i] + cin * w)
                    p = ps[i] * a
                    np_.append(p)
                    ng.append(gs[i] + p * (cout * s))
                return tuple(nh), tuple(np_), tuple(ng)
            rows = [pl.ds((n0 + i) * 8, 8) for i in range(group)]
            init = (tuple(e_ref[0, r, lanes] for r in rows), tuple(p_scr[r, lanes] for r in rows), tuple(g_ref[0, r, lanes] for r in rows))
            hs, ps, gs = lax.fori_loop(0, tc, body, init, unroll=tc)
            for i, r in enumerate(rows):
                e_ref[0, r, lanes] = hs[i]
                p_scr[r, lanes] = ps[i]
                g_ref[0, r, lanes] = gs[i]
        def total(t, acc):
            return acc + delta_ref[t, :, lanes]
        tot_ref[0, :, lanes] = lax.fori_loop(0, tc, total, tot_ref[0, :, lanes], unroll=tc)

def scan_ends(delta, w, ds, coef, rate, fan, tc=2 * STEPS, vmem=48 * 2**20):
    tokens, members, cd = delta.shape
    sg, nch = members // 8, tokens // tc
    rows = STATE * 8
    tok = lambda width: pl.BlockSpec((tc, 8, width), lambda s, c: (c, s, 0))
    keep = lambda r: pl.BlockSpec((1, r, cd), lambda s, c: (s, 0, 0))
    return pl.pallas_call(
        functools.partial(ends_kernel, cd, tc),
        grid=(sg, nch),
        in_specs=[tok(cd), tok(cd), tok(cd), pl.BlockSpec((tc, 8, 128), lambda s, c: (c, s, 0)), pl.BlockSpec((rows, cd), lambda s, c: (0, 0)), pl.BlockSpec(fan.shape, lambda s, c: (0, 0))],
        out_specs=[keep(rows), keep(rows), keep(8)],
        out_shape=[jax.ShapeDtypeStruct((sg, rows, cd), F32), jax.ShapeDtypeStruct((sg, rows, cd), F32), jax.ShapeDtypeStruct((sg, 8, cd), F32)],
        scratch_shapes=[pltpu.VMEM((rows, cd), F32), pltpu.VMEM((tc * 8, 2 * STATE * 128), F32)],
        compiler_params=pltpu.CompilerParams(vmem_limit_bytes=vmem),
        name="segment_ends",
    )(delta, w, ds, coef, rate, fan)

def forward_kernel(cd, tc, delta_ref, w_ref, ds_ref, coef_ref, rate_ref, fan_ref, fold_ref, sin_ref,
                   y_ref, hist_ref, dc_ref, h_scr, splat, acc_out):
    ch = pl.program_id(1)
    tiles = cd // 128

    @pl.when(ch == 0)
    def _():
        h_scr[...] = sin_ref[0]

    spread(coef_ref, fan_ref, splat, tc)
    at = [pl.ds(tile * 128, 128) for tile in range(tiles)]
    group = 4
    for n0 in range(0, STATE, group):
        pairs = [(n, i) for n in range(n0, n0 + group) for i in range(tiles)]
        init = tuple(h_scr[pl.ds(n * 8, 8), at[i]] for n, i in pairs)

        def forward(t, hs, n0=n0):
            d = [delta_ref[t, :, l] for l in at]
            w = [w_ref[t, :, l] for l in at]
            s = [ds_ref[t, :, l] for l in at]
            y = [None] * tiles if n0 == 0 else [y_ref[t, :, l] for l in at]
            out = []
            for n in range(n0, n0 + group):
                r = pl.ds(n * 8, 8)
                cin = splat[rows8(t), pl.ds(n * 128, 128)]
                cout = splat[rows8(t), pl.ds((STATE + n) * 128, 128)]
                acc = None
                for i in range(tiles):
                    old = hs[len(out)]
                    hist_ref[0, t, r, at[i]] = old
                    h = jnp.exp2(d[i] * rate_ref[r, at[i]]) * old + cin * w[i]
                    out.append(h)
                    y[i] = cout * h if n == 0 else y[i] + cout * h
                    acc = s[i] * h if i == 0 else acc + s[i] * h
                acc_out[rows8(t), pl.ds(n * 128, 128)] = acc
            for i in range(tiles):
                y_ref[t, :, at[i]] = y[i]
            return tuple(out)

        hs = lax.fori_loop(0, tc, forward, init, unroll=tc)
        for j, (n, i) in enumerate(pairs):
            h_scr[pl.ds(n * 8, 8), at[i]] = hs[j]
    sums = jnp.dot(acc_out[...].astype(BF16), fold_ref[1], preferred_element_type=F32)
    dc_ref[...] = sums.reshape(tc, 8, 128)


def scan_forward(delta, w, ds, coef, rate, fan, fold, s_in, tc=2 * STEPS, vmem=56 * 2**20):
    tokens, members, cd = delta.shape
    sg, nch = members // 8, tokens // tc
    rows = STATE * 8
    tok = lambda width: pl.BlockSpec((tc, 8, width), lambda s, c: (c, s, 0))
    keep = lambda r: pl.BlockSpec((1, r, cd), lambda s, c: (s, 0, 0))
    whole = lambda a: pl.BlockSpec(a.shape, lambda s, c: (0,) * a.ndim)
    return pl.pallas_call(
        functools.partial(forward_kernel, cd, tc),
        grid=(sg, nch),
        in_specs=[tok(cd), tok(cd), tok(cd), tok(128), whole(rate), whole(fan), whole(fold), keep(rows)],
        out_specs=[tok(cd), pl.BlockSpec((1, tc, rows, cd), lambda s, c: (s, c, 0, 0)), tok(128)],
        out_shape=[jax.ShapeDtypeStruct(delta.shape, F32), jax.ShapeDtypeStruct((sg, tokens, rows, cd), F32), jax.ShapeDtypeStruct((tokens, members, 128), F32)],
        scratch_shapes=[pltpu.VMEM((rows, cd), F32), pltpu.VMEM((tc * 8, 2 * STATE * 128), F32), pltpu.VMEM((tc * 8, STATE * 128), F32)],
        compiler_params=pltpu.CompilerParams(vmem_limit_bytes=vmem),
        cost_estimate=pl.CostEstimate(flops=30 * 10**9, bytes_accessed=90 * 10**6, transcendentals=0),
        name="scan_forward",
    )(delta, w, ds, coef, rate, fan, fold, s_in)


def backward_kernel(cd, tc, delta_ref, w_ref, ds_ref, coef_ref, rate_ref, fan_ref, fold_ref, hist_ref, dout_ref, gin_ref,
                    a_ref, s_ref, dc_ref, rs_ref, g_scr, splat, acc_in):
    ch = pl.program_id(1)
    tiles = cd // 128

    @pl.when(ch == 0)
    def _():
        rs_ref[...] = jnp.zeros_like(rs_ref)
        g_scr[...] = gin_ref[0]

    spread(coef_ref, fan_ref, splat, tc)
    at = [pl.ds(tile * 128, 128) for tile in range(tiles)]
    group = 2
    for n0 in range(0, STATE, group):
        pairs = [(n, i) for n in range(n0, n0 + group) for i in range(tiles)]
        init = (tuple(g_scr[pl.ds(n * 8, 8), at[i]] for n, i in pairs), tuple(rs_ref[0, pl.ds(n * 8, 8), at[i]] for n, i in pairs))

        def backward(k, carry, n0=n0):
            gs, rs = carry
            t = tc - 1 - k
            d = [delta_ref[t, :, l] for l in at]
            w = [w_ref[t, :, l] for l in at]
            s = [ds_ref[t, :, l] for l in at]
            da = [None] * tiles if n0 == 0 else [a_ref[t, :, l] for l in at]
            cs = [None] * tiles if n0 == 0 else [s_ref[t, :, l] for l in at]
            ng, nr = [], []
            for n in range(n0, n0 + group):
                r = pl.ds(n * 8, 8)
                cin = splat[rows8(t), pl.ds(n * 128, 128)]
                cout = splat[rows8(t), pl.ds((STATE + n) * 128, 128)]
                acc = None
                for i in range(tiles):
                    rate = rate_ref[r, at[i]]
                    j = len(ng)
                    a = jnp.exp2(d[i] * rate)
                    g = gs[j] + cout * s[i]
                    ga = g * a
                    ng.append(ga)
                    th = ga * hist_ref[0, t, r, at[i]]
                    da[i] = th * rate if n == 0 else da[i] + th * rate
                    cs[i] = cin * g if n == 0 else cs[i] + cin * g
                    acc = g * w[i] if i == 0 else acc + g * w[i]
                    nr.append(rs[j] + th * d[i])
                acc_in[rows8(t), pl.ds(n * 128, 128)] = acc
            for i in range(tiles):
                a_ref[t, :, at[i]] = da[i]
                s_ref[t, :, at[i]] = cs[i]
            return tuple(ng), tuple(nr)

        gs, rs = lax.fori_loop(0, tc, backward, init, unroll=tc)
        for j, (n, i) in enumerate(pairs):
            g_scr[pl.ds(n * 8, 8), at[i]] = gs[j]
            rs_ref[0, pl.ds(n * 8, 8), at[i]] = rs[j]
    sums = jnp.dot(acc_in[...].astype(BF16), fold_ref[0], preferred_element_type=F32)
    dc_ref[...] = sums.reshape(tc, 8, 128) + dout_ref[...]


def scan_backward(delta, w, ds, coef, rate, fan, fold, hist, dout, g_in, tc=STEPS, vmem=56 * 2**20):
    tokens, members, cd = delta.shape
    sg, nch = members // 8, tokens // tc
    rows = STATE * 8
    tok = lambda width: pl.BlockSpec((tc, 8, width), lambda s, c: (nch - 1 - c, s, 0))
    keep = lambda r: pl.BlockSpec((1, r, cd), lambda s, c: (s, 0, 0))
    whole = lambda a: pl.BlockSpec(a.shape, lambda s, c: (0,) * a.ndim)
    return pl.pallas_call(
        functools.partial(backward_kernel, cd, tc),
        grid=(sg, nch),
        in_specs=[tok(cd), tok(cd), tok(cd), tok(128), whole(rate), whole(fan), whole(fold),
                  pl.BlockSpec((1, tc, rows, cd), lambda s, c: (s, nch - 1 - c, 0, 0)), tok(128), keep(rows)],
        out_specs=[tok(cd), tok(cd), tok(128), keep(rows)],
        out_shape=[jax.ShapeDtypeStruct(delta.shape, F32)] * 2 + [jax.ShapeDtypeStruct((tokens, members, 128), F32), jax.ShapeDtypeStruct((sg, rows, cd), F32)],
        scratch_shapes=[pltpu.VMEM((rows, cd), F32), pltpu.VMEM((tc * 8, 2 * STATE * 128), F32), pltpu.VMEM((tc * 8, STATE * 128), F32)],
        compiler_params=pltpu.CompilerParams(vmem_limit_bytes=vmem),
        cost_estimate=pl.CostEstimate(flops=10**9, bytes_accessed=10**6, transcendentals=0),
        name="scan_backward",
    )(delta, w, ds, coef, rate, fan, fold, hist, dout, g_in)


def rounded(value):
    return lax.reduce_precision(value, 8, 7)


def silu_slope(value):
    sigma = jax.nn.sigmoid(value)
    return sigma * (1.0 + value * (1.0 - sigma))


def contract_rows(left, right):
    return lax.dot_general(left, right, (((0,), (0,)), ((), ())), preferred_element_type=F32)


def contract_cols(left, right):
    return lax.dot_general(left, right, (((1,), (1,)), ((), ())), preferred_element_type=F32)


def dot(left, right):
    return jnp.dot(left, right, preferred_element_type=F32)


def along_z(grid, value, d):
    ctx = grid.ctx
    return lax.ppermute(value, "ctx", [(c, (c + 4 * d) % ctx) for c in range(ctx)])


def swap(grid, value, bit):
    return lax.ppermute(value, "ctx", [(c, c ^ bit) for c in range(grid.ctx)])


def spread_tables():
    fan = np.zeros((128, 2 * STATE * 128), np.float32)
    for k in range(2 * STATE):
        fan[k, k * 128:(k + 1) * 128] = 1
        fan[2 * STATE + k, k * 128:(k + 1) * 128] = 1
    fold = np.zeros((2, STATE * 128, 128), np.float32)
    for n in range(STATE):
        fold[0, n * 128:(n + 1) * 128, n] = 1
        fold[1, n * 128:(n + 1) * 128, STATE + n] = 1
    return jnp.asarray(fan, BF16), jnp.asarray(fold, BF16)


def shards(grid, hidden_in, norm_gain, in_proj, conv_weight, conv_bias, state_proj, delta_proj, delta_bias,
           decay_log, skip_gain, out_proj, cotangent):
    F, C, Z = grid.fsdp, grid.members, grid.planes
    tokens = hidden_in.shape[1]
    rows = in_proj.shape[0]
    block = out_proj.shape[0]
    chans = Z * block
    z, q, f = grid.here()

    hidden_low = hidden_in.reshape(tokens, D)
    cot_rows = cotangent.reshape(tokens, D)
    gain_rows = rounded(norm_gain)
    lin = z * C + q * F + f
    slots = 128 // rows
    gain_tile = jnp.where(lax.broadcasted_iota(jnp.int32, (slots, 1), 0) == lin % slots, gain_rows[None, :], 0.0).reshape(1, 128)
    gain_tile = jnp.broadcast_to(gain_tile, (8, 128))
    out_low = out_proj.astype(BF16)
    wi = in_proj
    if block % 128:
        wi = rounded(in_proj).astype(BF16)
        wi = wi.reshape(rows, 2, Z, C, block).transpose(3, 0, 1, 2, 4).reshape(C, rows, 2 * chans)
    small = jnp.concatenate(
        [conv_weight, conv_bias[None], delta_bias[None], skip_gain[None], decay_log, jnp.zeros((9, block), F32), delta_proj, state_proj.T], axis=0
    )
    small = lax.optimization_barrier(small).astype(BF16)
    normed_all, cot_all, wi_all, small_all, gains = gather_all(grid, hidden_low, gain_tile, cot_rows, wi, small)
    gains = gains[0]
    count = C * tokens
    normed_all = normed_all.reshape(count, D)
    cot_all = cot_all.reshape(count, D)
    w_in = wi_all.reshape(D, 2 * chans)
    small_all = small_all.transpose(1, 0, 2).reshape(small.shape[0], chans)
    taps = small_all[:KW].astype(F32)
    conv_shift = small_all[KW].astype(F32)
    delta_shift = small_all[KW + 1].astype(F32)
    skip = small_all[KW + 2].astype(F32)
    decay_rate = -jnp.exp(small_all[KW + 3:KW + 3 + STATE].astype(F32))
    w_delta = small_all[32:32 + DT_RANK]
    w_state = small_all[32 + DT_RANK:]
    rate8 = jnp.repeat(decay_rate * LOG2E, 8, axis=0)

    def by_step(value):
        return value.reshape(C, tokens, -1).transpose(1, 0, 2)

    def by_member(value):
        return value.transpose(1, 0, 2).reshape(count, -1)

    mixed = lax.optimization_barrier(dot(normed_all, w_in).astype(BF16))
    tail = mixed.reshape(C, tokens, -1)[C - F:, tokens - (KW - 1):, :chans].transpose(1, 0, 2)
    tail = tail.reshape((KW - 1) * F, chans)
    edge_rows = -(-(KW - 1) * F // 16) * 16
    tails = send_edges(grid, jnp.pad(tail, ((0, edge_rows - (KW - 1) * F), (0, 0))), 1, [], 3, "conv_edges")[0]
    out_low, tails = lax.optimization_barrier((out_low, tails))
    w_out = [out_low] + [along_z(grid, out_low, d) for d in range(1, Z)]
    mixed, tails = lax.optimization_barrier((mixed, tails))
    mixed = by_step(mixed)
    conv_in = mixed[:, :, :chans]
    gate = mixed[:, :, chans:].astype(F32)
    before = tails[: (KW - 1) * F]
    before = jnp.where(z > 0, before, jnp.zeros_like(before)).reshape(KW - 1, F, chans)
    edge = jnp.concatenate([before, conv_in[tokens - (KW - 1):, : C - F]], axis=1)
    padded = jnp.concatenate([edge, conv_in], axis=0).astype(F32)
    conv_out = jnp.broadcast_to(conv_shift, (tokens, C, chans))
    for k in range(KW):
        conv_out = conv_out + taps[k] * padded[k:k + tokens]
    act = rounded(jax.nn.silu(conv_out))
    act_rows = lax.optimization_barrier(act.astype(BF16).reshape(count, chans))
    pad_lanes = 256 - DT_RANK - 2 * STATE
    w_state = jnp.pad(w_state, ((0, pad_lanes), (0, 0)))
    selected = contract_cols(act_rows, w_state)
    delta_in, coef = plane_sum(grid, selected, True, 4)
    coef = coef.reshape(tokens, C, 128)
    delta_pre = (dot(delta_in, w_delta) + delta_shift).reshape(tokens, C, chans)
    delta = jax.nn.softplus(delta_pre)
    drive = delta * act
    delta, drive = lax.optimization_barrier((delta, drive))
    w_out, _ = lax.optimization_barrier((w_out, delta))
    gate_act = jax.nn.silu(gate)
    w_out = in_place_order(grid, w_out).reshape(chans, D)
    d_gated = lax.optimization_barrier(by_step(lax.optimization_barrier(contract_cols(cot_all, w_out))))
    d_scanned = d_gated * gate_act

    fan, fold = spread_tables()
    ends, adjoints, totals = scan_ends(delta, drive, d_scanned, coef, rate8, fan)
    def by_segment(value):
        groups = C // 8
        value = value.reshape(groups, -1, 8, chans).transpose(0, 2, 1, 3)
        return value.reshape(4, F, -1, chans)

    def by_sublane(value):
        return value.reshape(C // 8, 8, STATE, chans).transpose(0, 2, 1, 3).reshape(C // 8, STATE * 8, chans)

    totals = by_segment(totals)
    kept, ends, adjoints = jnp.exp(decay_rate * totals), by_segment(ends), by_segment(adjoints)
    end = ends[0]
    for c in range(1, 4):
        end = kept[c] * end + ends[c]
    adj = adjoints[3]
    for c in reversed(range(3)):
        adj = kept[c] * adj + adjoints[c]
    plane_total = jnp.broadcast_to(jnp.sum(totals, axis=0), (F, 8, chans))

    def with_total(value):
        return jnp.concatenate([value, plane_total], axis=1).reshape(F * (STATE + 8), chans)

    ups, downs = exchange_states(grid, with_total(end), with_total(adj), 5)
    ups, downs = ups.reshape(Z, F, STATE + 8, chans), downs.reshape(Z, F, STATE + 8, chans)

    def through(received, p, value):
        return jnp.exp(decay_rate * received[p, :, STATE:STATE + 1]) * value + received[p, :, :STATE]

    state = jnp.zeros((F, STATE, chans), F32)
    adj = state
    for p in range(Z - 1):
        state = jnp.where(p < z, through(ups, p, state), state)
    for p in reversed(range(1, Z)):
        adj = jnp.where(p > z, through(downs, p, adj), adj)
    before_state, after_adj = [], []
    for c in range(4):
        before_state.append(state)
        state = kept[c] * state + ends[c]
    for c in reversed(range(4)):
        after_adj.append(adj)
        adj = kept[c] * adj + adjoints[c]
    after_adj.reverse()

    y, history, d_out_coef = scan_forward(delta, drive, d_scanned, coef, rate8, fan, fold, by_sublane(jnp.stack(before_state)))
    scanned = y + skip * act
    gated = (scanned * gate_act).astype(BF16)
    d_gate = d_gated * scanned * silu_slope(gate)
    gated, d_gate = lax.optimization_barrier((gated, d_gate.astype(BF16)))
    gated, d_gate = lax.optimization_barrier((by_member(gated), by_member(d_gate)))
    half = D // 2
    core = q % 2
    w_out_mine = lax.dynamic_slice_in_dim(w_out, core * half, half, 1)
    w_out_twin = lax.dynamic_slice_in_dim(w_out, (1 - core) * half, half, 1)

    near = [d for d in range(1, Z) if d != 2]

    def total(parts):
        return functools.reduce(lambda t, v: t + v.astype(F32), parts[1:], parts[0].astype(F32))

    def twin_summed(mine, twin_part):
        return (mine + swap(grid, twin_part, 1).astype(F32)).astype(BF16).reshape(4, F, tokens, half)

    def over_x(pick):
        return [pick(f)] + [lax.ppermute(pick((f + d) % F), "fsdp", [(g, (g + d) % F) for g in range(F)]) for d in range(1, F)]

    def over_y(low):
        cut = lambda y: lax.dynamic_slice_in_dim(low, 2 * y, 2, 0)
        return [cut(q // 2), swap(grid, cut(1 - q // 2), 2)]

    early = tokens // 2

    twin_part = dot(gated, w_out_twin).astype(BF16)
    out_part = contract_rows(gated, cot_all).astype(BF16).reshape(Z, block, D)
    gate_part = contract_rows(normed_all, d_gate).astype(BF16).reshape(Z, C * rows, chans)
    out_part, gate_part = lax.optimization_barrier((out_part, gate_part))
    chip_out = twin_summed(dot(gated, w_out_mine), twin_part)
    packed = packed_for_planes(grid, out_part, gate_part)
    sent_weights = [packed[0]] + [along_z(grid, packed[d], d) for d in range(1, Z)]
    sent_tokens = [over_x(lambda g: lax.dynamic_index_in_dim(chip_out[:, :, :early], g, 1, False)), over_y(chip_out[:, :, early:])]
    history, _ = lax.optimization_barrier((history, (out_part, gate_part, chip_out)))
    swept = scan_backward(delta, drive, d_scanned, coef, rate8, fan, fold, history, d_out_coef, by_sublane(jnp.stack(after_adj)))
    (d_delta_a, coef_sum, d_coef, rate_sum), arrived_weights, sent_tokens = lax.optimization_barrier((swept, [sent_weights[d] for d in near], sent_tokens))
    first, second = (total(parts).astype(BF16) for parts in sent_tokens)
    decay_grad = rate_sum.reshape(C // 8, STATE, 8, chans).sum(axis=(0, 2)) * decay_rate
    skip_grad = jnp.sum(d_scanned * act, axis=(0, 1))
    d_delta_pre = (d_delta_a * (1.0 / LOG2E) + act * coef_sum) * jax.nn.sigmoid(delta_pre)
    shift_grad = jnp.sum(d_delta_pre, axis=(0, 1))
    d_delta_low = d_delta_pre.astype(BF16).reshape(count, chans)
    dproj_grad = contract_rows(delta_in, d_delta_low)
    d_delta_in = contract_cols(d_delta_low, w_delta)
    partial = jnp.concatenate([d_delta_in, d_coef.reshape(count, 128)], axis=1)
    d_selected, far_weights = lax.optimization_barrier((plane_sum(grid, partial, False, 6)[0], sent_weights[2]))
    sproj_grad = contract_rows(act_rows, d_selected).T[:DT_RANK + 2 * STATE]
    d_activated = delta * coef_sum + skip * d_scanned + dot(d_selected, w_state).reshape(tokens, C, chans)
    d_conv = d_activated * silu_slope(conv_out)
    cbias_grad = jnp.sum(d_conv, axis=(0, 1))
    kernel_grad = jnp.stack([jnp.sum(d_conv * padded[k:k + tokens], axis=(0, 1)) for k in range(KW)])
    head = d_conv[:KW - 1, :F].reshape((KW - 1) * F, chans)
    head_rows = -(-(KW - 1) * F // 8) * 8
    weight_sum = total([sent_weights[0], far_weights] + arrived_weights)
    gate_sum = weight_sum[:C * rows].astype(BF16).reshape(C, rows, chans)
    out_grad = weight_sum[C * rows:].reshape(D // chans, block, chans).transpose(1, 0, 2).reshape(block, D)
    first, second = over_y(first), over_x(lambda g: lax.dynamic_index_in_dim(second, g, 1, False))
    heads = send_edges(grid, jnp.pad(head, ((0, head_rows - (KW - 1) * F), (0, 0))), -1, [], 7, "conv_grad_edges")[0]
    after = heads[: (KW - 1) * F]
    after = jnp.where(z < Z - 1, after, jnp.zeros_like(after)).reshape(KW - 1, F, chans)
    edge_grad = jnp.concatenate([d_conv[:KW - 1, F:], after], axis=1)
    grad_padded = jnp.concatenate([d_conv, edge_grad], axis=0)
    d_conv_in = jnp.zeros((tokens, C, chans), F32)
    for k in range(KW):
        d_conv_in = d_conv_in + taps[k] * grad_padded[KW - 1 - k:KW - 1 - k + tokens]
    d_conv_in = by_member(lax.optimization_barrier(d_conv_in.astype(BF16)))
    conv_part = contract_rows(normed_all, d_conv_in).astype(BF16).reshape(Z, C, rows, chans)
    d_mixed = jnp.concatenate([d_conv_in, d_gate], axis=1)
    w_in_mine = lax.dynamic_slice_in_dim(w_in, core * half, half, 0)
    w_in_twin = lax.dynamic_slice_in_dim(w_in, (1 - core) * half, half, 0)
    from_twin = swap(grid, contract_cols(d_mixed, w_in_twin).astype(BF16), 1)
    part_in = (contract_cols(d_mixed, w_in_mine) + from_twin.astype(F32)).astype(BF16).reshape(4, F, tokens, half)

    fine = jnp.concatenate([kernel_grad, cbias_grad[None], shift_grad[None], skip_grad[None], decay_grad, jnp.zeros((9, chans), F32)], axis=0)
    fine = lax.optimization_barrier(fine).reshape(32, Z, block).transpose(1, 0, 2)
    coarse = jnp.concatenate([dproj_grad, sproj_grad], axis=0).astype(BF16)
    coarse = coarse.reshape(-1, Z, block).transpose(1, 0, 2)
    part_in, first, second = lax.optimization_barrier((part_in, first, second))
    own = jnp.concatenate([total(first), total(second)], axis=1)
    mixer_own = lax.dynamic_index_in_dim(own, core, 0, False)
    mixer_twin = swap(grid, lax.dynamic_index_in_dim(own, 1 - core, 0, False).astype(BF16), 1)
    mixer_twin = mixer_twin.astype(F32)
    mixer_out = jnp.where(core == 0, jnp.concatenate([mixer_own, mixer_twin], 1), jnp.concatenate([mixer_twin, mixer_own], 1))
    d_normed, conv_rows, gate_rows, coarse, fine = token_sums(grid, part_in, conv_part, gate_sum, [coarse, fine], 9)
    in_grad = jnp.stack([conv_rows, gate_rows], axis=0).reshape(2, C, rows, Z, block).transpose(2, 0, 3, 1, 4)
    in_grad = in_grad.reshape(rows, 2 * DI).astype(F32)
    d_unit = jnp.concatenate([d_normed[0], d_normed[1]], axis=1).astype(F32) * gains[None, :]
    hidden = hidden_low.astype(F32)
    inv_rms = lax.rsqrt(jnp.mean(hidden * hidden, axis=1, keepdims=True) + EPS)
    unit = hidden * inv_rms
    block_out = (hidden + mixer_out).astype(BF16)
    coarse = coarse.astype(F32).sum(axis=0)
    fine = fine.sum(axis=0)
    gain_grad = jnp.sum(rounded(in_proj) * in_grad, axis=1) / gain_rows
    mean_term = jnp.mean(d_unit * unit, axis=1, keepdims=True)
    input_grad = (cot_rows.astype(F32) + inv_rms * (d_unit - unit * mean_term)).astype(BF16)
    return (
        block_out.reshape(1, tokens, D),
        input_grad.reshape(1, tokens, D),
        gain_grad,
        in_grad,
        fine[:KW],
        fine[KW],
        coarse[DT_RANK:].T,
        coarse[:DT_RANK],
        fine[KW + 1],
        fine[KW + 3:KW + 3 + STATE],
        fine[KW + 2],
        out_grad,
    )


def solution(mesh):
    grid = Grid(mesh.shape["ctx"], mesh.shape["fsdp"])
    both = ("ctx", "fsdp")
    tokens, flat, by_row, by_col = P("fsdp", "ctx", None), P(both), P(both, None), P(None, both)
    in_specs = (tokens, flat, by_row, by_col, flat, by_row, by_col, flat, by_col, flat, by_row, tokens)
    out_specs = (tokens, tokens, flat, by_row, by_col, flat, by_row, by_col, flat, by_col, flat, by_row)
    return jax.shard_map(functools.partial(shards, grid), mesh=mesh, in_specs=in_specs, out_specs=out_specs, check_vma=False)
```

```python
import functools

import jax
import jax.numpy as jnp
import numpy as np
from jax import lax
from jax.experimental import pallas as pl
from jax.experimental.pallas import tpu as pltpu
from jax.sharding import PartitionSpec as P

D = 2048
DI = 4096
STATE = 16
DT_RANK = 128
KW = 4
EPS = 1e-05
LOG2E = 1.4426950408889634
STEPS = 16
MESH = pl.DeviceIdType.MESH
BF16 = jnp.bfloat16
F32 = jnp.float32


class Grid:
    def __init__(self, ctx, fsdp):
        self.ctx, self.fsdp = ctx, fsdp
        self.planes = ctx // 4
        self.members = 4 * fsdp
        self.devices = ctx * fsdp

    def here(self):
        c, f = lax.axis_index("ctx"), lax.axis_index("fsdp")
        return c // 4, c % 4, f

    def at(self, z, q, f):
        return {"ctx": z * 4 + q, "fsdp": f}

    def member(self, z, j):
        return self.at(z, j // self.fsdp, j % self.fsdp)


def remote(src, dst, send, recv, where):
    return pltpu.make_async_remote_copy(
        src_ref=src, dst_ref=dst, send_sem=send, recv_sem=recv, device_id=where, device_id_type=MESH
    )


def greet(places):
    barrier = pltpu.get_barrier_semaphore()
    for place in places:
        pl.semaphore_signal(barrier, inc=1, device_id=place, device_id_type=MESH)
    pl.semaphore_wait(barrier, len(places))


def comm_call(kernel, outs, scratch, ident, name, args, vmem=None, in_vmem=(), out_vmem=False):
    spaces = [pl.BlockSpec(memory_space=pltpu.VMEM if i in in_vmem else pl.ANY) for i in range(len(args))]
    return pl.pallas_call(
        kernel,
        in_specs=spaces,
        out_specs=[pl.BlockSpec(memory_space=pltpu.VMEM if out_vmem else pl.ANY)] * len(outs),
        out_shape=outs,
        scratch_shapes=scratch,
        compiler_params=pltpu.CompilerParams(
            collective_id=ident, has_side_effects=True, vmem_limit_bytes=vmem or 16 * 2**20
        ),
        name=name,
    )(*args)


def gather_kernel(grid, rows, h_ref, g_ref, c_ref, in_ref, sm_ref, n_all, c_all, wi_all, sm_all, gain_out,
                  gain_buf, gains, n_low, wi_cut, local, g_send, g_recv, n_send, n_recv, c_send, c_recv, a_send, a_recv,
                  z_send, z_recv, s_send, s_recv):
    z, q, f = grid.here()
    F, C, Z, N = grid.fsdp, grid.members, grid.planes, grid.devices
    me = q * F + f
    lin = z * C + me
    opposite, twin = q ^ 2, q ^ 1
    barrier = pltpu.get_barrier_semaphore()

    def other(d):
        to = lax.rem(lin + d, N)
        return grid.member(to // C, lax.rem(to, C))

    @pl.loop(1, N)
    def _(d):
        pl.semaphore_signal(barrier, inc=1, device_id=other(d), device_id_type=MESH)

    wi_ref = in_ref
    if in_ref.dtype == F32:
        wi_ref, lanes = wi_cut, wi_cut.shape[2] // (2 * Z)
        for j in range(C):
            for m in range(2 * Z):
                wi_cut[j, :, m * lanes:(m + 1) * lanes] = in_ref[:, (m * C + j) * lanes:(m * C + j + 1) * lanes].astype(BF16)
    pl.semaphore_wait(barrier, N - 1)

    def gain_copy(d):
        return remote(g_ref, gain_buf.at[lin], g_send.at[d], g_recv.at[d], other(d))

    @pl.loop(1, N)
    def _(d):
        gain_copy(d).start()

    sends = []

    def push(copy):
        copy.start()
        sends.append(copy)

    def block_of(i):
        return lax.rem(me + C - i, C)

    def line_pair(step, i):
        right, left = z - step, z + step
        if step == 0 and i == 0:
            src_right = src_left = wi_ref.at[me]
        else:
            src_right, src_left = wi_all.at[right * C + block_of(i)], wi_all.at[left * C + block_of(i)]
        return (
            (z < Z - 1) & (right >= 0),
            remote(src_right, wi_all.at[right * C + block_of(i)], z_send.at[0, step, i], z_recv.at[0, step, i], grid.at(z + 1, q, f)),
            (z > 0) & (left <= Z - 1),
            remote(src_left, wi_all.at[left * C + block_of(i)], z_send.at[1, step, i], z_recv.at[1, step, i], grid.at(z - 1, q, f)),
        )

    def line_start(step, i):
        to_right, right, to_left, left = line_pair(step, i)

        @pl.when(to_right)
        def _():
            right.start()

        @pl.when(to_left)
        def _():
            left.start()

    def line_done(step, i):
        to_right, right, to_left, left = line_pair(step, i)

        @pl.when(to_right)
        def _():
            right.wait_send()

        @pl.when(to_left)
        def _():
            left.wait_send()

    def line_arrived(step, i):
        from_left, from_right = z - 1 - step, z + 1 + step

        @pl.when(from_left >= 0)
        def _():
            ref = wi_all.at[from_left * C + block_of(i)]
            remote(ref, ref, z_send.at[0, step, i], z_recv.at[0, step, i], grid.at(z - 1, q, f)).wait_recv()

        @pl.when(from_right <= Z - 1)
        def _():
            ref = wi_all.at[from_right * C + block_of(i)]
            remote(ref, ref, z_send.at[1, step, i], z_recv.at[1, step, i], grid.at(z + 1, q, f)).wait_recv()

    line_start(0, 0)
    for d in range(1, C):
        j = lax.rem(me + d, C)
        push(remote(wi_ref.at[j], wi_all.at[lin], a_send.at[d], a_recv.at[d], grid.member(z, j)))
    for d in range(1, Z):
        push(remote(sm_ref, sm_all.at[z], s_send.at[d], s_recv.at[d], grid.at(lax.rem(z + d, Z), q, f)))

    n_sent, c_sent = [0], [0]

    def push_n(block, src, where):
        push(remote(src, n_all.at[block], n_send.at[n_sent[0]], n_recv.at[block], where))
        n_sent[0] += 1

    def push_c(block, src, where):
        push(remote(src, c_all.at[block], c_send.at[c_sent[0]], c_recv.at[block], where))
        c_sent[0] += 1

    def arrived(ref, sems, block):
        remote(ref.at[block], ref.at[block], n_send.at[0], sems.at[block], grid.at(z, twin, f)).wait_recv()

    others = [lax.rem(f + d, F) for d in range(1, F)]

    gain_buf[lin] = g_ref[...]

    @pl.loop(1, N)
    def _(d):
        back = lax.rem(lin + N - d, N)
        remote(g_ref, gain_buf.at[back], g_send.at[d], g_recv.at[d], grid.member(back // C, lax.rem(back, C))).wait_recv()

    per = max(1, 128 // rows)
    for chunk in range(D // 128):
        gain = gain_buf[chunk * per]
        for k in range(1, per):
            gain = gain + gain_buf[chunk * per + k]
        gains[:, chunk * 128:(chunk + 1) * 128] = gain

    @pl.loop(0, h_ref.shape[0] // 16)
    def _(r):
        at = pl.ds(pl.multiple_of(r * 16, 16), 16)
        hidden = h_ref[at, :].astype(F32)
        scale = lax.rsqrt(jnp.mean(hidden * hidden, axis=1, keepdims=True) + EPS)
        n_low[at, :] = (hidden * scale * gains[0:1, :]).astype(BF16)

    for g in others:
        push_n(me, n_low, grid.at(z, q, g))
    push_c(me, c_ref, grid.at(z, opposite, f))
    push_n(me, n_low, grid.at(z, opposite, f))
    for g in others:
        push_c(me, c_ref, grid.at(z, q, g))
    push_n(me, n_low, grid.at(z, twin, f))
    push_c(me, c_ref, grid.at(z, twin, f))
    mine = [
        pltpu.make_async_copy(n_low, n_all.at[me], local.at[0]),
        pltpu.make_async_copy(c_ref, c_all.at[me], local.at[1]),
        pltpu.make_async_copy(wi_ref.at[me], wi_all.at[lin], local.at[2]),
        pltpu.make_async_copy(sm_ref, sm_all.at[z], local.at[3]),
        pltpu.make_async_copy(gains, gain_out, local.at[4]),
    ]
    for copy in mine:
        copy.start()
    for d in range(1, C):
        back = block_of(d)
        remote(wi_ref.at[me], wi_all.at[z * C + back], a_send.at[d], a_recv.at[d], grid.member(z, back)).wait_recv()
        line_start(0, d)
    mine[2].wait()

    def pass_on(step, blocks):
        for i in blocks:
            line_arrived(step, i)
            if step < Z - 2:
                line_start(step + 1, i)

    pass_on(0, range(C // 2))
    for g in others:
        block = q * F + g
        arrived(n_all, n_recv, block)
        push_n(block, n_all.at[block], grid.at(z, opposite, f))
        push_n(block, n_all.at[block], grid.at(z, twin, f))
    arrived(c_all, c_recv, opposite * F + f)
    for g in others:
        push_c(opposite * F + f, c_all.at[opposite * F + f], grid.at(z, q, g))
    push_c(opposite * F + f, c_all.at[opposite * F + f], grid.at(z, twin, f))
    pass_on(0, range(C // 2, C))
    for step in range(1, Z - 2):
        pass_on(step, range(C))
    for g in others:
        arrived(c_all, c_recv, q * F + g)
        push_c(q * F + g, c_all.at[q * F + g], grid.at(z, twin, f))
    for g in [f] + others:
        block = opposite * F + g
        arrived(n_all, n_recv, block)
        push_n(block, n_all.at[block], grid.at(z, twin, f))
    for g in others:
        block = opposite * F + g
        arrived(c_all, c_recv, block)
        push_c(block, c_all.at[block], grid.at(z, twin, f))
    pass_on(Z - 2, range(C))
    for side in (twin, twin ^ 2):
        for g in [f] + others:
            arrived(n_all, n_recv, side * F + g)
            arrived(c_all, c_recv, side * F + g)
    for d in range(1, Z):
        back = lax.rem(z + Z - d, Z)
        remote(sm_ref, sm_all.at[back], s_send.at[d], s_recv.at[d], grid.at(back, q, f)).wait_recv()
    for i in (0, 1, 3, 4):
        mine[i].wait()
    for copy in sends:
        copy.wait_send()
    for step in range(Z - 1):
        for i in range(C):
            line_done(step, i)

    @pl.loop(1, N)
    def _(d):
        gain_copy(d).wait_send()


def gather_all(grid, hidden, gain_tile, cot, wi, small):
    F, C, Z, N = grid.fsdp, grid.members, grid.planes, grid.devices
    cut = wi.dtype == F32
    rows, width = wi.shape[0 if cut else 1], 2 * DI // C
    tokens = hidden.shape[0]
    dma = pltpu.SemaphoreType.DMA
    outs = [
        jax.ShapeDtypeStruct((C, tokens, D), BF16),
        jax.ShapeDtypeStruct((C, tokens, D), BF16),
        jax.ShapeDtypeStruct((Z * C, rows, width), BF16),
        jax.ShapeDtypeStruct((Z,) + small.shape, BF16),
        jax.ShapeDtypeStruct((8, D), F32),
    ]
    count = (F - 1) + F + 2 * F
    scratch = [pltpu.VMEM((N, 8, 128), F32), pltpu.VMEM((8, D), F32), pltpu.VMEM((tokens, D), BF16)]
    scratch += [pltpu.VMEM((C, rows, width) if cut else (1, 16, 128), BF16)]
    scratch += [dma((5,)), dma((N,)), dma((N,)), dma((count,)), dma((C,)), dma((count,)), dma((C,)), dma((C,)), dma((C,))]
    scratch += [dma((2, Z, C)), dma((2, Z, C)), dma((Z,)), dma((Z,))]
    return comm_call(
        functools.partial(gather_kernel, grid, rows), outs, scratch, 1, "gather_weights_and_tokens",
        (hidden, gain_tile, cot, wi, small), vmem=32 * 2**20, in_vmem=(0, 1, 3) if cut else (0, 1),
    )


def plane_sum_kernel(grid, split, part_ref, *refs):
    outs, (send_buf, recv_buf, result, landed, send, recv, out_send, out_recv) = refs[:1 + split], refs[1 + split:]
    out_low, out_coef = outs if split else (outs[0].at[:, pl.ds(0, 128)], outs[0].at[:, pl.ds(128, 128)])
    z, q, f = grid.here()
    C = grid.members
    me = q * grid.fsdp + f
    rows = part_ref.shape[0] // C
    quarter = rows // 4
    greet([grid.member(z, lax.rem(me + d, C)) for d in range(1, C)])
    lane = lax.broadcasted_iota(jnp.int32, (quarter, 128), 1)

    def span(k, m, size):
        return pl.ds(pl.multiple_of(k * rows + m * size, 16), size)

    def pack(k):
        send_buf[k, 0:rows, :] = part_ref[span(k, 0, rows), 0:128].astype(BF16)
        mixed = part_ref[span(k, 0, quarter), 128:256]
        for m in range(1, 4):
            mixed = mixed + pltpu.roll(part_ref[span(k, m, quarter), 128:256], 32 * m, 1)
        send_buf[k, rows:, :] = mixed.astype(BF16)

    copies = []
    for d in range(1, C):
        j = lax.rem(me + d, C)
        pack(j)
        copy = remote(send_buf.at[j], recv_buf.at[d], send.at[d], recv.at[d], grid.member(z, j))
        copy.start()
        copies.append(copy)
    pack(me)
    total = send_buf[me].astype(F32)
    for d in range(1, C):
        copies[d - 1].wait_recv()
        total = total + recv_buf[d].astype(F32)
    result[...] = total.astype(BF16)
    pushes = []
    for d in range(1, C):
        copy = remote(result, landed.at[me], out_send.at[d], out_recv.at[d], grid.member(z, lax.rem(me + d, C)))
        copy.start()
        pushes.append(copy)

    def unpack(k, block):
        out_low[span(k, 0, rows), :] = block[0:rows, :]
        mixed = block[rows:, :].astype(F32)
        for m in range(4):
            part = pltpu.roll(mixed, 128 - 32 * m, 1) if m else mixed
            out_coef[span(k, m, quarter), :] = jnp.where(lane < 32, part, 0.0).astype(BF16)

    unpack(me, result)
    for d in range(1, C):
        back = lax.rem(me + C - d, C)
        remote(result, landed.at[back], out_send.at[d], out_recv.at[d], grid.member(z, back)).wait_recv()
        unpack(back, landed.at[back])
    for copy in copies + pushes:
        copy.wait_send()


def plane_sum(grid, part, split, ident):
    C = grid.members
    count = part.shape[0]
    rows = count // C
    packed = rows + rows // 4
    dma = pltpu.SemaphoreType.DMA
    return comm_call(
        functools.partial(plane_sum_kernel, grid, split),
        [jax.ShapeDtypeStruct((count, 128), BF16)] * 2 if split else [jax.ShapeDtypeStruct((count, 256), BF16)],
        [pltpu.VMEM((C, packed, 128), BF16), pltpu.VMEM((C, packed, 128), BF16), pltpu.VMEM((packed, 128), BF16), pltpu.VMEM((C, packed, 128), BF16)]
        + [dma((C,))] * 4,
        ident, "plane_sum", (part,), vmem=40 * 2**20, in_vmem=(0,), out_vmem=True,
    )


def edges_kernel(grid, step, count, edge_ref, *refs):
    z, q, f = grid.here()
    C, Z = grid.members, grid.planes
    me = q * grid.fsdp + f
    ins, edge_out, outs = refs[:count], refs[count], refs[count + 1:2 * count + 1]
    e_send, e_recv, local, send, recv = refs[2 * count + 1:]
    above, below = z < Z - 1, z > 0
    to, source = (above, below) if step > 0 else (below, above)
    barrier = pltpu.get_barrier_semaphore()

    @pl.when(above)
    def _():
        pl.semaphore_signal(barrier, inc=1, device_id=grid.at(z + 1, q, f), device_id_type=MESH)

    @pl.when(below)
    def _():
        pl.semaphore_signal(barrier, inc=1, device_id=grid.at(z - 1, q, f), device_id_type=MESH)

    members = [lax.rem(me + d, C) for d in range(1, C)] if count else []
    for j in members:
        pl.semaphore_signal(barrier, inc=1, device_id=grid.member(z, j), device_id_type=MESH)
    pl.semaphore_wait(barrier, len(members) + jnp.where(above & below, 2, 1))
    edge = remote(edge_ref, edge_out, e_send, e_recv, grid.at(z + step, q, f))

    @pl.when(to)
    def _():
        edge.start()

    pushes, waits = [], []
    for i in range(count):
        for d, j in enumerate(members, 1):
            back = lax.rem(me + C - d, C)
            pushes.append(remote(ins[i].at[j], outs[i].at[me], send.at[i, d], recv.at[i, d], grid.member(z, j)))
            waits.append(remote(ins[i].at[me], outs[i].at[back], send.at[i, d], recv.at[i, d], grid.member(z, back)))
    for copy in pushes:
        copy.start()
    for i in range(count):
        own = pltpu.make_async_copy(ins[i].at[me], outs[i].at[me], local.at[i])
        own.start()
        own.wait()
    for copy in waits:
        copy.wait_recv()

    @pl.when(source)
    def _():
        remote(edge_ref, edge_out, e_send, e_recv, grid.at(z - step, q, f)).wait_recv()

    for copy in pushes:
        copy.wait_send()

    @pl.when(to)
    def _():
        edge.wait_send()


def send_edges(grid, edge, step, arrays, ident, name):
    dma = pltpu.SemaphoreType.DMA
    n, C = len(arrays), grid.members
    m = max(n, 1)
    args = (edge,) + tuple(arrays)
    return comm_call(
        functools.partial(edges_kernel, grid, step, n), [jax.ShapeDtypeStruct(a.shape, a.dtype) for a in args],
        [dma, dma, dma((m,)), dma((m, C)), dma((m, C))], ident, name, args,
        in_vmem=tuple(range(n + 1)), out_vmem=True,
    )


def token_sums_kernel(grid, lines_in, part_ref, rows_ref, gate_ref, *refs):
    ins, outs = refs[:lines_in], refs[3 + lines_in:3 + 2 * lines_in]
    out_ref, row_out, gate_out = refs[lines_in:lines_in + 3]
    (x_in, y_in, x_sum, y_sum, x_last, y_last, final, landed, row_in, row_sum, local, x_send, x_recv, y_send, y_recv, b_send,
     b_recv, a_send, a_recv, t_send, t_recv, l_send, l_recv, f_send, f_recv, r_send, r_recv, g_send, g_recv) = refs[3 + 2 * lines_in:]
    z, q, f = grid.here()
    F, Z, C = grid.fsdp, grid.planes, grid.members
    me = q * F + f
    y, core = q // 2, lax.rem(q, 2)
    rows = part_ref.shape[2] // 2
    first, second = pl.ds(0, rows), pl.ds(rows, rows)
    across, twin = grid.at(z, q ^ 2, f), grid.at(z, q ^ 1, f)
    others = [lax.rem(f + d, F) for d in range(1, F)]
    greet([grid.member(z, lax.rem(me + d, C)) for d in range(1, C)] + [grid.at(lax.rem(z + d, Z), q, f) for d in range(1, Z)])
    far, near = pl.ds(2 * (1 - y), 2), pl.ds(2 * y, 2)

    def add(target, sources):
        @pl.loop(0, rows // 16)
        def _(r):
            at = pl.ds(pl.multiple_of(r * 16, 16), 16)
            value = sources[0][at, :].astype(F32)
            for source in sources[1:]:
                value = value + source[at, :].astype(F32)
            target[at, :] = value.astype(BF16)

    x_copies = [
        remote(part_ref.at[pl.ds(0, 4), g, first], x_in.at[d], x_send.at[d], x_recv.at[d], grid.at(z, q, g))
        for d, g in enumerate(others, 1)
    ]
    y_copy = remote(part_ref.at[far, :, second], y_in, y_send, y_recv, across)
    row_copies = []
    for d in range(1, Z):
        j = lax.rem(z + d, Z)
        row_copies.append(remote(rows_ref.at[j], row_in.at[d], f_send.at[d], f_recv.at[d], grid.at(j, q, f)))
    for copy in row_copies + x_copies + [y_copy]:
        copy.start()
    mine, pushes, waits, late = [], [], [], []
    for d in range(1, C):
        j, back = lax.rem(me + d, C), lax.rem(me + C - d, C)
        pushes.append(remote(gate_ref.at[j], gate_out.at[me], g_send.at[d], g_recv.at[d], grid.member(z, j)))
        waits.append(remote(gate_ref.at[me], gate_out.at[back], g_send.at[d], g_recv.at[d], grid.member(z, back)))
    gate_out[me] = gate_ref[me]
    for i in range(lines_in):
        mine.append(pltpu.make_async_copy(ins[i].at[z], outs[i].at[z], local.at[i]))
        for d in range(1, Z):
            j, back = lax.rem(z + d, Z), lax.rem(z + Z - d, Z)
            late.append(remote(ins[i].at[j], outs[i].at[z], l_send.at[i, d], l_recv.at[i, d], grid.at(j, q, f)))
            waits.append(remote(ins[i].at[z], outs[i].at[back], l_send.at[i, d], l_recv.at[i, d], grid.at(back, q, f)))
    for copy in pushes + mine:
        copy.start()
    for copy in x_copies:
        copy.wait_recv()

    def x_block(k):
        add(x_sum.at[k], [part_ref.at[k, f, first]] + [x_in.at[d, k] for d in range(1, F)])

    for c in range(2):
        x_block(2 * (1 - y) + c)
    a_copy = remote(x_sum.at[far], x_last, a_send, a_recv, across)
    a_copy.start()
    y_copy.wait_recv()
    b_copies = []
    for d, g in enumerate(others, 1):
        for c in range(2):
            add(y_sum.at[g, c], [part_ref.at[2 * y + c, g, second], y_in.at[c, g]])
        copy = remote(y_sum.at[g], y_last.at[d], b_send.at[d], b_recv.at[d], grid.at(z, q, g))
        copy.start()
        b_copies.append(copy)
    for c in range(2):
        x_block(2 * y + c)
        add(y_sum.at[f, c], [part_ref.at[2 * y + c, f, second], y_in.at[c, f]])
    a_copy.wait_recv()
    for c in range(2):
        add(final.at[c, first], [x_sum.at[2 * y + c], x_last.at[c]])
    for copy in b_copies:
        copy.wait_recv()
    for c in range(2):
        add(final.at[c, second], [y_sum.at[f, c]] + [y_last.at[d, c] for d in range(1, F)])
    t_copy = remote(final.at[1 - core], landed, t_send, t_recv, twin)
    t_copy.start()
    for copy in row_copies:
        copy.wait_recv()
    for copy in late:
        copy.start()

    @pl.loop(0, C)
    def _(j):
        value = rows_ref[z, j].astype(F32)
        for d in range(1, Z):
            value = value + row_in[d, j].astype(F32)
        row_sum[j] = value.astype(BF16)

    for d in range(1, C):
        j, back = lax.rem(me + d, C), lax.rem(me + C - d, C)
        copy = remote(row_sum.at[j], row_out.at[me], r_send.at[d], r_recv.at[d], grid.member(z, j))
        copy.start()
        pushes.append(copy)
        waits.append(remote(row_sum.at[me], row_out.at[back], r_send.at[d], r_recv.at[d], grid.member(z, back)))
    row_out[me] = row_sum[me]
    out_ref[core] = final[core]
    t_copy.wait_recv()
    out_ref[1 - core] = landed[...]
    for copy in mine:
        copy.wait()
    for copy in waits:
        copy.wait_recv()
    for copy in x_copies + [y_copy, a_copy, t_copy] + b_copies + row_copies + pushes + late:
        copy.wait_send()


def token_sums(grid, part, weight_rows, gate_rows, line_arrays, ident):
    dma = pltpu.SemaphoreType.DMA
    F, Z, n = grid.fsdp, grid.planes, len(line_arrays)
    tokens, half = part.shape[2:]
    rows = tokens // 2
    buf = lambda *shape: pltpu.VMEM(shape + (rows, half), BF16)
    hbm, vmem = pl.BlockSpec(memory_space=pl.ANY), pl.BlockSpec(memory_space=pltpu.VMEM)
    return pl.pallas_call(
        functools.partial(token_sums_kernel, grid, n),
        in_specs=[vmem] * 3 + [hbm] * n,
        out_specs=[vmem] * 3 + [hbm] * n,
        out_shape=[jax.ShapeDtypeStruct((2, tokens, half), BF16), jax.ShapeDtypeStruct(gate_rows.shape, BF16), jax.ShapeDtypeStruct(gate_rows.shape, BF16)] + [jax.ShapeDtypeStruct(a.shape, a.dtype) for a in line_arrays],
        scratch_shapes=[buf(F, 4), buf(2, F), buf(4), buf(F, 2), buf(2), buf(F, 2), pltpu.VMEM((2, tokens, half), BF16), pltpu.VMEM((tokens, half), BF16), pltpu.VMEM(weight_rows.shape, BF16), pltpu.VMEM(weight_rows.shape[1:], BF16)]
        + [dma((n,)), dma((F,)), dma((F,)), dma, dma, dma((F,)), dma((F,)), dma, dma, dma, dma, dma((n, Z)), dma((n, Z)), dma((Z,)), dma((Z,))] + [dma((grid.members,))] * 4,
        compiler_params=pltpu.CompilerParams(collective_id=ident, has_side_effects=True, vmem_limit_bytes=56 * 2**20),
        cost_estimate=pl.CostEstimate(flops=45 * 10**9, bytes_accessed=10**8, transcendentals=0),
        name="token_sums",
    )(part, weight_rows, gate_rows, *line_arrays)


def pack_kernel(grid, out_ref, gate_ref, *outs):
    z, _, _ = grid.here()
    rows, chans = gate_ref.shape[1:]
    block, width = out_ref.shape[1:]
    for d in range(grid.planes):
        p = lax.rem(z + d, grid.planes)
        outs[d][0:rows, :] = gate_ref[p]
        for i in range(width // chans):
            outs[d][rows + i * block:rows + (i + 1) * block, :] = out_ref[p, :, i * chans:(i + 1) * chans]


def packed_for_planes(grid, out_part, gate_part):
    Z, rows, chans = gate_part.shape
    shape = (rows + out_part.shape[1] * out_part.shape[2] // chans, chans)
    vmem = pl.BlockSpec(memory_space=pltpu.VMEM)
    return pl.pallas_call(
        functools.partial(pack_kernel, grid),
        in_specs=[vmem] * 2,
        out_specs=[vmem] * Z,
        out_shape=[jax.ShapeDtypeStruct(shape, BF16)] * Z,
        compiler_params=pltpu.CompilerParams(vmem_limit_bytes=32 * 2**20),
        name="packed_for_planes",
    )(out_part, gate_part)


def states_kernel(grid, up_ref, down_ref, up_all, down_all, send, recv):
    z, q, f = grid.here()
    Z = grid.planes
    greet([grid.at(lax.rem(z + d, Z), q, f) for d in range(1, Z)])

    def each(act):
        for d in range(1, Z):
            above, below = z + d, z - d

            @pl.when(above <= Z - 1)
            def _():
                act(
                    remote(up_ref, up_all.at[z], send.at[0, d], recv.at[0, d], grid.at(above, q, f)),
                    remote(down_ref, down_all.at[above], send.at[1, d], recv.at[1, d], grid.at(above, q, f)),
                )

            @pl.when(below >= 0)
            def _():
                act(
                    remote(down_ref, down_all.at[z], send.at[1, d], recv.at[1, d], grid.at(below, q, f)),
                    remote(up_ref, up_all.at[below], send.at[0, d], recv.at[0, d], grid.at(below, q, f)),
                )

    each(lambda push, pull: push.start())
    each(lambda push, pull: pull.wait_recv())
    each(lambda push, pull: push.wait_send())


def exchange_states(grid, up, down, ident):
    dma = pltpu.SemaphoreType.DMA
    Z = grid.planes
    return comm_call(
        functools.partial(states_kernel, grid),
        [jax.ShapeDtypeStruct((Z,) + a.shape, a.dtype) for a in (up, down)],
        [dma((2, Z)), dma((2, Z))], ident, "segment_states", (up, down),
    )


def owners_kernel(grid, planes_in, lines_in, *refs):
    z, q, f = grid.here()
    C, Z = grid.members, grid.planes
    me = q * grid.fsdp + f
    total = 1 + planes_in + lines_in
    ins, outs = refs[:total], refs[total:2 * total]
    slots, own, result, local, w_send, w_recv, r_send, r_recv, p_send, p_recv, l_send, l_recv = refs[2 * total:]
    greet([grid.member(z, lax.rem(me + d, C)) for d in range(1, C)] + [grid.at(lax.rem(z + d, Z), q, f) for d in range(1, Z)])
    load = pltpu.make_async_copy(ins[0].at[z], own, local.at[0])
    load.start()
    weights, mine, pushes, waits = [], [], [], []
    for d in range(1, Z):
        j = lax.rem(z + d, Z)
        weights.append(remote(ins[0].at[j], slots.at[d], w_send.at[d], w_recv.at[d], grid.at(j, q, f)))
    for copy in weights:
        copy.start()
    for i in range(planes_in):
        mine.append(pltpu.make_async_copy(ins[1 + i].at[me], outs[1 + i].at[me], local.at[1 + i]))
        for d in range(1, C):
            j, back = lax.rem(me + d, C), lax.rem(me + C - d, C)
            pushes.append(remote(ins[1 + i].at[j], outs[1 + i].at[me], p_send.at[i, d], p_recv.at[i, d], grid.member(z, j)))
            waits.append(remote(ins[1 + i].at[me], outs[1 + i].at[back], p_send.at[i, d], p_recv.at[i, d], grid.member(z, back)))
    for i in range(lines_in):
        k = 1 + planes_in + i
        mine.append(pltpu.make_async_copy(ins[k].at[z], outs[k].at[z], local.at[k]))
        for d in range(1, Z):
            j, back = lax.rem(z + d, Z), lax.rem(z + Z - d, Z)
            pushes.append(remote(ins[k].at[j], outs[k].at[z], l_send.at[i, d], l_recv.at[i, d], grid.at(j, q, f)))
            waits.append(remote(ins[k].at[z], outs[k].at[back], l_send.at[i, d], l_recv.at[i, d], grid.at(back, q, f)))
    for copy in pushes + mine:
        copy.start()
    load.wait()
    for copy in weights:
        copy.wait_recv()

    @pl.loop(0, C)
    def _(j):
        value = own[j].astype(F32)
        for d in range(1, Z):
            value = value + slots[d, j].astype(F32)
        result[j] = value.astype(BF16)

    mine.append(pltpu.make_async_copy(result.at[me], outs[0].at[me], local.at[0]))
    mine[-1].start()
    for d in range(1, C):
        j, back = lax.rem(me + d, C), lax.rem(me + C - d, C)
        copy = remote(result.at[j], outs[0].at[me], r_send.at[d], r_recv.at[d], grid.member(z, j))
        copy.start()
        pushes.append(copy)
        waits.append(remote(result.at[me], outs[0].at[back], r_send.at[d], r_recv.at[d], grid.member(z, back)))
    for copy in mine:
        copy.wait()
    for copy in waits:
        copy.wait_recv()
    for copy in pushes + weights:
        copy.wait_send()


def to_owners(grid, weight, plane_arrays, line_arrays, ident):
    dma = pltpu.SemaphoreType.DMA
    C, Z = grid.members, grid.planes
    p, l = len(plane_arrays), len(line_arrays)
    args = (weight,) + tuple(plane_arrays) + tuple(line_arrays)
    part = weight.shape[1:]
    outs = [jax.ShapeDtypeStruct(part, BF16)] + [jax.ShapeDtypeStruct(a.shape, a.dtype) for a in args[1:]]
    return comm_call(
        functools.partial(owners_kernel, grid, p, l), outs,
        [pltpu.VMEM((Z,) + part, BF16), pltpu.VMEM(part, BF16), pltpu.VMEM(part, BF16)]
        + [dma((1 + p + l,)), dma((Z,)), dma((Z,)), dma((C,)), dma((C,)), dma((p, C)), dma((p, C)), dma((l, Z)), dma((l, Z))],
        ident, "to_owners", args,
    )


def place_kernel(grid, *refs):
    z, _, _ = grid.here()
    Z = grid.planes
    for d in range(Z):
        refs[Z][lax.rem(z + Z - d, Z)] = refs[d][...]


def in_place_order(grid, pieces):
    Z = grid.planes
    return pl.pallas_call(
        functools.partial(place_kernel, grid),
        in_specs=[pl.BlockSpec(memory_space=pltpu.VMEM)] * Z,
        out_specs=pl.BlockSpec(memory_space=pltpu.VMEM),
        out_shape=jax.ShapeDtypeStruct((Z,) + pieces[0].shape, pieces[0].dtype),
        compiler_params=pltpu.CompilerParams(vmem_limit_bytes=16 * 2**20),
        name="in_place_order",
    )(*pieces)

def spread(coef_ref, fan_ref, splat, tc):
    c = coef_ref[...].reshape(8 * tc, 128)
    for k in range(0, 2 * STATE, 4):
        l = pl.ds(k * 128, 512)
        splat[:, l] = jnp.dot(c, fan_ref[:, l], preferred_element_type=F32)

def rows8(t):
    return pl.ds(pl.multiple_of(t * 8, 8), 8)

def ends_kernel(cd, tc, delta_ref, w_ref, ds_ref, coef_ref, rate_ref, fan_ref, e_ref, g_ref, tot_ref, p_scr, splat):
    ch = pl.program_id(1)
    tiles = cd // 128
    @pl.when(ch == 0)
    def _():
        e_ref[...] = jnp.zeros_like(e_ref)
        g_ref[...] = jnp.zeros_like(g_ref)
        tot_ref[...] = jnp.zeros_like(tot_ref)
        p_scr[...] = jnp.ones_like(p_scr)
    spread(coef_ref, fan_ref, splat, tc)
    group = 4
    for tile in range(tiles):
        lanes = pl.ds(tile * 128, 128)
        for n0 in range(0, STATE, group):
            rates = [rate_ref[(n0 + i) * 8:(n0 + i + 1) * 8, lanes] for i in range(group)]
            def body(t, carry):
                hs, ps, gs = carry
                tok = pl.ds(pl.multiple_of(t * 8, 8), 8)
                d, w, s = delta_ref[t, :, lanes], w_ref[t, :, lanes], ds_ref[t, :, lanes]
                nh, np_, ng = [], [], []
                for i in range(group):
                    a = jnp.exp2(d * rates[i])
                    cin = splat[rows8(t), pl.ds((n0 + i) * 128, 128)]
                    cout = splat[rows8(t), pl.ds((STATE + n0 + i) * 128, 128)]
                    nh.append(a * hs[i] + cin * w)
                    p = ps[i] * a
                    np_.append(p)
                    ng.append(gs[i] + p * (cout * s))
                return tuple(nh), tuple(np_), tuple(ng)
            rows = [pl.ds((n0 + i) * 8, 8) for i in range(group)]
            init = (tuple(e_ref[0, r, lanes] for r in rows), tuple(p_scr[r, lanes] for r in rows), tuple(g_ref[0, r, lanes] for r in rows))
            hs, ps, gs = lax.fori_loop(0, tc, body, init, unroll=tc)
            for i, r in enumerate(rows):
                e_ref[0, r, lanes] = hs[i]
                p_scr[r, lanes] = ps[i]
                g_ref[0, r, lanes] = gs[i]
        def total(t, acc):
            return acc + delta_ref[t, :, lanes]
        tot_ref[0, :, lanes] = lax.fori_loop(0, tc, total, tot_ref[0, :, lanes], unroll=tc)

def scan_ends(delta, w, ds, coef, rate, fan, tc=2 * STEPS, vmem=48 * 2**20):
    tokens, members, cd = delta.shape
    sg, nch = members // 8, tokens // tc
    rows = STATE * 8
    tok = lambda width: pl.BlockSpec((tc, 8, width), lambda s, c: (c, s, 0))
    keep = lambda r: pl.BlockSpec((1, r, cd), lambda s, c: (s, 0, 0))
    return pl.pallas_call(
        functools.partial(ends_kernel, cd, tc),
        grid=(sg, nch),
        in_specs=[tok(cd), tok(cd), tok(cd), pl.BlockSpec((tc, 8, 128), lambda s, c: (c, s, 0)), pl.BlockSpec((rows, cd), lambda s, c: (0, 0)), pl.BlockSpec(fan.shape, lambda s, c: (0, 0))],
        out_specs=[keep(rows), keep(rows), keep(8)],
        out_shape=[jax.ShapeDtypeStruct((sg, rows, cd), F32), jax.ShapeDtypeStruct((sg, rows, cd), F32), jax.ShapeDtypeStruct((sg, 8, cd), F32)],
        scratch_shapes=[pltpu.VMEM((rows, cd), F32), pltpu.VMEM((tc * 8, 2 * STATE * 128), F32)],
        compiler_params=pltpu.CompilerParams(vmem_limit_bytes=vmem),
        name="segment_ends",
    )(delta, w, ds, coef, rate, fan)

def forward_kernel(cd, tc, delta_ref, w_ref, ds_ref, coef_ref, rate_ref, fan_ref, fold_ref, sin_ref,
                   y_ref, hist_ref, dc_ref, h_scr, splat, acc_out):
    ch = pl.program_id(1)
    tiles = cd // 128

    @pl.when(ch == 0)
    def _():
        h_scr[...] = sin_ref[0]

    spread(coef_ref, fan_ref, splat, tc)
    at = [pl.ds(tile * 128, 128) for tile in range(tiles)]
    group = 4
    for n0 in range(0, STATE, group):
        pairs = [(n, i) for n in range(n0, n0 + group) for i in range(tiles)]
        init = tuple(h_scr[pl.ds(n * 8, 8), at[i]] for n, i in pairs)

        def forward(t, hs, n0=n0):
            d = [delta_ref[t, :, l] for l in at]
            w = [w_ref[t, :, l] for l in at]
            s = [ds_ref[t, :, l] for l in at]
            y = [None] * tiles if n0 == 0 else [y_ref[t, :, l] for l in at]
            out = []
            for n in range(n0, n0 + group):
                r = pl.ds(n * 8, 8)
                cin = splat[rows8(t), pl.ds(n * 128, 128)]
                cout = splat[rows8(t), pl.ds((STATE + n) * 128, 128)]
                acc = None
                for i in range(tiles):
                    old = hs[len(out)]
                    hist_ref[0, t, r, at[i]] = old
                    h = jnp.exp2(d[i] * rate_ref[r, at[i]]) * old + cin * w[i]
                    out.append(h)
                    y[i] = cout * h if n == 0 else y[i] + cout * h
                    acc = s[i] * h if i == 0 else acc + s[i] * h
                acc_out[rows8(t), pl.ds(n * 128, 128)] = acc
            for i in range(tiles):
                y_ref[t, :, at[i]] = y[i]
            return tuple(out)

        hs = lax.fori_loop(0, tc, forward, init, unroll=tc)
        for j, (n, i) in enumerate(pairs):
            h_scr[pl.ds(n * 8, 8), at[i]] = hs[j]
    sums = jnp.dot(acc_out[...].astype(BF16), fold_ref[1], preferred_element_type=F32)
    dc_ref[...] = sums.reshape(tc, 8, 128)


def scan_forward(delta, w, ds, coef, rate, fan, fold, s_in, tc=2 * STEPS, vmem=56 * 2**20):
    tokens, members, cd = delta.shape
    sg, nch = members // 8, tokens // tc
    rows = STATE * 8
    tok = lambda width: pl.BlockSpec((tc, 8, width), lambda s, c: (c, s, 0))
    keep = lambda r: pl.BlockSpec((1, r, cd), lambda s, c: (s, 0, 0))
    whole = lambda a: pl.BlockSpec(a.shape, lambda s, c: (0,) * a.ndim)
    return pl.pallas_call(
        functools.partial(forward_kernel, cd, tc),
        grid=(sg, nch),
        in_specs=[tok(cd), tok(cd), tok(cd), tok(128), whole(rate), whole(fan), whole(fold), keep(rows)],
        out_specs=[tok(cd), pl.BlockSpec((1, tc, rows, cd), lambda s, c: (s, c, 0, 0)), tok(128)],
        out_shape=[jax.ShapeDtypeStruct(delta.shape, F32), jax.ShapeDtypeStruct((sg, tokens, rows, cd), F32), jax.ShapeDtypeStruct((tokens, members, 128), F32)],
        scratch_shapes=[pltpu.VMEM((rows, cd), F32), pltpu.VMEM((tc * 8, 2 * STATE * 128), F32), pltpu.VMEM((tc * 8, STATE * 128), F32)],
        compiler_params=pltpu.CompilerParams(vmem_limit_bytes=vmem),
        cost_estimate=pl.CostEstimate(flops=30 * 10**9, bytes_accessed=90 * 10**6, transcendentals=0),
        name="scan_forward",
    )(delta, w, ds, coef, rate, fan, fold, s_in)


def backward_kernel(cd, tc, delta_ref, w_ref, ds_ref, coef_ref, rate_ref, fan_ref, fold_ref, hist_ref, dout_ref, gin_ref,
                    a_ref, s_ref, dc_ref, rs_ref, g_scr, splat, acc_in):
    ch = pl.program_id(1)
    tiles = cd // 128

    @pl.when(ch == 0)
    def _():
        rs_ref[...] = jnp.zeros_like(rs_ref)
        g_scr[...] = gin_ref[0]

    spread(coef_ref, fan_ref, splat, tc)
    at = [pl.ds(tile * 128, 128) for tile in range(tiles)]
    group = 2
    for n0 in range(0, STATE, group):
        pairs = [(n, i) for n in range(n0, n0 + group) for i in range(tiles)]
        init = (tuple(g_scr[pl.ds(n * 8, 8), at[i]] for n, i in pairs), tuple(rs_ref[0, pl.ds(n * 8, 8), at[i]] for n, i in pairs))

        def backward(k, carry, n0=n0):
            gs, rs = carry
            t = tc - 1 - k
            d = [delta_ref[t, :, l] for l in at]
            w = [w_ref[t, :, l] for l in at]
            s = [ds_ref[t, :, l] for l in at]
            da = [None] * tiles if n0 == 0 else [a_ref[t, :, l] for l in at]
            cs = [None] * tiles if n0 == 0 else [s_ref[t, :, l] for l in at]
            ng, nr = [], []
            for n in range(n0, n0 + group):
                r = pl.ds(n * 8, 8)
                cin = splat[rows8(t), pl.ds(n * 128, 128)]
                cout = splat[rows8(t), pl.ds((STATE + n) * 128, 128)]
                acc = None
                for i in range(tiles):
                    rate = rate_ref[r, at[i]]
                    j = len(ng)
                    a = jnp.exp2(d[i] * rate)
                    g = gs[j] + cout * s[i]
                    ga = g * a
                    ng.append(ga)
                    th = ga * hist_ref[0, t, r, at[i]]
                    da[i] = th * rate if n == 0 else da[i] + th * rate
                    cs[i] = cin * g if n == 0 else cs[i] + cin * g
                    acc = g * w[i] if i == 0 else acc + g * w[i]
                    nr.append(rs[j] + th * d[i])
                acc_in[rows8(t), pl.ds(n * 128, 128)] = acc
            for i in range(tiles):
                a_ref[t, :, at[i]] = da[i]
                s_ref[t, :, at[i]] = cs[i]
            return tuple(ng), tuple(nr)

        gs, rs = lax.fori_loop(0, tc, backward, init, unroll=tc)
        for j, (n, i) in enumerate(pairs):
            g_scr[pl.ds(n * 8, 8), at[i]] = gs[j]
            rs_ref[0, pl.ds(n * 8, 8), at[i]] = rs[j]
    sums = jnp.dot(acc_in[...].astype(BF16), fold_ref[0], preferred_element_type=F32)
    dc_ref[...] = sums.reshape(tc, 8, 128) + dout_ref[...]


def scan_backward(delta, w, ds, coef, rate, fan, fold, hist, dout, g_in, tc=STEPS, vmem=56 * 2**20):
    tokens, members, cd = delta.shape
    sg, nch = members // 8, tokens // tc
    rows = STATE * 8
    tok = lambda width: pl.BlockSpec((tc, 8, width), lambda s, c: (nch - 1 - c, s, 0))
    keep = lambda r: pl.BlockSpec((1, r, cd), lambda s, c: (s, 0, 0))
    whole = lambda a: pl.BlockSpec(a.shape, lambda s, c: (0,) * a.ndim)
    return pl.pallas_call(
        functools.partial(backward_kernel, cd, tc),
        grid=(sg, nch),
        in_specs=[tok(cd), tok(cd), tok(cd), tok(128), whole(rate), whole(fan), whole(fold),
                  pl.BlockSpec((1, tc, rows, cd), lambda s, c: (s, nch - 1 - c, 0, 0)), tok(128), keep(rows)],
        out_specs=[tok(cd), tok(cd), tok(128), keep(rows)],
        out_shape=[jax.ShapeDtypeStruct(delta.shape, F32)] * 2 + [jax.ShapeDtypeStruct((tokens, members, 128), F32), jax.ShapeDtypeStruct((sg, rows, cd), F32)],
        scratch_shapes=[pltpu.VMEM((rows, cd), F32), pltpu.VMEM((tc * 8, 2 * STATE * 128), F32), pltpu.VMEM((tc * 8, STATE * 128), F32)],
        compiler_params=pltpu.CompilerParams(vmem_limit_bytes=vmem),
        cost_estimate=pl.CostEstimate(flops=10**9, bytes_accessed=10**6, transcendentals=0),
        name="scan_backward",
    )(delta, w, ds, coef, rate, fan, fold, hist, dout, g_in)


def rounded(value):
    return lax.reduce_precision(value, 8, 7)


def silu_slope(value):
    sigma = jax.nn.sigmoid(value)
    return sigma * (1.0 + value * (1.0 - sigma))


def contract_rows(left, right):
    return lax.dot_general(left, right, (((0,), (0,)), ((), ())), preferred_element_type=F32)


def contract_cols(left, right):
    return lax.dot_general(left, right, (((1,), (1,)), ((), ())), preferred_element_type=F32)


def dot(left, right):
    return jnp.dot(left, right, preferred_element_type=F32)


def along_z(grid, value, d):
    ctx = grid.ctx
    return lax.ppermute(value, "ctx", [(c, (c + 4 * d) % ctx) for c in range(ctx)])


def swap(grid, value, bit):
    return lax.ppermute(value, "ctx", [(c, c ^ bit) for c in range(grid.ctx)])


def spread_tables():
    fan = np.zeros((128, 2 * STATE * 128), np.float32)
    for k in range(2 * STATE):
        fan[k, k * 128:(k + 1) * 128] = 1
        fan[2 * STATE + k, k * 128:(k + 1) * 128] = 1
    fold = np.zeros((2, STATE * 128, 128), np.float32)
    for n in range(STATE):
        fold[0, n * 128:(n + 1) * 128, n] = 1
        fold[1, n * 128:(n + 1) * 128, STATE + n] = 1
    return jnp.asarray(fan, BF16), jnp.asarray(fold, BF16)


def shards(grid, hidden_in, norm_gain, in_proj, conv_weight, conv_bias, state_proj, delta_proj, delta_bias,
           decay_log, skip_gain, out_proj, cotangent):
    F, C, Z = grid.fsdp, grid.members, grid.planes
    tokens = hidden_in.shape[1]
    rows = in_proj.shape[0]
    block = out_proj.shape[0]
    chans = Z * block
    z, q, f = grid.here()

    hidden_low = hidden_in.reshape(tokens, D)
    cot_rows = cotangent.reshape(tokens, D)
    gain_rows = rounded(norm_gain)
    lin = z * C + q * F + f
    slots = 128 // rows
    gain_tile = jnp.where(lax.broadcasted_iota(jnp.int32, (slots, 1), 0) == lin % slots, gain_rows[None, :], 0.0).reshape(1, 128)
    gain_tile = jnp.broadcast_to(gain_tile, (8, 128))
    out_low = out_proj.astype(BF16)
    wi = in_proj
    if block % 128:
        wi = rounded(in_proj).astype(BF16)
        wi = wi.reshape(rows, 2, Z, C, block).transpose(3, 0, 1, 2, 4).reshape(C, rows, 2 * chans)
    small = jnp.concatenate(
        [conv_weight, conv_bias[None], delta_bias[None], skip_gain[None], decay_log, jnp.zeros((9, block), F32), delta_proj, state_proj.T], axis=0
    )
    small = lax.optimization_barrier(small).astype(BF16)
    normed_all, cot_all, wi_all, small_all, gains = gather_all(grid, hidden_low, gain_tile, cot_rows, wi, small)
    gains = gains[0]
    count = C * tokens
    normed_all = normed_all.reshape(count, D)
    cot_all = cot_all.reshape(count, D)
    w_in = wi_all.reshape(D, 2 * chans)
    small_all = small_all.transpose(1, 0, 2).reshape(small.shape[0], chans)
    taps = small_all[:KW].astype(F32)
    conv_shift = small_all[KW].astype(F32)
    delta_shift = small_all[KW + 1].astype(F32)
    skip = small_all[KW + 2].astype(F32)
    decay_rate = -jnp.exp(small_all[KW + 3:KW + 3 + STATE].astype(F32))
    w_delta = small_all[32:32 + DT_RANK]
    w_state = small_all[32 + DT_RANK:]
    rate8 = jnp.repeat(decay_rate * LOG2E, 8, axis=0)

    def by_step(value):
        return value.reshape(C, tokens, -1).transpose(1, 0, 2)

    def by_member(value):
        return value.transpose(1, 0, 2).reshape(count, -1)

    mixed = lax.optimization_barrier(dot(normed_all, w_in).astype(BF16))
    tail = mixed.reshape(C, tokens, -1)[C - F:, tokens - (KW - 1):, :chans].transpose(1, 0, 2)
    tail = tail.reshape((KW - 1) * F, chans)
    edge_rows = -(-(KW - 1) * F // 16) * 16
    tails = send_edges(grid, jnp.pad(tail, ((0, edge_rows - (KW - 1) * F), (0, 0))), 1, [], 3, "conv_edges")[0]
    out_low, tails = lax.optimization_barrier((out_low, tails))
    w_out = [out_low] + [along_z(grid, out_low, d) for d in range(1, Z)]
    mixed, tails = lax.optimization_barrier((mixed, tails))
    mixed = by_step(mixed)
    conv_in = mixed[:, :, :chans]
    gate = mixed[:, :, chans:].astype(F32)
    before = tails[: (KW - 1) * F]
    before = jnp.where(z > 0, before, jnp.zeros_like(before)).reshape(KW - 1, F, chans)
    edge = jnp.concatenate([before, conv_in[tokens - (KW - 1):, : C - F]], axis=1)
    padded = jnp.concatenate([edge, conv_in], axis=0).astype(F32)
    conv_out = jnp.broadcast_to(conv_shift, (tokens, C, chans))
    for k in range(KW):
        conv_out = conv_out + taps[k] * padded[k:k + tokens]
    act = rounded(jax.nn.silu(conv_out))
    act_rows = lax.optimization_barrier(act.astype(BF16).reshape(count, chans))
    pad_lanes = 256 - DT_RANK - 2 * STATE
    w_state = jnp.pad(w_state, ((0, pad_lanes), (0, 0)))
    selected = contract_cols(act_rows, w_state)
    delta_in, coef = plane_sum(grid, selected, True, 4)
    coef = coef.reshape(tokens, C, 128)
    delta_pre = (dot(delta_in, w_delta) + delta_shift).reshape(tokens, C, chans)
    delta = jax.nn.softplus(delta_pre)
    drive = delta * act
    delta, drive = lax.optimization_barrier((delta, drive))
    w_out, _ = lax.optimization_barrier((w_out, delta))
    gate_act = jax.nn.silu(gate)
    w_out = in_place_order(grid, w_out).reshape(chans, D)
    d_gated = lax.optimization_barrier(by_step(lax.optimization_barrier(contract_cols(cot_all, w_out))))
    d_scanned = d_gated * gate_act

    fan, fold = spread_tables()
    ends, adjoints, totals = scan_ends(delta, drive, d_scanned, coef, rate8, fan)
    def by_segment(value):
        groups = C // 8
        value = value.reshape(groups, -1, 8, chans).transpose(0, 2, 1, 3)
        return value.reshape(4, F, -1, chans)

    def by_sublane(value):
        return value.reshape(C // 8, 8, STATE, chans).transpose(0, 2, 1, 3).reshape(C // 8, STATE * 8, chans)

    totals = by_segment(totals)
    kept, ends, adjoints = jnp.exp(decay_rate * totals), by_segment(ends), by_segment(adjoints)
    end = ends[0]
    for c in range(1, 4):
        end = kept[c] * end + ends[c]
    adj = adjoints[3]
    for c in reversed(range(3)):
        adj = kept[c] * adj + adjoints[c]
    plane_total = jnp.pad(jnp.sum(totals, axis=0).reshape(F, chans), ((0, -F % 8), (0, 0)))

    def with_total(value):
        return jnp.concatenate([value.reshape(F * STATE, chans), plane_total], axis=0)

    ups, downs = exchange_states(grid, with_total(end), with_total(adj), 5)

    def through(received, p, value):
        total_steps = received[p, F * STATE:F * STATE + F].reshape(F, 1, chans)
        return jnp.exp(decay_rate * total_steps) * value + received[p, :F * STATE].reshape(F, STATE, chans)

    state = jnp.zeros((F, STATE, chans), F32)
    adj = state
    for p in range(Z - 1):
        state = jnp.where(p < z, through(ups, p, state), state)
    for p in reversed(range(1, Z)):
        adj = jnp.where(p > z, through(downs, p, adj), adj)
    before_state, after_adj = [], []
    for c in range(4):
        before_state.append(state)
        state = kept[c] * state + ends[c]
    for c in reversed(range(4)):
        after_adj.append(adj)
        adj = kept[c] * adj + adjoints[c]
    after_adj.reverse()

    y, history, d_out_coef = scan_forward(delta, drive, d_scanned, coef, rate8, fan, fold, by_sublane(jnp.stack(before_state)))
    scanned = y + skip * act
    gated = (scanned * gate_act).astype(BF16)
    d_gate = d_gated * scanned * silu_slope(gate)
    gated, d_gate = lax.optimization_barrier((gated, d_gate.astype(BF16)))
    gated, d_gate = lax.optimization_barrier((by_member(gated), by_member(d_gate)))
    half = D // 2
    core = q % 2
    w_out_mine = lax.dynamic_slice_in_dim(w_out, core * half, half, 1)
    w_out_twin = lax.dynamic_slice_in_dim(w_out, (1 - core) * half, half, 1)

    near = [d for d in range(1, Z) if d != 2]

    def total(parts):
        return functools.reduce(lambda t, v: t + v.astype(F32), parts[1:], parts[0].astype(F32))

    def twin_summed(mine, twin_part):
        return (mine + swap(grid, twin_part, 1).astype(F32)).astype(BF16).reshape(4, F, tokens, half)

    def over_x(pick):
        return [pick(f)] + [lax.ppermute(pick((f + d) % F), "fsdp", [(g, (g + d) % F) for g in range(F)]) for d in range(1, F)]

    def over_y(low):
        cut = lambda y: lax.dynamic_slice_in_dim(low, 2 * y, 2, 0)
        return [cut(q // 2), swap(grid, cut(1 - q // 2), 2)]

    early = tokens // 2

    twin_part = dot(gated, w_out_twin).astype(BF16)
    out_part = contract_rows(gated, cot_all).astype(BF16).reshape(Z, block, D)
    gate_part = contract_rows(normed_all, d_gate).astype(BF16).reshape(Z, C * rows, chans)
    out_part, gate_part = lax.optimization_barrier((out_part, gate_part))
    chip_out = twin_summed(dot(gated, w_out_mine), twin_part)
    packed = packed_for_planes(grid, out_part, gate_part)
    sent_weights = [packed[0]] + [along_z(grid, packed[d], d) for d in range(1, Z)]
    sent_tokens = [over_x(lambda g: lax.dynamic_index_in_dim(chip_out[:, :, :early], g, 1, False)), over_y(chip_out[:, :, early:])]
    history, _ = lax.optimization_barrier((history, (out_part, gate_part, chip_out)))
    swept = scan_backward(delta, drive, d_scanned, coef, rate8, fan, fold, history, d_out_coef, by_sublane(jnp.stack(after_adj)))
    (d_delta_a, coef_sum, d_coef, rate_sum), arrived_weights, sent_tokens = lax.optimization_barrier((swept, [sent_weights[d] for d in near], sent_tokens))
    first, second = (total(parts).astype(BF16) for parts in sent_tokens)
    decay_grad = rate_sum.reshape(C // 8, STATE, 8, chans).sum(axis=(0, 2)) * decay_rate
    skip_grad = jnp.sum(d_scanned * act, axis=(0, 1))
    d_delta_pre = (d_delta_a * (1.0 / LOG2E) + act * coef_sum) * jax.nn.sigmoid(delta_pre)
    shift_grad = jnp.sum(d_delta_pre, axis=(0, 1))
    d_delta_low = d_delta_pre.astype(BF16).reshape(count, chans)
    dproj_grad = contract_rows(delta_in, d_delta_low)
    d_delta_in = contract_cols(d_delta_low, w_delta)
    partial = jnp.concatenate([d_delta_in, d_coef.reshape(count, 128)], axis=1)
    d_selected, far_weights = lax.optimization_barrier((plane_sum(grid, partial, False, 6)[0], sent_weights[2]))
    sproj_grad = contract_rows(act_rows, d_selected).T[:DT_RANK + 2 * STATE]
    d_activated = delta * coef_sum + skip * d_scanned + dot(d_selected, w_state).reshape(tokens, C, chans)
    d_conv = d_activated * silu_slope(conv_out)
    cbias_grad = jnp.sum(d_conv, axis=(0, 1))
    kernel_grad = jnp.stack([jnp.sum(d_conv * padded[k:k + tokens], axis=(0, 1)) for k in range(KW)])
    head = d_conv[:KW - 1, :F].reshape((KW - 1) * F, chans)
    head_rows = -(-(KW - 1) * F // 8) * 8
    weight_sum = total([sent_weights[0], far_weights] + arrived_weights)
    gate_sum = weight_sum[:C * rows].astype(BF16).reshape(C, rows, chans)
    out_grad = weight_sum[C * rows:].reshape(D // chans, block, chans).transpose(1, 0, 2).reshape(block, D)
    first, second = over_y(first), over_x(lambda g: lax.dynamic_index_in_dim(second, g, 1, False))
    heads = send_edges(grid, jnp.pad(head, ((0, head_rows - (KW - 1) * F), (0, 0))), -1, [], 7, "conv_grad_edges")[0]
    after = heads[: (KW - 1) * F]
    after = jnp.where(z < Z - 1, after, jnp.zeros_like(after)).reshape(KW - 1, F, chans)
    edge_grad = jnp.concatenate([d_conv[:KW - 1, F:], after], axis=1)
    grad_padded = jnp.concatenate([d_conv, edge_grad], axis=0)
    d_conv_in = jnp.zeros((tokens, C, chans), F32)
    for k in range(KW):
        d_conv_in = d_conv_in + taps[k] * grad_padded[KW - 1 - k:KW - 1 - k + tokens]
    d_conv_in = by_member(lax.optimization_barrier(d_conv_in.astype(BF16)))
    conv_part = contract_rows(normed_all, d_conv_in).astype(BF16).reshape(Z, C, rows, chans)
    d_mixed = jnp.concatenate([d_conv_in, d_gate], axis=1)
    w_in_mine = lax.dynamic_slice_in_dim(w_in, core * half, half, 0)
    w_in_twin = lax.dynamic_slice_in_dim(w_in, (1 - core) * half, half, 0)
    from_twin = swap(grid, contract_cols(d_mixed, w_in_twin).astype(BF16), 1)
    part_in = (contract_cols(d_mixed, w_in_mine) + from_twin.astype(F32)).astype(BF16).reshape(4, F, tokens, half)

    fine = jnp.concatenate([kernel_grad, cbias_grad[None], shift_grad[None], skip_grad[None], decay_grad, jnp.zeros((9, chans), F32)], axis=0)
    fine = lax.optimization_barrier(fine).reshape(32, Z, block).transpose(1, 0, 2)
    coarse = jnp.concatenate([dproj_grad, sproj_grad], axis=0).astype(BF16)
    coarse = coarse.reshape(-1, Z, block).transpose(1, 0, 2)
    part_in, first, second = lax.optimization_barrier((part_in, first, second))
    own = jnp.concatenate([total(first), total(second)], axis=1)
    mixer_own = lax.dynamic_index_in_dim(own, core, 0, False)
    mixer_twin = swap(grid, lax.dynamic_index_in_dim(own, 1 - core, 0, False).astype(BF16), 1)
    mixer_twin = mixer_twin.astype(F32)
    mixer_out = jnp.where(core == 0, jnp.concatenate([mixer_own, mixer_twin], 1), jnp.concatenate([mixer_twin, mixer_own], 1))
    d_normed, conv_rows, gate_rows, coarse, fine = token_sums(grid, part_in, conv_part, gate_sum, [coarse, fine], 9)
    in_grad = jnp.stack([conv_rows, gate_rows], axis=0).reshape(2, C, rows, Z, block).transpose(2, 0, 3, 1, 4)
    in_grad = in_grad.reshape(rows, 2 * DI).astype(F32)
    d_unit = jnp.concatenate([d_normed[0], d_normed[1]], axis=1).astype(F32) * gains[None, :]
    hidden = hidden_low.astype(F32)
    inv_rms = lax.rsqrt(jnp.mean(hidden * hidden, axis=1, keepdims=True) + EPS)
    unit = hidden * inv_rms
    block_out = (hidden + mixer_out).astype(BF16)
    coarse = coarse.astype(F32).sum(axis=0)
    fine = fine.sum(axis=0)
    gain_grad = jnp.sum(rounded(in_proj) * in_grad, axis=1) / gain_rows
    mean_term = jnp.mean(d_unit * unit, axis=1, keepdims=True)
    input_grad = (cot_rows.astype(F32) + inv_rms * (d_unit - unit * mean_term)).astype(BF16)
    return (
        block_out.reshape(1, tokens, D),
        input_grad.reshape(1, tokens, D),
        gain_grad,
        in_grad,
        fine[:KW],
        fine[KW],
        coarse[DT_RANK:].T,
        coarse[:DT_RANK],
        fine[KW + 1],
        fine[KW + 3:KW + 3 + STATE],
        fine[KW + 2],
        out_grad,
    )


def solution(mesh):
    grid = Grid(mesh.shape["ctx"], mesh.shape["fsdp"])
    both = ("ctx", "fsdp")
    tokens, flat, by_row, by_col = P("fsdp", "ctx", None), P(both), P(both, None), P(None, both)
    in_specs = (tokens, flat, by_row, by_col, flat, by_row, by_col, flat, by_col, flat, by_row, tokens)
    out_specs = (tokens, tokens, flat, by_row, by_col, flat, by_row, by_col, flat, by_col, flat, by_row)
    return jax.shard_map(functools.partial(shards, grid), mesh=mesh, in_specs=in_specs, out_specs=out_specs, check_vma=False)
```
